32 devices in a mesh: cp: 4 (over y, x), tp: 8 (over z, core).
Axes of the slice: x: 2, y: 2, z: 4, core: 2. Of those that a mesh axis runs over, the one named last changes fastest.
Arguments:
- tokens: bfloat16 [4096, 2048], P('cp'), may hold values from -6 to 6
- cotangent: bfloat16 [4096, 2048], P('cp'), may hold values from -6 to 6
- first_gain: bfloat16 [2048], replicated, may hold values from 0.5 to 1.5
- first_bias: bfloat16 [2048], replicated, may hold values from -4 to 4
- query_weight: bfloat16 [2048, 2048], P(None, 'tp'), may hold values from -0.125 to 0.125
- query_bias: bfloat16 [2048], P('tp'), may hold values from -4 to 4
- key_weight: bfloat16 [2048, 128], replicated, may hold values from -0.125 to 0.125
- value_weight: bfloat16 [2048, 128], replicated, may hold values from -0.125 to 0.125
- value_bias: bfloat16 [128], replicated, may hold values from -4 to 4
- out_weight: bfloat16 [2048, 2048], P('tp'), may hold values from -1 to 1
- out_bias: bfloat16 [2048], replicated, may hold values from -4 to 4
- second_gain: bfloat16 [2048], replicated, may hold values from 0.5 to 1.5
- second_bias: bfloat16 [2048], replicated, may hold values from -4 to 4
- up_weight: bfloat16 [2048, 8192], P(None, 'tp'), may hold values from -0.125 to 0.125
- up_bias: bfloat16 [8192], P('tp'), may hold values from -4 to 4
- down_weight: bfloat16 [8192, 2048], P('tp'), may hold values from -0.0625 to 0.0625
- down_bias: bfloat16 [2048], replicated, may hold values from -4 to 4
- file_lengths: int32 [12], replicated, may hold values from 1 to 2048, 4096 in all
- pad_mask: int32 [4096], replicated, may hold values 0 or 1
Outputs:
- block_out: bfloat16 [4096, 2048], P('cp')
- tokens_grad: float32 [4096, 2048], P('cp')
- first_gain_grad: float32 [2048], replicated
- first_bias_grad: float32 [2048], replicated
- query_weight_grad: float32 [2048, 2048], P('cp', 'tp')
- query_bias_grad: float32 [2048], P('tp')
- key_weight_grad: float32 [2048, 128], P('cp')
- value_weight_grad: float32 [2048, 128], P('cp')
- value_bias_grad: float32 [128], replicated
- out_weight_grad: float32 [2048, 2048], P('tp', 'cp')
- out_bias_grad: float32 [2048], replicated
- second_gain_grad: float32 [2048], replicated
- second_bias_grad: float32 [2048], replicated
- up_weight_grad: float32 [2048, 8192], P('cp', 'tp')
- up_bias_grad: float32 [8192], P('tp')
- down_weight_grad: float32 [8192, 2048], P('tp', 'cp')
- down_bias_grad: float32 [2048], replicated
The draws below stay inside these ranges and needn't reach their ends.
Inputs may be any that keep to these rules, and one draw needn't show every extreme that they name: `file_lengths`: the lengths sum to 4096; the longest file has exactly 2048 tokens.
All inputs are finite; a program needn't handle non-finite values.
Results may differ from the reference program's by a relative error of at most 0.025.
Values may be sent and summed in bfloat16 or wider, within the bound.
A program may use at most 192 MiB of HBM per device.

```python
import math
import jax
import jax.numpy as jnp
import numpy as np
from jax import lax

D = 2048
HEADS = 16
HS = 128
FF = 8192
FILES = 12
WINDOW = 4096
MOST = 2048


def set_ends(drawn, stream_key, low, top_value):
    longest = drawn.shape.index(max(drawn.shape))
    spots = []
    for shift in (0, 1):
        where = [jax.random.randint(jax.random.fold_in(stream_key, axis), (), 0, length) for axis, length in enumerate(drawn.shape)]
        where[longest] = (where[longest] + shift) % drawn.shape[longest]
        spots.append(tuple(where))
    return drawn.at[spots[0]].set(low).at[spots[1]].set(top_value)


def steps_of(rng, shape, pieces, smallest, largest):
    level, own = 1.0, jax.random.fold_in(rng, 6)
    for axis_at, shards_of in pieces:
        draws = jnp.exp(jax.random.uniform(jax.random.fold_in(own, axis_at), (shards_of,), jnp.float32, smallest / len(pieces), largest / len(pieces)))
        level = level * jnp.repeat(draws, shape[axis_at] // shards_of).reshape([-1 if axis == axis_at else 1 for axis in range(len(shape))])
    return level


def length_profile(count, total, most, skew):
    loads = [(1 << 20) // math.isqrt(grade ** skew) + 1 for grade in range(2, count + 1)]
    rest, counts = total - most - (count - 1), [1] * (count - 1)
    while rest > 0:
        free = [i for i in range(count - 1) if counts[i] < most]
        pool, remaining = sum([loads[i] for i in free]), rest
        for i in free:
            extra = min(most - counts[i], max(1, remaining * loads[i] // pool), rest)
            counts[i] = counts[i] + extra
            rest = rest - extra
    return np.array([most] + counts)


def uneven_parts(stream_key, number_of, total, bound, lean):
    if number_of == 2:
        one = jax.random.randint(stream_key, (), max(1, total - bound), min(bound, total - 1) + 1)
        return jnp.stack([one, total - one])
    tallies = jnp.asarray(length_profile(number_of, total, bound, lean), jnp.int32)
    pairs = (number_of - 1) // 2
    donor, sink = tallies[1:1 + 2 * pairs:2], tallies[2:2 + 2 * pairs:2]
    slack = jnp.minimum(donor - 1, bound - sink)
    moved = jax.random.randint(jax.random.fold_in(stream_key, 1), (pairs,), 0, 1 << 20) % (slack + 1)
    tallies = tallies.at[1:1 + 2 * pairs:2].set(donor - moved).at[2:2 + 2 * pairs:2].set(sink + moved)
    return tallies[jax.random.permutation(jax.random.fold_in(stream_key, 2), number_of)]


def scatter_about(rng, dims, width, bound, split=(), held_as=jnp.bfloat16):
    loudness = steps_of(rng, dims, split, -0.22, 0.18) if split else 1.0
    values = jax.random.normal(rng, dims, jnp.float32) * width * loudness
    return jnp.minimum(jnp.maximum(values, -bound), bound).astype(held_as)


def setup_inputs(seed: int = 0) -> dict:
    arg_keys = jax.random.split(jax.random.key(seed), 20)
    tokens = scatter_about(arg_keys[0], (WINDOW, D), 1.0, 6.0, ((0, 4),))
    cotangent = scatter_about(arg_keys[1], (WINDOW, D), 1.0, 6.0, ((0, 4),))
    first_gain = jnp.clip(1.0 + 0.1 * jax.random.normal(arg_keys[2], (D,), jnp.float32), 0.5, 1.5).astype(jnp.bfloat16)
    first_bias = scatter_about(arg_keys[3], (D,), 0.3, 4.0)
    query_weight = scatter_about(arg_keys[4], (D, HEADS * HS), D ** -0.5, 0.125, ((1, 8),))
    query_bias = scatter_about(arg_keys[5], (HEADS * HS,), 0.3, 4.0, ((0, 8),))
    key_weight = scatter_about(arg_keys[6], (D, HS), D ** -0.5, 0.125)
    value_weight = scatter_about(arg_keys[7], (D, HS), D ** -0.5, 0.125)
    value_bias = scatter_about(arg_keys[8], (HS,), 0.3, 4.0)
    out_weight = scatter_about(arg_keys[9], (HEADS * HS, D), (HEADS * HS // 64) ** -0.5, 1.0, ((0, 8),))
    out_bias = scatter_about(arg_keys[10], (D,), 0.3, 4.0)
    second_gain = jnp.clip(1.0 + 0.1 * jax.random.normal(arg_keys[11], (D,), jnp.float32), 0.5, 1.5).astype(jnp.bfloat16)
    second_bias = scatter_about(arg_keys[12], (D,), 0.3, 4.0)
    up_weight = scatter_about(arg_keys[13], (D, FF), D ** -0.5, 0.125, ((1, 8),))
    up_bias = scatter_about(arg_keys[14], (FF,), 0.3, 4.0, ((0, 8),))
    down_weight = scatter_about(arg_keys[15], (FF, D), FF ** -0.5, 0.0625, ((0, 8),))
    down_bias = scatter_about(arg_keys[16], (D,), 0.3, 4.0)
    file_lengths = uneven_parts(arg_keys[17], FILES, WINDOW, MOST, 2).astype(jnp.int32)
    pad_mask = set_ends((jax.random.randint(arg_keys[18], (WINDOW,), 0, 8) < 7).astype(jnp.int32), jax.random.fold_in(arg_keys[18], 1), 0, 1)
    return {"tokens": tokens, "cotangent": cotangent, "first_gain": first_gain, "first_bias": first_bias, "query_weight": query_weight, "query_bias": query_bias, "key_weight": key_weight, "value_weight": value_weight, "value_bias": value_bias, "out_weight": out_weight, "out_bias": out_bias, "second_gain": second_gain, "second_bias": second_bias, "up_weight": up_weight, "up_bias": up_bias, "down_weight": down_weight, "down_bias": down_bias, "file_lengths": file_lengths, "pad_mask": pad_mask}


EPSILON = 1e-05
NEGATIVE = -1e+30

@jax.custom_vjp
def low(v):
    return lax.optimization_barrier(v.astype(jnp.bfloat16)).astype(jnp.float32)

@jax.custom_vjp
def low_back(v):
    return v

def low_keep(v):
    return (low(v), None)

def low_pass(kept, grad):
    return (grad,)

def back_keep(v):
    return (v, None)

def back_low(kept, grad):
    return (low(grad),)
low.defvjp(low_keep, low_pass)
low_back.defvjp(back_keep, back_low)

def layer_norm(values, gain, bias):
    centre = lax.optimization_barrier(jnp.mean(values, axis=-1, keepdims=True))
    centred = values - centre
    spread = lax.optimization_barrier(jnp.mean(centred * centred, axis=-1, keepdims=True))
    return centred * lax.rsqrt(spread + EPSILON) * gain + bias

def gelu_tanh(values):
    return 0.5 * values * (1.0 + jnp.tanh(0.7978845608028654 * (values + 0.044715 * values * values * values)))

def matmul(left, right):
    return jnp.dot(left, right, precision=lax.Precision.HIGHEST)

def reference(tokens, cotangent, first_gain, first_bias, query_weight, query_bias, key_weight, value_weight, value_bias, out_weight, out_bias, second_gain, second_bias, up_weight, up_bias, down_weight, down_bias, file_lengths, pad_mask):
    positions = jnp.arange(WINDOW, dtype=jnp.int32)
    doc_ends = jnp.cumsum(file_lengths).astype(jnp.int32)
    doc_ids = lax.optimization_barrier(jnp.sum((positions[:, None] >= doc_ends[None, :]).astype(jnp.int32), axis=1))
    block_rows = min(512, WINDOW)
    block_count = WINDOW // block_rows
    score_scale = 1.0 / math.sqrt(HS)

    def forward(stream, gain_one, bias_one, w_query, b_query, w_key, w_value, b_value, w_out, b_out, gain_two, bias_two, w_up, b_up, w_down, b_down):
        normed = low(layer_norm(stream, gain_one, bias_one))
        queries = low(low_back(matmul(normed, w_query) + b_query))
        keys = low(low_back(matmul(normed, w_key)))
        values = low(low_back(matmul(normed, w_value) + b_value))
        query_blocks = queries.reshape(block_count, block_rows, HEADS, HS)

        def attend(inputs):
            query_block, block_index = inputs
            query_pos = block_index * block_rows + jnp.arange(block_rows, dtype=jnp.int32)
            query_doc = lax.dynamic_slice_in_dim(doc_ids, block_index * block_rows, block_rows)
            allowed = (query_doc[:, None] == doc_ids[None, :]) & (positions[None, :] <= query_pos[:, None])
            allowed = allowed & ((pad_mask[None, :] == 1) | (positions[None, :] == query_pos[:, None]))
            scores = jnp.einsum('qhd,kd->hqk', query_block, keys, precision=lax.Precision.HIGHEST) * score_scale
            scores = low_back(scores)
            scores = jnp.where(allowed[None], scores, NEGATIVE)
            top_score = lax.optimization_barrier(jnp.max(scores, axis=-1, keepdims=True))
            expon = jnp.exp(scores - top_score)
            weights = low(expon / lax.optimization_barrier(jnp.sum(expon, axis=-1, keepdims=True)))
            result = jnp.einsum('hqk,kd->qhd', weights, values, precision=lax.Precision.HIGHEST)
            return result.reshape(block_rows, HEADS * HS)
        attended = lax.map(jax.checkpoint(attend), (query_blocks, jnp.arange(block_count, dtype=jnp.int32)))
        attended = low(low_back(attended.reshape(WINDOW, HEADS * HS)))
        mixed = low_back(matmul(attended, w_out) + b_out)
        middle = stream + mixed
        normed_two = low(layer_norm(middle, gain_two, bias_two))
        upward = low_back(matmul(normed_two, w_up) + b_up)
        hidden = low(gelu_tanh(upward))
        downward = low_back(matmul(hidden, w_down) + b_down)
        return middle + downward
    floats = (tokens, first_gain, first_bias, query_weight, query_bias, key_weight, value_weight, value_bias, out_weight, out_bias, second_gain, second_bias, up_weight, up_bias, down_weight, down_bias)
    floats = tuple((item.astype(jnp.float32) for item in floats))
    result, backward = jax.vjp(forward, *floats)
    grads = backward(cotangent.astype(jnp.float32))
    return (result.astype(jnp.bfloat16), grads[0], grads[1], grads[2], grads[3], grads[4], grads[5], grads[6], grads[7], grads[8], grads[9], grads[10], grads[11], grads[12], grads[13], grads[14], grads[15])
```

```python
import functools
import math

import jax
import jax.numpy as jnp
from jax import lax
from jax.experimental import pallas as pl
from jax.experimental.pallas import tpu as pltpu
from jax.sharding import PartitionSpec as P

EPSILON = 1e-05
NEGATIVE = -1e30
LOG2E = 1.4426950408889634
LN2 = 0.6931471805599453
NT = (((1,), (1,)), ((), ()))
NN = (((1,), (0,)), ((), ()))
TN = (((0,), (0,)), ((), ()))
MIB = 2**20


def mm(a, b, dims=NN):
    return lax.dot_general(a, b, dims, preferred_element_type=jnp.float32)


def attend_kernel(rows, keys, heads, size, first_ref, q_ref, kv_ref, start_ref, kid_ref, o_ref, lse_ref):
    i = pl.program_id(0)
    scale2 = LOG2E / math.sqrt(size)
    base = first_ref[pl.num_programs(0)] + i * rows
    row_pos = base + lax.broadcasted_iota(jnp.int32, (rows, 1), 0)
    row_start = start_ref[...]
    ones = jnp.ones((keys, size), jnp.bfloat16)

    def block(j, carry, diagonal):
        here = pl.ds(pl.multiple_of(j * keys, keys), keys)
        k = kv_ref[here, :size]
        v1 = jnp.concatenate([kv_ref[here, size:], ones], axis=1)
        kid = kid_ref[:, here]
        ok = kid >= row_start
        if diagonal:
            col = j * keys + lax.broadcasted_iota(jnp.int32, (1, keys), 1)
            ok = (ok & (kid <= row_pos)) | (col == row_pos)
        out = []
        for h in range(heads):
            top, acc = carry[h]
            s = jnp.where(ok, mm(q_ref[:, h * size : (h + 1) * size], k, NT) * scale2, NEGATIVE)
            new = jnp.maximum(top, jnp.max(s, axis=1, keepdims=True))
            w = jnp.exp2(s - new).astype(jnp.bfloat16)
            out.append((new, acc * jnp.exp2(top - new) + mm(w, v1)))
        return tuple(out)

    carry = tuple(
        (jnp.full((rows, 1), NEGATIVE, jnp.float32), jnp.zeros((rows, 2 * size), jnp.float32))
        for _ in range(heads)
    )
    full = base // keys
    carry = lax.fori_loop(first_ref[i], full, lambda j, c: block(j, c, False), carry)
    last = (base + rows + keys - 1) // keys
    carry = lax.fori_loop(full, last, lambda j, c: block(j, c, True), carry)
    for h in range(heads):
        top, acc = carry[h]
        total = acc[:, size:]
        o_ref[:, h * size : (h + 1) * size] = acc[:, :size] / total
        lse_ref[h : h + 1, :] = jnp.transpose(top + jnp.log2(total))[0:1]


def attend(q, kv, firsts, row_start, kid, rows, keys):
    total, wide = q.shape
    size = kv.shape[1] // 2
    heads = wide // size
    return pl.pallas_call(
        functools.partial(attend_kernel, rows, keys, heads, size),
        out_shape=(
            jax.ShapeDtypeStruct((total, wide), jnp.float32),
            jax.ShapeDtypeStruct((heads, total), jnp.float32),
        ),
        grid_spec=pltpu.PrefetchScalarGridSpec(
            num_scalar_prefetch=1,
            grid=(total // rows,),
            in_specs=[
                pl.BlockSpec((rows, wide), lambda i, f: (i, 0)),
                pl.BlockSpec(kv.shape, lambda i, f: (0, 0)),
                pl.BlockSpec((rows, 1), lambda i, f: (i, 0)),
                pl.BlockSpec((1, kid.shape[1]), lambda i, f: (0, 0)),
            ],
            out_specs=[
                pl.BlockSpec((rows, wide), lambda i, f: (i, 0)),
                pl.BlockSpec((heads, rows), lambda i, f: (0, i)),
            ],
        ),
        compiler_params=pltpu.CompilerParams(vmem_limit_bytes=40 * MIB),
        name="attend",
    )(firsts, q, kv, row_start, kid)


def attend_back_kernel(
    rows, keys, heads, size, first_ref, q_ref, do_ref, o_ref, lse_ref, kv_ref, start_ref, kid_ref,
    dq_ref, dkv_ref, acc_ref,
):
    i = pl.program_id(0)
    scale = 1.0 / math.sqrt(size)
    base = first_ref[pl.num_programs(0)] + i * rows
    row_pos = base + lax.broadcasted_iota(jnp.int32, (1, rows), 1)
    row_start = start_ref[...]

    @pl.when(i == 0)
    def _():
        acc_ref[...] = jnp.zeros_like(acc_ref)

    deltas = []
    for h in range(heads):
        cols = slice(h * size, (h + 1) * size)
        both = do_ref[:, cols].astype(jnp.float32) * o_ref[:, cols]
        deltas.append(jnp.sum(jnp.transpose(both), axis=0, keepdims=True))

    def block(j, carry, diagonal):
        here = pl.ds(pl.multiple_of(j * keys, keys), keys)
        k = kv_ref[here, :size]
        v = kv_ref[here, size:]
        kid = kid_ref[here, :]
        ok = kid >= row_start
        if diagonal:
            col = j * keys + lax.broadcasted_iota(jnp.int32, (keys, 1), 0)
            ok = (ok & (kid <= row_pos)) | (col == row_pos)
        out = []
        dk = acc_ref[here, :size]
        dv = acc_ref[here, size:]
        for h in range(heads):
            cols = slice(h * size, (h + 1) * size)
            q = q_ref[:, cols]
            do = do_ref[:, cols]
            s = mm(k, q, NT) * (scale * LOG2E) - lse_ref[h : h + 1, :]
            p = jnp.where(ok, jnp.exp2(s), 0.0)
            ds = (p * (mm(v, do, NT) - deltas[h])).astype(jnp.bfloat16)
            dv = dv + mm(p.astype(jnp.bfloat16), do)
            dk = dk + mm(ds, q)
            out.append(carry[h] + mm(ds, k, TN))
        acc_ref[here, :size] = dk
        acc_ref[here, size:] = dv
        return tuple(out)

    carry = tuple(jnp.zeros((rows, size), jnp.float32) for _ in range(heads))
    full = base // keys
    carry = lax.fori_loop(first_ref[i], full, lambda j, c: block(j, c, False), carry)
    last = (base + rows + keys - 1) // keys
    carry = lax.fori_loop(full, last, lambda j, c: block(j, c, True), carry)
    for h in range(heads):
        dq_ref[:, h * size : (h + 1) * size] = (carry[h] * scale).astype(dq_ref.dtype)

    @pl.when(i == pl.num_programs(0) - 1)
    def _():
        dkv_ref[:, :size] = (acc_ref[:, :size] * scale).astype(dkv_ref.dtype)
        dkv_ref[:, size:] = acc_ref[:, size:].astype(dkv_ref.dtype)


def attend_back(q, do, o, lse, kv, firsts, row_start, kid, rows, keys):
    total, wide = q.shape
    size = kv.shape[1] // 2
    heads = wide // size
    return pl.pallas_call(
        functools.partial(attend_back_kernel, rows, keys, heads, size),
        out_shape=(
            jax.ShapeDtypeStruct((total, wide), jnp.bfloat16),
            jax.ShapeDtypeStruct(kv.shape, jnp.bfloat16),
        ),
        grid_spec=pltpu.PrefetchScalarGridSpec(
            num_scalar_prefetch=1,
            grid=(total // rows,),
            in_specs=[
                pl.BlockSpec((rows, wide), lambda i, f: (i, 0)),
                pl.BlockSpec((rows, wide), lambda i, f: (i, 0)),
                pl.BlockSpec((rows, wide), lambda i, f: (i, 0)),
                pl.BlockSpec((heads, rows), lambda i, f: (0, i)),
                pl.BlockSpec(kv.shape, lambda i, f: (0, 0)),
                pl.BlockSpec((1, rows), lambda i, f: (0, i)),
                pl.BlockSpec((kid.shape[0], 1), lambda i, f: (0, 0)),
            ],
            out_specs=[
                pl.BlockSpec((rows, wide), lambda i, f: (i, 0)),
                pl.BlockSpec(kv.shape, lambda i, f: (0, 0)),
            ],
            scratch_shapes=[pltpu.VMEM(kv.shape, jnp.float32)],
        ),
        compiler_params=pltpu.CompilerParams(vmem_limit_bytes=48 * MIB),
        name="attend_back",
    )(firsts, q, do, o, lse, kv, row_start, kid)


def layer_norm(values, gain, bias):
    centre = jnp.mean(values, axis=-1, keepdims=True)
    centred = values - centre
    spread = jnp.mean(centred * centred, axis=-1, keepdims=True)
    return centred * lax.rsqrt(spread + EPSILON) * gain + bias


def gelu_tanh(values):
    return (
        0.5
        * values
        * (1.0 + jnp.tanh(0.7978845608028654 * (values + 0.044715 * values * values * values)))
    )


def positions_of(file_lengths, pad_mask, own_pos, rows, keys):
    files = jnp.arange(file_lengths.shape[0], dtype=jnp.int32)
    doc_ends = jnp.sum(
        jnp.where(files[:, None] <= files[None, :], file_lengths[:, None], 0), axis=0
    )
    row_start = jnp.max(
        jnp.where(doc_ends[None, :] <= own_pos[:, None], doc_ends[None, :], 0), axis=1
    )
    kid = jnp.where(pad_mask == 1, jnp.arange(pad_mask.shape[0], dtype=jnp.int32), -1)
    firsts = jnp.concatenate([row_start[::rows] // keys, own_pos[:1]])
    return firsts, row_start, kid


def shards(
    tokens,
    cotangent,
    first_gain,
    first_bias,
    query_weight,
    query_bias,
    key_weight,
    value_weight,
    value_bias,
    out_weight,
    out_bias,
    second_gain,
    second_bias,
    up_weight,
    up_bias,
    down_weight,
    down_bias,
    file_lengths,
    pad_mask,
):
    local_rows = tokens.shape[0]
    head_size = key_weight.shape[1]
    cp_index = lax.axis_index("cp")
    block_rows, block_keys = 512, 512
    own_pos = cp_index * local_rows + jnp.arange(local_rows, dtype=jnp.int32)
    firsts, row_start, kid = positions_of(file_lengths, pad_mask, own_pos, block_rows, block_keys)
    gain_one = first_gain.astype(jnp.float32)
    bias_one = first_bias.astype(jnp.float32)
    gain_two = second_gain.astype(jnp.float32)
    bias_two = second_bias.astype(jnp.float32)
    stream = tokens.astype(jnp.float32)
    cot_float = cotangent.astype(jnp.float32)
    kv_weight = jnp.concatenate([key_weight, value_weight], axis=1)
    kv_bias = jnp.concatenate([jnp.zeros_like(value_bias), value_bias]).astype(jnp.float32)

    def first_half(stream_in):
        normed_in = layer_norm(stream_in, gain_one, bias_one).astype(jnp.bfloat16)
        query_low = (
            jnp.dot(normed_in, query_weight, preferred_element_type=jnp.float32)
            + query_bias.astype(jnp.float32)
        ).astype(jnp.bfloat16)
        return (normed_in, query_low)

    def second_half(middle_in):
        normed_in = layer_norm(middle_in, gain_two, bias_two).astype(jnp.bfloat16)
        upward_in = jnp.dot(
            normed_in, up_weight, preferred_element_type=jnp.float32
        ) + up_bias.astype(jnp.float32)
        return (normed_in, upward_in, gelu_tanh(upward_in).astype(jnp.bfloat16))

    normed, queries = first_half(stream)
    kv_own = (jnp.dot(normed, kv_weight, preferred_element_type=jnp.float32) + kv_bias).astype(
        jnp.bfloat16
    )
    gathered = lax.all_gather(kv_own, "cp", axis=0, tiled=True)
    attn_f32, log_total = attend(
        queries, gathered, firsts, row_start[:, None], kid[None, :], block_rows, block_keys
    )
    attn_low = attn_f32.astype(jnp.bfloat16)
    mixed = lax.psum(
        jnp.dot(attn_low, out_weight, preferred_element_type=jnp.float32).astype(jnp.bfloat16), "tp"
    ).astype(jnp.float32)
    middle = stream + mixed + out_bias.astype(jnp.float32)
    normed_two, upward, hidden = second_half(middle)
    downward = lax.psum(
        jnp.dot(hidden, down_weight, preferred_element_type=jnp.float32).astype(jnp.bfloat16), "tp"
    ).astype(jnp.float32)
    block_out = (middle + downward + down_bias.astype(jnp.float32)).astype(jnp.bfloat16)
    down_grad = jnp.einsum("tf,td->fd", hidden, cotangent, preferred_element_type=jnp.float32)
    down_bias_grad = jnp.sum(cot_float, axis=0)
    grad_hidden = jnp.einsum(
        "td,fd->tf", cotangent, down_weight, preferred_element_type=jnp.float32
    )
    unused, gelu_back = jax.vjp(gelu_tanh, upward)
    grad_up = gelu_back(grad_hidden)[0].astype(jnp.bfloat16)
    up_grad = jnp.einsum("td,tf->df", normed_two, grad_up, preferred_element_type=jnp.float32)
    up_bias_grad = jnp.sum(grad_up.astype(jnp.float32), axis=0)
    unused, norm_two_back = jax.vjp(layer_norm, middle, gain_two, bias_two)
    grad_normed_two = lax.psum(
        jnp.einsum("tf,df->td", grad_up, up_weight, preferred_element_type=jnp.float32).astype(
            jnp.bfloat16
        ),
        "tp",
    ).astype(jnp.float32)
    grad_middle_norm, second_gain_grad, second_bias_grad = norm_two_back(grad_normed_two)
    grad_middle = cot_float + grad_middle_norm
    grad_mixed = grad_middle.astype(jnp.bfloat16)
    out_grad = jnp.einsum("ta,td->ad", attn_low, grad_mixed, preferred_element_type=jnp.float32)
    out_bias_grad = jnp.sum(grad_mixed.astype(jnp.float32), axis=0)
    grad_attn = jnp.einsum(
        "td,ad->ta", grad_mixed, out_weight, preferred_element_type=jnp.float32
    ).astype(jnp.bfloat16)
    grad_queries, key_value_parts = attend_back(
        queries, grad_attn, attn_f32, log_total, gathered, firsts,
        row_start[None, :], kid[:, None], block_rows, block_keys,
    )
    own_key_value = lax.psum_scatter(
        key_value_parts,
        "cp",
        scatter_dimension=0,
        tiled=True,
    )
    grad_from_queries = jnp.einsum(
        "ta,da->td", grad_queries, query_weight, preferred_element_type=jnp.float32
    )
    summed_input, summed_kv = (
        lax.psum(grad_from_queries.astype(jnp.bfloat16), "tp").astype(jnp.float32),
        lax.psum(own_key_value, "tp").astype(jnp.float32),
    )
    grad_kv = summed_kv.astype(jnp.bfloat16)
    grad_normed = summed_input + jnp.einsum(
        "tc,dc->td", grad_kv, kv_weight, preferred_element_type=jnp.float32
    )
    unused, norm_one_back = jax.vjp(layer_norm, stream, gain_one, bias_one)
    grad_stream, first_gain_grad, first_bias_grad = norm_one_back(grad_normed)
    tokens_grad = grad_middle + grad_stream
    query_grad = jnp.einsum("td,ta->da", normed, grad_queries, preferred_element_type=jnp.float32)
    query_bias_grad = jnp.sum(grad_queries.astype(jnp.float32), axis=0)
    kv_grad = jnp.einsum("td,tc->dc", normed, grad_kv, preferred_element_type=jnp.float32)
    value_bias_grad = jnp.sum(grad_kv[:, head_size:].astype(jnp.float32), axis=0)
    query_grad, kv_grad, up_grad = (
        lax.psum_scatter(
            query_grad.astype(jnp.bfloat16), "cp", scatter_dimension=0, tiled=True
        ).astype(jnp.float32),
        lax.psum_scatter(
            kv_grad.astype(jnp.bfloat16), "cp", scatter_dimension=0, tiled=True
        ).astype(jnp.float32),
        lax.psum_scatter(
            up_grad.astype(jnp.bfloat16), "cp", scatter_dimension=0, tiled=True
        ).astype(jnp.float32),
    )
    out_grad, down_grad = (
        lax.psum_scatter(
            out_grad.astype(jnp.bfloat16), "cp", scatter_dimension=1, tiled=True
        ).astype(jnp.float32),
        lax.psum_scatter(
            down_grad.astype(jnp.bfloat16), "cp", scatter_dimension=1, tiled=True
        ).astype(jnp.float32),
    )
    small_sums = (
        lax.psum(first_gain_grad.astype(jnp.bfloat16), "cp").astype(jnp.float32),
        lax.psum(first_bias_grad.astype(jnp.bfloat16), "cp").astype(jnp.float32),
        lax.psum(query_bias_grad.astype(jnp.bfloat16), "cp").astype(jnp.float32),
        lax.psum(value_bias_grad.astype(jnp.bfloat16), "cp").astype(jnp.float32),
        lax.psum(out_bias_grad.astype(jnp.bfloat16), "cp").astype(jnp.float32),
        lax.psum(second_gain_grad.astype(jnp.bfloat16), "cp").astype(jnp.float32),
        lax.psum(second_bias_grad.astype(jnp.bfloat16), "cp").astype(jnp.float32),
        lax.psum(up_bias_grad.astype(jnp.bfloat16), "cp").astype(jnp.float32),
        lax.psum(down_bias_grad.astype(jnp.bfloat16), "cp").astype(jnp.float32),
    )
    return (
        block_out,
        tokens_grad,
        small_sums[0],
        small_sums[1],
        query_grad,
        small_sums[2],
        kv_grad[:, :head_size],
        kv_grad[:, head_size:],
        small_sums[3],
        out_grad,
        small_sums[4],
        small_sums[5],
        small_sums[6],
        up_grad,
        small_sums[7],
        down_grad,
        small_sums[8],
    )


def solution(mesh):
    placed = (
        P("cp", None),
        P("cp", None),
        P(),
        P(),
        P(None, "tp"),
        P("tp"),
        P(),
        P(),
        P(),
        P("tp", None),
        P(),
        P(),
        P(),
        P(None, "tp"),
        P("tp"),
        P("tp", None),
        P(),
        P(),
        P(),
    )
    return jax.shard_map(
        shards,
        mesh=mesh,
        in_specs=placed,
        out_specs=(
            P("cp", None),
            P("cp", None),
            P(),
            P(),
            P("cp", "tp"),
            P("tp"),
            P("cp", None),
            P("cp", None),
            P(),
            P("tp", "cp"),
            P(),
            P(),
            P(),
            P("cp", "tp"),
            P("tp"),
            P("tp", "cp"),
            P(),
        ),
        check_vma=False,
    )
```

```python
import functools
import math

import jax
import jax.numpy as jnp
from jax import lax
from jax.experimental import pallas as pl
from jax.experimental.pallas import tpu as pltpu
from jax.sharding import PartitionSpec as P

EPSILON = 1e-05
NEGATIVE = -1e30
LOG2E = 1.4426950408889634
LN2 = 0.6931471805599453
NT = (((1,), (1,)), ((), ()))
NN = (((1,), (0,)), ((), ()))
TN = (((0,), (0,)), ((), ()))
MIB = 2**20


def mm(a, b, dims=NN):
    return lax.dot_general(a, b, dims, preferred_element_type=jnp.float32)


def attend_kernel(rows, keys, heads, size, first_ref, q_ref, kv_ref, start_ref, kid_ref, o_ref, lse_ref):
    i = pl.program_id(0)
    scale2 = LOG2E / math.sqrt(size)
    base = first_ref[pl.num_programs(0)] + i * rows
    row_pos = base + lax.broadcasted_iota(jnp.int32, (rows, 1), 0)
    row_start = start_ref[...]
    ones = jnp.ones((keys, size), jnp.bfloat16)

    def block(j, carry, diagonal):
        here = pl.ds(pl.multiple_of(j * keys, keys), keys)
        k = kv_ref[here, :size]
        v1 = jnp.concatenate([kv_ref[here, size:], ones], axis=1)
        kid = kid_ref[:, here]
        ok = kid >= row_start
        if diagonal:
            col = j * keys + lax.broadcasted_iota(jnp.int32, (1, keys), 1)
            ok = (ok & (kid <= row_pos)) | (col == row_pos)
        out = []
        for h in range(heads):
            top, acc = carry[h]
            s = jnp.where(ok, mm(q_ref[:, h * size : (h + 1) * size], k, NT) * scale2, NEGATIVE)
            new = jnp.maximum(top, jnp.max(s, axis=1, keepdims=True))
            w = jnp.exp2(s - new).astype(jnp.bfloat16)
            out.append((new, acc * jnp.exp2(top - new) + mm(w, v1)))
        return tuple(out)

    carry = tuple(
        (jnp.full((rows, 1), NEGATIVE, jnp.float32), jnp.zeros((rows, 2 * size), jnp.float32))
        for _ in range(heads)
    )
    full = base // keys
    carry = lax.fori_loop(first_ref[i], full, lambda j, c: block(j, c, False), carry)
    last = (base + rows + keys - 1) // keys
    carry = lax.fori_loop(full, last, lambda j, c: block(j, c, True), carry)
    for h in range(heads):
        top, acc = carry[h]
        total = acc[:, size:]
        o_ref[:, h * size : (h + 1) * size] = acc[:, :size] / total
        lse_ref[h : h + 1, :] = jnp.transpose(top + jnp.log2(total))[0:1]


def attend(q, kv, firsts, row_start, kid, rows, keys):
    total, wide = q.shape
    size = kv.shape[1] // 2
    heads = wide // size
    return pl.pallas_call(
        functools.partial(attend_kernel, rows, keys, heads, size),
        out_shape=(
            jax.ShapeDtypeStruct((total, wide), jnp.float32),
            jax.ShapeDtypeStruct((heads, total), jnp.float32),
        ),
        grid_spec=pltpu.PrefetchScalarGridSpec(
            num_scalar_prefetch=1,
            grid=(total // rows,),
            in_specs=[
                pl.BlockSpec((rows, wide), lambda i, f: (i, 0)),
                pl.BlockSpec(kv.shape, lambda i, f: (0, 0)),
                pl.BlockSpec((rows, 1), lambda i, f: (i, 0)),
                pl.BlockSpec((1, kid.shape[1]), lambda i, f: (0, 0)),
            ],
            out_specs=[
                pl.BlockSpec((rows, wide), lambda i, f: (i, 0)),
                pl.BlockSpec((heads, rows), lambda i, f: (0, i)),
            ],
        ),
        compiler_params=pltpu.CompilerParams(vmem_limit_bytes=40 * MIB),
        name="attend",
    )(firsts, q, kv, row_start, kid)


def attend_back_kernel(
    rows, keys, heads, size, first_ref, q_ref, do_ref, o_ref, lse_ref, kv_ref, start_ref, kid_ref,
    dq_ref, dkv_ref, acc_ref,
):
    i = pl.program_id(0)
    scale = 1.0 / math.sqrt(size)
    base = first_ref[pl.num_programs(0)] + i * rows
    row_pos = base + lax.broadcasted_iota(jnp.int32, (1, rows), 1)
    row_start = start_ref[...]

    @pl.when(i == 0)
    def _():
        acc_ref[...] = jnp.zeros_like(acc_ref)

    deltas = []
    for h in range(heads):
        cols = slice(h * size, (h + 1) * size)
        both = do_ref[:, cols].astype(jnp.float32) * o_ref[:, cols]
        deltas.append(jnp.sum(jnp.transpose(both), axis=0, keepdims=True))

    def block(j, carry, diagonal):
        here = pl.ds(pl.multiple_of(j * keys, keys), keys)
        k = kv_ref[here, :size]
        v = kv_ref[here, size:]
        kid = kid_ref[here, :]
        ok = kid >= row_start
        if diagonal:
            col = j * keys + lax.broadcasted_iota(jnp.int32, (keys, 1), 0)
            ok = (ok & (kid <= row_pos)) | (col == row_pos)
        out = []
        dk = acc_ref[here, :size]
        dv = acc_ref[here, size:]
        for h in range(heads):
            cols = slice(h * size, (h + 1) * size)
            q = q_ref[:, cols]
            do = do_ref[:, cols]
            s = mm(k, q, NT) * (scale * LOG2E) - lse_ref[h : h + 1, :]
            p = jnp.where(ok, jnp.exp2(s), 0.0)
            ds = (p * (mm(v, do, NT) - deltas[h])).astype(jnp.bfloat16)
            dv = dv + mm(p.astype(jnp.bfloat16), do)
            dk = dk + mm(ds, q)
            out.append(carry[h] + mm(ds, k, TN))
        acc_ref[here, :size] = dk
        acc_ref[here, size:] = dv
        return tuple(out)

    carry = tuple(jnp.zeros((rows, size), jnp.float32) for _ in range(heads))
    full = base // keys
    carry = lax.fori_loop(first_ref[i], full, lambda j, c: block(j, c, False), carry)
    last = (base + rows + keys - 1) // keys
    carry = lax.fori_loop(full, last, lambda j, c: block(j, c, True), carry)
    for h in range(heads):
        dq_ref[:, h * size : (h + 1) * size] = (carry[h] * scale).astype(dq_ref.dtype)

    @pl.when(i == pl.num_programs(0) - 1)
    def _():
        dkv_ref[:, :size] = (acc_ref[:, :size] * scale).astype(dkv_ref.dtype)
        dkv_ref[:, size:] = acc_ref[:, size:].astype(dkv_ref.dtype)


def attend_back(q, do, o, lse, kv, firsts, row_start, kid, rows, keys):
    total, wide = q.shape
    size = kv.shape[1] // 2
    heads = wide // size
    return pl.pallas_call(
        functools.partial(attend_back_kernel, rows, keys, heads, size),
        out_shape=(
            jax.ShapeDtypeStruct((total, wide), jnp.bfloat16),
            jax.ShapeDtypeStruct(kv.shape, jnp.bfloat16),
        ),
        grid_spec=pltpu.PrefetchScalarGridSpec(
            num_scalar_prefetch=1,
            grid=(total // rows,),
            in_specs=[
                pl.BlockSpec((rows, wide), lambda i, f: (i, 0)),
                pl.BlockSpec((rows, wide), lambda i, f: (i, 0)),
                pl.BlockSpec((rows, wide), lambda i, f: (i, 0)),
                pl.BlockSpec((heads, rows), lambda i, f: (0, i)),
                pl.BlockSpec(kv.shape, lambda i, f: (0, 0)),
                pl.BlockSpec((1, rows), lambda i, f: (0, i)),
                pl.BlockSpec((kid.shape[0], 1), lambda i, f: (0, 0)),
            ],
            out_specs=[
                pl.BlockSpec((rows, wide), lambda i, f: (i, 0)),
                pl.BlockSpec(kv.shape, lambda i, f: (0, 0)),
            ],
            scratch_shapes=[pltpu.VMEM(kv.shape, jnp.float32)],
        ),
        compiler_params=pltpu.CompilerParams(vmem_limit_bytes=48 * MIB),
        name="attend_back",
    )(firsts, q, do, o, lse, kv, row_start, kid)


MESH = pl.DeviceIdType.MESH


class Chain:
    def __init__(self, chunks, quarter, part, snd, out, mate, in0, in1, tmp, sems):
        tp = lax.axis_index("tp")
        self.n = lax.axis_size("tp") // 2
        self.p, self.c = tp // 2, tp % 2
        self.chunks, self.q = chunks, quarter
        self.part, self.snd, self.out, self.mate, self.in0, self.in1, self.tmp = part, snd, out, mate, in0, in1, tmp
        (self.mate_s, self.mate_r, self.ch_s, self.in0_r, self.in1_r, self.bl_s, self.br_s, self.bc_r, self.fin_s, self.fin_r) = sems
        self.roots = (self.n // 2 - 1, self.n // 2)
        self.reach = max(self.roots[0], self.n - 1 - self.roots[0])

    @staticmethod
    def sems(chunks):
        one, two = pltpu.SemaphoreType.DMA((chunks,)), pltpu.SemaphoreType.DMA((chunks, 2))
        return [one, one, two, two, one, two, two, two, two, two]

    def at(self, p, c):
        return {"tp": p * 2 + c}

    def rows(self, g, c, part):
        q = self.q
        return pl.ds(pl.multiple_of(g * (4 * q) + c * (2 * q) + part * q, q), q)

    def own(self, g, part):
        q = self.q
        return pl.ds(pl.multiple_of(g * (2 * q) + part * q, q), q)

    def copy(self, src, dst, s, r, p, c):
        return pltpu.make_async_remote_copy(src, dst, s, r, device_id=self.at(p, c), device_id_type=MESH)

    def mate_copy(self, g):
        q = self.q
        src = self.part.at[pl.ds(pl.multiple_of(g * (4 * q) + (1 - self.c) * (2 * q), 2 * q), 2 * q)]
        dst = self.mate.at[pl.ds(pl.multiple_of(g * (2 * q), 2 * q), 2 * q)]
        return self.copy(src, dst, self.mate_s.at[g], self.mate_r.at[g], self.p, 1 - self.c)

    def in_copy(self, g, k, to):
        return self.copy(self.snd.at[self.own(g, k)], self.in0.at[self.own(g, k)], self.ch_s.at[g, k], self.in0_r.at[g, k], to, self.c)

    def in1_copy(self, g, k, to):
        q = self.q
        dst = self.in1.at[pl.ds(pl.multiple_of(g * q, q), q)]
        return self.copy(self.snd.at[self.own(g, k)], dst, self.ch_s.at[g, k], self.in1_r.at[g], to, self.c)

    def out_copy(self, g, k, to, sem):
        here = self.out.at[self.rows(g, self.c, k)]
        return self.copy(here, here, sem.at[g, k], self.bc_r.at[g, k], to, self.c)

    def fin_copy(self, g, k):
        here = self.out.at[self.rows(g, self.c, k)]
        return self.copy(here, here, self.fin_s.at[g, k], self.fin_r.at[g, k], self.p, 1 - self.c)

    def lag_up(self, k):
        root = self.roots[k]
        return jnp.where(self.p == root, self.reach, jnp.where(self.p < root, self.p, self.n - 1 - self.p))

    def lag_down(self, k):
        return self.reach + jnp.abs(self.p - self.roots[k])

    def start_mate(self, g):
        self.mate_copy(g).start()

    def reduce(self, g, k):
        root, p, n, q = self.roots[k], self.p, self.n, self.q
        rows, own, tmp = self.rows(g, self.c, k), self.own(g, k), self.tmp
        tmp[...] = self.part[rows, :].astype(jnp.float32) + self.mate[own, :].astype(jnp.float32)

        @pl.when(((p > 0) & (p <= root)) | ((p > root) & (p < n - 1)))
        def _():
            self.in_copy(g, k, p).wait_recv()
            tmp[...] += self.in0[own, :].astype(jnp.float32)

        @pl.when((p == root) & (p < n - 1))
        def _():
            self.in1_copy(g, k, p).wait_recv()
            tmp[...] += self.in1[pl.ds(pl.multiple_of(g * q, q), q), :].astype(jnp.float32)

        @pl.when(p != root)
        def _():
            self.snd[own, :] = tmp[...].astype(jnp.bfloat16)

        @pl.when(p < root)
        def _():
            self.in_copy(g, k, p + 1).start()

        @pl.when(p > root + 1)
        def _():
            self.in_copy(g, k, p - 1).start()

        @pl.when(p == root + 1)
        def _():
            self.in1_copy(g, k, p - 1).start()

        @pl.when(p == root)
        def _():
            self.out[rows, :] = tmp[...].astype(jnp.bfloat16)
            self.spread(g, k)

    def spread(self, g, k):
        root, p, n = self.roots[k], self.p, self.n

        @pl.when((p <= root) & (p > 0))
        def _():
            self.out_copy(g, k, p - 1, self.bl_s).start()

        @pl.when((p >= root) & (p < n - 1))
        def _():
            self.out_copy(g, k, p + 1, self.br_s).start()

        self.fin_copy(g, k).start()

    def down(self, g, k):
        @pl.when(self.p != self.roots[k])
        def _():
            self.out_copy(g, k, self.p, self.bl_s).wait_recv()
            self.spread(g, k)

    def done(self, g):
        for k in range(2):
            self.fin_copy(g, k).wait_recv()

    def drain(self, g):
        p, n = self.p, self.n
        self.mate_copy(g).wait_send()
        for k, root in enumerate(self.roots):

            @pl.when(p != root)
            def _():
                self.in_copy(g, k, p).wait_send()

            @pl.when((p <= root) & (p > 0))
            def _():
                self.out_copy(g, k, p, self.bl_s).wait_send()

            @pl.when((p >= root) & (p < n - 1))
            def _():
                self.out_copy(g, k, p, self.br_s).wait_send()

            self.fin_copy(g, k).wait_send()


def greet_tp():
    tp = lax.axis_index("tp")
    n = lax.axis_size("tp") // 2
    p, c = tp // 2, tp % 2
    bar = pltpu.get_barrier_semaphore()
    pl.semaphore_signal(bar, 1, device_id={"tp": p * 2 + 1 - c}, device_id_type=MESH)

    @pl.when(p > 0)
    def _():
        pl.semaphore_signal(bar, 1, device_id={"tp": tp - 2}, device_id_type=MESH)

    @pl.when(p < n - 1)
    def _():
        pl.semaphore_signal(bar, 1, device_id={"tp": tp + 2}, device_id_type=MESH)

    pl.semaphore_wait(bar, 1 + (p > 0).astype(jnp.int32) + (p < n - 1).astype(jnp.int32))


def within(g, chunks):
    return (g >= 0) & (g < chunks)


def sum_kernel(chunks, slack, part, out, snd, mate, in0, in1, tmp, *sems):
    quarter = part.shape[0] // (4 * chunks)
    ch = Chain(chunks, quarter, part, snd, out, mate, in0, in1, tmp, sems)
    greet_tp()

    @pl.loop(0, chunks)
    def _(g):
        ch.start_mate(g)

    last = 2 * ch.reach + 1 + slack

    @pl.loop(0, chunks + last)
    def _(s):
        @pl.when(s < chunks)
        def _():
            ch.mate_copy(s).wait_recv()

        for k in range(2):
            g = s - ch.lag_up(k)

            @pl.when(within(g, chunks))
            def _():
                ch.reduce(g, k)

        for k in range(2):
            g = s - ch.lag_down(k) - slack

            @pl.when(within(g, chunks))
            def _():
                ch.down(g, k)

    @pl.loop(0, chunks)
    def _(g):
        ch.done(g)
        ch.drain(g)


def tp_sum(x, collective_id, chunks=16, slack=1):
    rows, wide = x.shape
    q = rows // (4 * chunks)
    return pl.pallas_call(
        functools.partial(sum_kernel, chunks, slack),
        out_shape=jax.ShapeDtypeStruct(x.shape, x.dtype),
        in_specs=[pl.BlockSpec(memory_space=pltpu.VMEM)],
        out_specs=pl.BlockSpec(memory_space=pltpu.VMEM),
        scratch_shapes=[
            pltpu.VMEM((rows // 2, wide), x.dtype),
            pltpu.VMEM((rows // 2, wide), x.dtype),
            pltpu.VMEM((rows // 2, wide), x.dtype),
            pltpu.VMEM((rows // 4, wide), x.dtype),
            pltpu.VMEM((q, wide), jnp.float32),
            *Chain.sems(chunks),
        ],
        compiler_params=pltpu.CompilerParams(
            collective_id=collective_id, has_side_effects=True, vmem_limit_bytes=48 * MIB
        ),
        name="tp_sum",
    )(x)


def layer_norm(values, gain, bias):
    centre = jnp.mean(values, axis=-1, keepdims=True)
    centred = values - centre
    spread = jnp.mean(centred * centred, axis=-1, keepdims=True)
    return centred * lax.rsqrt(spread + EPSILON) * gain + bias


def gelu_tanh(values):
    return (
        0.5
        * values
        * (1.0 + jnp.tanh(0.7978845608028654 * (values + 0.044715 * values * values * values)))
    )


def positions_of(file_lengths, pad_mask, own_pos, rows, keys):
    files = jnp.arange(file_lengths.shape[0], dtype=jnp.int32)
    doc_ends = jnp.sum(
        jnp.where(files[:, None] <= files[None, :], file_lengths[:, None], 0), axis=0
    )
    row_start = jnp.max(
        jnp.where(doc_ends[None, :] <= own_pos[:, None], doc_ends[None, :], 0), axis=1
    )
    kid = jnp.where(pad_mask == 1, jnp.arange(pad_mask.shape[0], dtype=jnp.int32), -1)
    firsts = jnp.concatenate([row_start[::rows] // keys, own_pos[:1]])
    return firsts, row_start, kid


def shards(
    tokens,
    cotangent,
    first_gain,
    first_bias,
    query_weight,
    query_bias,
    key_weight,
    value_weight,
    value_bias,
    out_weight,
    out_bias,
    second_gain,
    second_bias,
    up_weight,
    up_bias,
    down_weight,
    down_bias,
    file_lengths,
    pad_mask,
):
    local_rows = tokens.shape[0]
    head_size = key_weight.shape[1]
    cp_index = lax.axis_index("cp")
    block_rows, block_keys = 512, 512
    own_pos = cp_index * local_rows + jnp.arange(local_rows, dtype=jnp.int32)
    firsts, row_start, kid = positions_of(file_lengths, pad_mask, own_pos, block_rows, block_keys)
    gain_one = first_gain.astype(jnp.float32)
    bias_one = first_bias.astype(jnp.float32)
    gain_two = second_gain.astype(jnp.float32)
    bias_two = second_bias.astype(jnp.float32)
    stream = tokens.astype(jnp.float32)
    cot_float = cotangent.astype(jnp.float32)
    kv_weight = jnp.concatenate([key_weight, value_weight], axis=1)
    kv_bias = jnp.concatenate([jnp.zeros_like(value_bias), value_bias]).astype(jnp.float32)

    def first_half(stream_in):
        normed_in = layer_norm(stream_in, gain_one, bias_one).astype(jnp.bfloat16)
        query_low = (
            jnp.dot(normed_in, query_weight, preferred_element_type=jnp.float32)
            + query_bias.astype(jnp.float32)
        ).astype(jnp.bfloat16)
        return (normed_in, query_low)

    def second_half(middle_in):
        normed_in = layer_norm(middle_in, gain_two, bias_two).astype(jnp.bfloat16)
        upward_in = jnp.dot(
            normed_in, up_weight, preferred_element_type=jnp.float32
        ) + up_bias.astype(jnp.float32)
        return (normed_in, upward_in, gelu_tanh(upward_in).astype(jnp.bfloat16))

    normed, queries = first_half(stream)
    kv_own = (jnp.dot(normed, kv_weight, preferred_element_type=jnp.float32) + kv_bias).astype(
        jnp.bfloat16
    )
    gathered = lax.all_gather(kv_own, "cp", axis=0, tiled=True)
    attn_f32, log_total = attend(
        queries, gathered, firsts, row_start[:, None], kid[None, :], block_rows, block_keys
    )
    attn_low = attn_f32.astype(jnp.bfloat16)
    mixed = tp_sum(
        jnp.dot(attn_low, out_weight, preferred_element_type=jnp.float32).astype(jnp.bfloat16), 1
    ).astype(jnp.float32)
    middle = stream + mixed + out_bias.astype(jnp.float32)
    normed_two, upward, hidden = second_half(middle)
    downward = tp_sum(
        jnp.dot(hidden, down_weight, preferred_element_type=jnp.float32).astype(jnp.bfloat16), 2
    ).astype(jnp.float32)
    block_out = (middle + downward + down_bias.astype(jnp.float32)).astype(jnp.bfloat16)
    down_grad = jnp.einsum("tf,td->fd", hidden, cotangent, preferred_element_type=jnp.float32)
    down_bias_grad = jnp.sum(cot_float, axis=0)
    grad_hidden = jnp.einsum(
        "td,fd->tf", cotangent, down_weight, preferred_element_type=jnp.float32
    )
    unused, gelu_back = jax.vjp(gelu_tanh, upward)
    grad_up = gelu_back(grad_hidden)[0].astype(jnp.bfloat16)
    up_grad = jnp.einsum("td,tf->df", normed_two, grad_up, preferred_element_type=jnp.float32)
    up_bias_grad = jnp.sum(grad_up.astype(jnp.float32), axis=0)
    unused, norm_two_back = jax.vjp(layer_norm, middle, gain_two, bias_two)
    grad_normed_two = tp_sum(
        jnp.einsum("tf,df->td", grad_up, up_weight, preferred_element_type=jnp.float32).astype(
            jnp.bfloat16
        ),
        3,
    ).astype(jnp.float32)
    grad_middle_norm, second_gain_grad, second_bias_grad = norm_two_back(grad_normed_two)
    grad_middle = cot_float + grad_middle_norm
    grad_mixed = grad_middle.astype(jnp.bfloat16)
    out_grad = jnp.einsum("ta,td->ad", attn_low, grad_mixed, preferred_element_type=jnp.float32)
    out_bias_grad = jnp.sum(grad_mixed.astype(jnp.float32), axis=0)
    grad_attn = jnp.einsum(
        "td,ad->ta", grad_mixed, out_weight, preferred_element_type=jnp.float32
    ).astype(jnp.bfloat16)
    grad_queries, key_value_parts = attend_back(
        queries, grad_attn, attn_f32, log_total, gathered, firsts,
        row_start[None, :], kid[:, None], block_rows, block_keys,
    )
    own_key_value = lax.psum_scatter(
        key_value_parts,
        "cp",
        scatter_dimension=0,
        tiled=True,
    )
    grad_from_queries = jnp.einsum(
        "ta,da->td", grad_queries, query_weight, preferred_element_type=jnp.float32
    )
    summed_input, summed_kv = (
        tp_sum(grad_from_queries.astype(jnp.bfloat16), 4).astype(jnp.float32),
        lax.psum(own_key_value, "tp").astype(jnp.float32),
    )
    grad_kv = summed_kv.astype(jnp.bfloat16)
    grad_normed = summed_input + jnp.einsum(
        "tc,dc->td", grad_kv, kv_weight, preferred_element_type=jnp.float32
    )
    unused, norm_one_back = jax.vjp(layer_norm, stream, gain_one, bias_one)
    grad_stream, first_gain_grad, first_bias_grad = norm_one_back(grad_normed)
    tokens_grad = grad_middle + grad_stream
    query_grad = jnp.einsum("td,ta->da", normed, grad_queries, preferred_element_type=jnp.float32)
    query_bias_grad = jnp.sum(grad_queries.astype(jnp.float32), axis=0)
    kv_grad = jnp.einsum("td,tc->dc", normed, grad_kv, preferred_element_type=jnp.float32)
    value_bias_grad = jnp.sum(grad_kv[:, head_size:].astype(jnp.float32), axis=0)
    query_grad, kv_grad, up_grad = (
        lax.psum_scatter(
            query_grad.astype(jnp.bfloat16), "cp", scatter_dimension=0, tiled=True
        ).astype(jnp.float32),
        lax.psum_scatter(
            kv_grad.astype(jnp.bfloat16), "cp", scatter_dimension=0, tiled=True
        ).astype(jnp.float32),
        lax.psum_scatter(
            up_grad.astype(jnp.bfloat16), "cp", scatter_dimension=0, tiled=True
        ).astype(jnp.float32),
    )
    out_grad, down_grad = (
        lax.psum_scatter(
            out_grad.astype(jnp.bfloat16), "cp", scatter_dimension=1, tiled=True
        ).astype(jnp.float32),
        lax.psum_scatter(
            down_grad.astype(jnp.bfloat16), "cp", scatter_dimension=1, tiled=True
        ).astype(jnp.float32),
    )
    small_sums = (
        lax.psum(first_gain_grad.astype(jnp.bfloat16), "cp").astype(jnp.float32),
        lax.psum(first_bias_grad.astype(jnp.bfloat16), "cp").astype(jnp.float32),
        lax.psum(query_bias_grad.astype(jnp.bfloat16), "cp").astype(jnp.float32),
        lax.psum(value_bias_grad.astype(jnp.bfloat16), "cp").astype(jnp.float32),
        lax.psum(out_bias_grad.astype(jnp.bfloat16), "cp").astype(jnp.float32),
        lax.psum(second_gain_grad.astype(jnp.bfloat16), "cp").astype(jnp.float32),
        lax.psum(second_bias_grad.astype(jnp.bfloat16), "cp").astype(jnp.float32),
        lax.psum(up_bias_grad.astype(jnp.bfloat16), "cp").astype(jnp.float32),
        lax.psum(down_bias_grad.astype(jnp.bfloat16), "cp").astype(jnp.float32),
    )
    return (
        block_out,
        tokens_grad,
        small_sums[0],
        small_sums[1],
        query_grad,
        small_sums[2],
        kv_grad[:, :head_size],
        kv_grad[:, head_size:],
        small_sums[3],
        out_grad,
        small_sums[4],
        small_sums[5],
        small_sums[6],
        up_grad,
        small_sums[7],
        down_grad,
        small_sums[8],
    )


def solution(mesh):
    placed = (
        P("cp", None),
        P("cp", None),
        P(),
        P(),
        P(None, "tp"),
        P("tp"),
        P(),
        P(),
        P(),
        P("tp", None),
        P(),
        P(),
        P(),
        P(None, "tp"),
        P("tp"),
        P("tp", None),
        P(),
        P(),
        P(),
    )
    return jax.shard_map(
        shards,
        mesh=mesh,
        in_specs=placed,
        out_specs=(
            P("cp", None),
            P("cp", None),
            P(),
            P(),
            P("cp", "tp"),
            P("tp"),
            P("cp", None),
            P("cp", None),
            P(),
            P("tp", "cp"),
            P(),
            P(),
            P(),
            P("cp", "tp"),
            P("tp"),
            P("tp", "cp"),
            P(),
        ),
        check_vma=False,
    )
```

```python
import functools
import math

import jax
import jax.numpy as jnp
from jax import lax
from jax.experimental import pallas as pl
from jax.experimental.pallas import tpu as pltpu
from jax.sharding import PartitionSpec as P

EPSILON = 1e-05
NEGATIVE = -1e30
LOG2E = 1.4426950408889634
LN2 = 0.6931471805599453
NT = (((1,), (1,)), ((), ()))
NN = (((1,), (0,)), ((), ()))
TN = (((0,), (0,)), ((), ()))
MIB = 2**20


def mm(a, b, dims=NN):
    return lax.dot_general(a, b, dims, preferred_element_type=jnp.float32)


def attend_kernel(rows, keys, heads, size, first_ref, q_ref, kv_ref, start_ref, kid_ref, o_ref, lse_ref):
    i = pl.program_id(0)
    scale2 = LOG2E / math.sqrt(size)
    base = first_ref[pl.num_programs(0)] + i * rows
    row_pos = base + lax.broadcasted_iota(jnp.int32, (rows, 1), 0)
    row_start = start_ref[...]
    ones = jnp.ones((keys, size), jnp.bfloat16)

    def block(j, carry, diagonal):
        here = pl.ds(pl.multiple_of(j * keys, keys), keys)
        k = kv_ref[here, :size]
        v1 = jnp.concatenate([kv_ref[here, size:], ones], axis=1)
        kid = kid_ref[:, here]
        ok = kid >= row_start
        if diagonal:
            col = j * keys + lax.broadcasted_iota(jnp.int32, (1, keys), 1)
            ok = (ok & (kid <= row_pos)) | (col == row_pos)
        out = []
        for h in range(heads):
            top, acc = carry[h]
            s = jnp.where(ok, mm(q_ref[:, h * size : (h + 1) * size], k, NT) * scale2, NEGATIVE)
            new = jnp.maximum(top, jnp.max(s, axis=1, keepdims=True))
            w = jnp.exp2(s - new).astype(jnp.bfloat16)
            out.append((new, acc * jnp.exp2(top - new) + mm(w, v1)))
        return tuple(out)

    carry = tuple(
        (jnp.full((rows, 1), NEGATIVE, jnp.float32), jnp.zeros((rows, 2 * size), jnp.float32))
        for _ in range(heads)
    )
    full = base // keys
    carry = lax.fori_loop(first_ref[i], full, lambda j, c: block(j, c, False), carry)
    last = (base + rows + keys - 1) // keys
    carry = lax.fori_loop(full, last, lambda j, c: block(j, c, True), carry)
    for h in range(heads):
        top, acc = carry[h]
        total = acc[:, size:]
        o_ref[:, h * size : (h + 1) * size] = acc[:, :size] / total
        lse_ref[h : h + 1, :] = jnp.transpose(top + jnp.log2(total))[0:1]


def attend(q, kv, firsts, row_start, kid, rows, keys):
    total, wide = q.shape
    size = kv.shape[1] // 2
    heads = wide // size
    return pl.pallas_call(
        functools.partial(attend_kernel, rows, keys, heads, size),
        out_shape=(
            jax.ShapeDtypeStruct((total, wide), jnp.float32),
            jax.ShapeDtypeStruct((heads, total), jnp.float32),
        ),
        grid_spec=pltpu.PrefetchScalarGridSpec(
            num_scalar_prefetch=1,
            grid=(total // rows,),
            in_specs=[
                pl.BlockSpec((rows, wide), lambda i, f: (i, 0)),
                pl.BlockSpec(kv.shape, lambda i, f: (0, 0)),
                pl.BlockSpec((rows, 1), lambda i, f: (i, 0)),
                pl.BlockSpec((1, kid.shape[1]), lambda i, f: (0, 0)),
            ],
            out_specs=[
                pl.BlockSpec((rows, wide), lambda i, f: (i, 0)),
                pl.BlockSpec((heads, rows), lambda i, f: (0, i)),
            ],
        ),
        compiler_params=pltpu.CompilerParams(vmem_limit_bytes=40 * MIB),
        name="attend",
    )(firsts, q, kv, row_start, kid)


def attend_back_kernel(
    rows, keys, heads, size, first_ref, q_ref, do_ref, o_ref, lse_ref, kv_ref, start_ref, kid_ref,
    dq_ref, dkv_ref, acc_ref,
):
    i = pl.program_id(0)
    scale = 1.0 / math.sqrt(size)
    base = first_ref[pl.num_programs(0)] + i * rows
    row_pos = base + lax.broadcasted_iota(jnp.int32, (1, rows), 1)
    row_start = start_ref[...]

    @pl.when(i == 0)
    def _():
        acc_ref[...] = jnp.zeros_like(acc_ref)

    deltas = []
    for h in range(heads):
        cols = slice(h * size, (h + 1) * size)
        both = do_ref[:, cols].astype(jnp.float32) * o_ref[:, cols]
        deltas.append(jnp.sum(jnp.transpose(both), axis=0, keepdims=True))

    def block(j, carry, diagonal):
        here = pl.ds(pl.multiple_of(j * keys, keys), keys)
        k = kv_ref[here, :size]
        v = kv_ref[here, size:]
        kid = kid_ref[here, :]
        ok = kid >= row_start
        if diagonal:
            col = j * keys + lax.broadcasted_iota(jnp.int32, (keys, 1), 0)
            ok = (ok & (kid <= row_pos)) | (col == row_pos)
        out = []
        dk = acc_ref[here, :size]
        dv = acc_ref[here, size:]
        for h in range(heads):
            cols = slice(h * size, (h + 1) * size)
            q = q_ref[:, cols]
            do = do_ref[:, cols]
            s = mm(k, q, NT) * (scale * LOG2E) - lse_ref[h : h + 1, :]
            p = jnp.where(ok, jnp.exp2(s), 0.0)
            ds = (p * (mm(v, do, NT) - deltas[h])).astype(jnp.bfloat16)
            dv = dv + mm(p.astype(jnp.bfloat16), do)
            dk = dk + mm(ds, q)
            out.append(carry[h] + mm(ds, k, TN))
        acc_ref[here, :size] = dk
        acc_ref[here, size:] = dv
        return tuple(out)

    carry = tuple(jnp.zeros((rows, size), jnp.float32) for _ in range(heads))
    full = base // keys
    carry = lax.fori_loop(first_ref[i], full, lambda j, c: block(j, c, False), carry)
    last = (base + rows + keys - 1) // keys
    carry = lax.fori_loop(full, last, lambda j, c: block(j, c, True), carry)
    for h in range(heads):
        dq_ref[:, h * size : (h + 1) * size] = (carry[h] * scale).astype(dq_ref.dtype)

    @pl.when(i == pl.num_programs(0) - 1)
    def _():
        dkv_ref[:, :size] = (acc_ref[:, :size] * scale).astype(dkv_ref.dtype)
        dkv_ref[:, size:] = acc_ref[:, size:].astype(dkv_ref.dtype)


def attend_back(q, do, o, lse, kv, firsts, row_start, kid, rows, keys):
    total, wide = q.shape
    size = kv.shape[1] // 2
    heads = wide // size
    return pl.pallas_call(
        functools.partial(attend_back_kernel, rows, keys, heads, size),
        out_shape=(
            jax.ShapeDtypeStruct((total, wide), jnp.bfloat16),
            jax.ShapeDtypeStruct(kv.shape, jnp.bfloat16),
        ),
        grid_spec=pltpu.PrefetchScalarGridSpec(
            num_scalar_prefetch=1,
            grid=(total // rows,),
            in_specs=[
                pl.BlockSpec((rows, wide), lambda i, f: (i, 0)),
                pl.BlockSpec((rows, wide), lambda i, f: (i, 0)),
                pl.BlockSpec((rows, wide), lambda i, f: (i, 0)),
                pl.BlockSpec((heads, rows), lambda i, f: (0, i)),
                pl.BlockSpec(kv.shape, lambda i, f: (0, 0)),
                pl.BlockSpec((1, rows), lambda i, f: (0, i)),
                pl.BlockSpec((kid.shape[0], 1), lambda i, f: (0, 0)),
            ],
            out_specs=[
                pl.BlockSpec((rows, wide), lambda i, f: (i, 0)),
                pl.BlockSpec(kv.shape, lambda i, f: (0, 0)),
            ],
            scratch_shapes=[pltpu.VMEM(kv.shape, jnp.float32)],
        ),
        compiler_params=pltpu.CompilerParams(vmem_limit_bytes=48 * MIB),
        name="attend_back",
    )(firsts, q, do, o, lse, kv, row_start, kid)


MESH = pl.DeviceIdType.MESH


class Chain:
    def __init__(self, chunks, quarter, part, snd, out, mate, in0, in1, tmp, sems):
        tp = lax.axis_index("tp")
        self.n = lax.axis_size("tp") // 2
        self.p, self.c = tp // 2, tp % 2
        self.chunks, self.q = chunks, quarter
        self.part, self.snd, self.out, self.mate, self.in0, self.in1, self.tmp = part, snd, out, mate, in0, in1, tmp
        (self.mate_s, self.mate_r, self.ch_s, self.in0_r, self.in1_r, self.bl_s, self.br_s, self.bc_r, self.fin_s, self.fin_r) = sems
        self.roots = (self.n // 2 - 1, self.n // 2)
        self.reach = max(self.roots[0], self.n - 1 - self.roots[0])

    @staticmethod
    def sems(chunks):
        one, two = pltpu.SemaphoreType.DMA((chunks,)), pltpu.SemaphoreType.DMA((chunks, 2))
        return [one, one, two, two, one, two, two, two, two, two]

    def at(self, p, c):
        return {"tp": p * 2 + c}

    def rows(self, g, c, part):
        q = self.q
        return pl.ds(pl.multiple_of(g * (4 * q) + c * (2 * q) + part * q, q), q)

    def own(self, g, part):
        q = self.q
        return pl.ds(pl.multiple_of(g * (2 * q) + part * q, q), q)

    def copy(self, src, dst, s, r, p, c):
        return pltpu.make_async_remote_copy(src, dst, s, r, device_id=self.at(p, c), device_id_type=MESH)

    def mate_copy(self, g):
        q = self.q
        src = self.part.at[pl.ds(pl.multiple_of(g * (4 * q) + (1 - self.c) * (2 * q), 2 * q), 2 * q)]
        dst = self.mate.at[pl.ds(pl.multiple_of(g * (2 * q), 2 * q), 2 * q)]
        return self.copy(src, dst, self.mate_s.at[g], self.mate_r.at[g], self.p, 1 - self.c)

    def in_copy(self, g, k, to):
        return self.copy(self.snd.at[self.own(g, k)], self.in0.at[self.own(g, k)], self.ch_s.at[g, k], self.in0_r.at[g, k], to, self.c)

    def in1_copy(self, g, k, to):
        q = self.q
        dst = self.in1.at[pl.ds(pl.multiple_of(g * q, q), q)]
        return self.copy(self.snd.at[self.own(g, k)], dst, self.ch_s.at[g, k], self.in1_r.at[g], to, self.c)

    def out_copy(self, g, k, to, sem):
        here = self.out.at[self.rows(g, self.c, k)]
        return self.copy(here, here, sem.at[g, k], self.bc_r.at[g, k], to, self.c)

    def fin_copy(self, g, k):
        here = self.out.at[self.rows(g, self.c, k)]
        return self.copy(here, here, self.fin_s.at[g, k], self.fin_r.at[g, k], self.p, 1 - self.c)

    def lag_up(self, k):
        root = self.roots[k]
        return jnp.where(self.p == root, self.reach, jnp.where(self.p < root, self.p, self.n - 1 - self.p))

    def lag_down(self, k):
        return self.reach + jnp.abs(self.p - self.roots[k])

    def start_mate(self, g):
        self.mate_copy(g).start()

    def reduce(self, g, k):
        root, p, n, q = self.roots[k], self.p, self.n, self.q
        rows, own, tmp = self.rows(g, self.c, k), self.own(g, k), self.tmp
        tmp[...] = self.part[rows, :].astype(jnp.float32) + self.mate[own, :].astype(jnp.float32)

        @pl.when(((p > 0) & (p <= root)) | ((p > root) & (p < n - 1)))
        def _():
            self.in_copy(g, k, p).wait_recv()
            tmp[...] += self.in0[own, :].astype(jnp.float32)

        @pl.when((p == root) & (p < n - 1))
        def _():
            self.in1_copy(g, k, p).wait_recv()
            tmp[...] += self.in1[pl.ds(pl.multiple_of(g * q, q), q), :].astype(jnp.float32)

        @pl.when(p != root)
        def _():
            self.snd[own, :] = tmp[...].astype(jnp.bfloat16)

        @pl.when(p < root)
        def _():
            self.in_copy(g, k, p + 1).start()

        @pl.when(p > root + 1)
        def _():
            self.in_copy(g, k, p - 1).start()

        @pl.when(p == root + 1)
        def _():
            self.in1_copy(g, k, p - 1).start()

        @pl.when(p == root)
        def _():
            self.out[rows, :] = tmp[...].astype(jnp.bfloat16)
            self.spread(g, k)

    def spread(self, g, k):
        root, p, n = self.roots[k], self.p, self.n

        @pl.when((p <= root) & (p > 0))
        def _():
            self.out_copy(g, k, p - 1, self.bl_s).start()

        @pl.when((p >= root) & (p < n - 1))
        def _():
            self.out_copy(g, k, p + 1, self.br_s).start()

        self.fin_copy(g, k).start()

    def down(self, g, k):
        @pl.when(self.p != self.roots[k])
        def _():
            self.out_copy(g, k, self.p, self.bl_s).wait_recv()
            self.spread(g, k)

    def done(self, g):
        for k in range(2):
            self.fin_copy(g, k).wait_recv()

    def drain(self, g):
        p, n = self.p, self.n
        self.mate_copy(g).wait_send()
        for k, root in enumerate(self.roots):

            @pl.when(p != root)
            def _():
                self.in_copy(g, k, p).wait_send()

            @pl.when((p <= root) & (p > 0))
            def _():
                self.out_copy(g, k, p, self.bl_s).wait_send()

            @pl.when((p >= root) & (p < n - 1))
            def _():
                self.out_copy(g, k, p, self.br_s).wait_send()

            self.fin_copy(g, k).wait_send()


def greet_tp():
    tp = lax.axis_index("tp")
    n = lax.axis_size("tp") // 2
    p, c = tp // 2, tp % 2
    bar = pltpu.get_barrier_semaphore()
    pl.semaphore_signal(bar, 1, device_id={"tp": p * 2 + 1 - c}, device_id_type=MESH)

    @pl.when(p > 0)
    def _():
        pl.semaphore_signal(bar, 1, device_id={"tp": tp - 2}, device_id_type=MESH)

    @pl.when(p < n - 1)
    def _():
        pl.semaphore_signal(bar, 1, device_id={"tp": tp + 2}, device_id_type=MESH)

    pl.semaphore_wait(bar, 1 + (p > 0).astype(jnp.int32) + (p < n - 1).astype(jnp.int32))


def within(g, chunks):
    return (g >= 0) & (g < chunks)


def sum_kernel(chunks, slack, part, out, snd, mate, in0, in1, tmp, *sems):
    quarter = part.shape[0] // (4 * chunks)
    ch = Chain(chunks, quarter, part, snd, out, mate, in0, in1, tmp, sems)
    greet_tp()

    @pl.loop(0, chunks)
    def _(g):
        ch.start_mate(g)

    last = 2 * ch.reach + 1 + slack

    @pl.loop(0, chunks + last)
    def _(s):
        @pl.when(s < chunks)
        def _():
            ch.mate_copy(s).wait_recv()

        for k in range(2):
            g = s - ch.lag_up(k)

            @pl.when(within(g, chunks))
            def _():
                ch.reduce(g, k)

        for k in range(2):
            g = s - ch.lag_down(k) - slack

            @pl.when(within(g, chunks))
            def _():
                ch.down(g, k)

    @pl.loop(0, chunks)
    def _(g):
        ch.done(g)
        ch.drain(g)


def tp_sum(x, collective_id, chunks=16, slack=1):
    rows, wide = x.shape
    q = rows // (4 * chunks)
    return pl.pallas_call(
        functools.partial(sum_kernel, chunks, slack),
        out_shape=jax.ShapeDtypeStruct(x.shape, x.dtype),
        in_specs=[pl.BlockSpec(memory_space=pltpu.VMEM)],
        out_specs=pl.BlockSpec(memory_space=pltpu.VMEM),
        scratch_shapes=[
            pltpu.VMEM((rows // 2, wide), x.dtype),
            pltpu.VMEM((rows // 2, wide), x.dtype),
            pltpu.VMEM((rows // 2, wide), x.dtype),
            pltpu.VMEM((rows // 4, wide), x.dtype),
            pltpu.VMEM((q, wide), jnp.float32),
            *Chain.sems(chunks),
        ],
        compiler_params=pltpu.CompilerParams(
            collective_id=collective_id, has_side_effects=True, vmem_limit_bytes=48 * MIB
        ),
        name="tp_sum",
    )(x)


def chunk_rows(g, rows):
    return pl.ds(pl.multiple_of(g * rows, rows), rows)


def norm_parts(values):
    centre = jnp.mean(values, axis=1, keepdims=True)
    centred = values - centre
    inv = lax.rsqrt(jnp.mean(centred * centred, axis=1, keepdims=True) + EPSILON)
    return centred * inv, inv


def norm_back(grad, unit, inv, gain):
    e = grad * gain
    return inv * (
        e - jnp.mean(e, axis=1, keepdims=True) - unit * jnp.mean(e * unit, axis=1, keepdims=True)
    )


def greet(with_cp):
    tp, me = lax.axis_index("tp"), lax.axis_index("cp")
    n, groups = lax.axis_size("tp") // 2, lax.axis_size("cp")
    p, c = tp // 2, tp % 2
    bar = pltpu.get_barrier_semaphore()
    pl.semaphore_signal(bar, 1, device_id={"tp": p * 2 + 1 - c}, device_id_type=MESH)

    @pl.when(p > 0)
    def _():
        pl.semaphore_signal(bar, 1, device_id={"tp": tp - 2}, device_id_type=MESH)

    @pl.when(p < n - 1)
    def _():
        pl.semaphore_signal(bar, 1, device_id={"tp": tp + 2}, device_id_type=MESH)

    count = 1
    if with_cp:
        for i in range(1, groups):
            pl.semaphore_signal(bar, 1, device_id={"cp": lax.rem(me + i, groups)}, device_id_type=MESH)
        count += groups - 1
    pl.semaphore_wait(bar, count + (p > 0).astype(jnp.int32) + (p < n - 1).astype(jnp.int32))


def cp_copy(i, src, dst, send, recv):
    to = lax.rem(lax.axis_index("cp") + i + 1, lax.axis_size("cp"))
    return pltpu.make_async_remote_copy(
        src, dst, send.at[i], recv.at[i], device_id={"cp": to}, device_id_type=MESH
    )


SLACK = 1


def middle_kernel(
    chunks,
    attn, wo, vec, ub, tok_h, cot_h, wu_h, wd_h,
    out_h, gmix_h, gattn, down_own, up_h, outw, sums, usum,
    tok, cot, wu, wd, hid, h2, gup, pa, pb, out1, out2, snd, mate, in0, in1, tmp, down_in,
    load_s, save_s, gm_s, up_s, dn_s, dn_r,
    *sems,
):
    rows = tok.shape[0] // chunks
    groups, me = lax.axis_size("cp"), lax.axis_index("cp")
    wide = tok.shape[1]
    per = wide // groups
    bf = jnp.bfloat16
    third = len(sems) // 3
    shared = (mate, in0, in1, tmp)
    ch1 = Chain(chunks, rows // 4, pa, snd, out1, *shared, sems[:third])
    ch3 = Chain(chunks, rows // 4, pa, snd, out2, *shared, sems[third : 2 * third])
    ch2 = Chain(chunks, rows // 4, pb, snd, out2, *shared, sems[2 * third :])
    loads = [
        pltpu.make_async_copy(src, dst, load_s.at[i])
        for i, (src, dst) in enumerate(((tok_h, tok), (wu_h, wu), (wd_h, wd), (cot_h, cot)))
    ]
    for load in loads:
        load.start()
    greet(True)
    gain, bias, out_bias, down_bias = (vec[i : i + 1, :] for i in range(4))
    sums[...] = jnp.zeros_like(sums)
    usum[...] = jnp.zeros_like(usum)

    def project(g):
        r = chunk_rows(g, rows)
        pa[r, :] = mm(attn[r, :], wo[...]).astype(bf)
        ch1.start_mate(g)

    def middle_of(r):
        return tok[r, :].astype(jnp.float32) + out1[r, :].astype(jnp.float32) + out_bias

    def feed(g):
        r = chunk_rows(g, rows)
        ch1.done(g)
        unit, _ = norm_parts(middle_of(r))
        h2[r, :] = (unit * gain + bias).astype(bf)
        up = mm(h2[r, :], wu[...]) + ub[...]
        sq = up * up
        t = jnp.tanh(0.7978845608028654 * up * (1.0 + 0.044715 * sq))
        half = 0.5 * (1.0 + t)
        hid[r, :] = (half * up).astype(bf)
        slope = half + 0.5 * up * (1.0 - t * t) * (0.7978845608028654 * (1.0 + 3.0 * 0.044715 * sq))
        gu = (slope * mm(cot[r, :], wd[...], NT)).astype(bf)
        gup[r, :] = gu
        usum[...] += jnp.sum(gu.astype(jnp.float32), axis=0, keepdims=True)
        sums[0:1, :] += jnp.sum(cot[r, :].astype(jnp.float32), axis=0, keepdims=True)
        ch1.drain(g)
        pa[r, :] = mm(gup[r, :], wu[...], NT).astype(bf)
        ch3.start_mate(g)
        pb[r, :] = mm(hid[r, :], wd[...]).astype(bf)

    def back(g):
        r = chunk_rows(g, rows)
        ch3.done(g)
        unit, inv = norm_parts(middle_of(r))
        grad = out2[r, :].astype(jnp.float32)
        sums[1:2, :] += jnp.sum(grad * unit, axis=0, keepdims=True)
        sums[2:3, :] += jnp.sum(grad, axis=0, keepdims=True)
        gm = (cot[r, :].astype(jnp.float32) + norm_back(grad, unit, inv, gain)).astype(bf)
        sums[3:4, :] += jnp.sum(gm.astype(jnp.float32), axis=0, keepdims=True)
        ch3.drain(g)
        pa[r, :] = gm
        pltpu.make_async_copy(pa.at[r], gmix_h.at[r], gm_s.at[g]).start()
        gattn[r, :] = mm(gm, wo[...], NT).astype(bf)
        ch2.start_mate(g)

    def finish(g):
        r = chunk_rows(g, rows)
        ch2.done(g)
        ch2.drain(g)
        pb[r, :] = (middle_of(r) + out2[r, :].astype(jnp.float32) + down_bias).astype(bf)
        pltpu.make_async_copy(pb.at[r], out_h.at[r], save_s.at[g]).start()

    def down_copy(i):
        to = lax.rem(me + i + 1, groups)
        cols = pl.ds(pl.multiple_of(to * per, per), per)
        return cp_copy(i, wd.at[:, cols], down_in.at[i], dn_s, dn_r)

    def down_block(i):
        cols = pl.ds(pl.multiple_of(lax.rem(me + i + 1, groups) * per, per), per)
        part = mm(hid[...], cot[:, cols], TN)

        @pl.when(i < groups - 1)
        def _():
            wd[:, cols] = part.astype(bf)
            down_copy(i).start()

        @pl.when(i == groups - 1)
        def _():
            down_own[...] = part

    up_rows = wide // 4

    def up_copy(j):
        r = chunk_rows(j, up_rows)
        return pltpu.make_async_copy(wu.at[r], up_h.at[r], up_s.at[j])

    def up_block(j):
        r = chunk_rows(j, up_rows)
        wu[r, :] = mm(h2[:, r], gup[...], TN).astype(bf)
        up_copy(j).start()

    def serve(ch, s):
        for k in range(2):
            g = s - ch.lag_up(k)
            pl.when(within(g, chunks))(functools.partial(ch.reduce, g, k))
        for k in range(2):
            g = s - ch.lag_down(k) - SLACK
            pl.when(within(g, chunks))(functools.partial(ch.down, g, k))

    def due(ch, s):
        pl.when(within(s, chunks))(lambda: ch.mate_copy(s).wait_recv())

    turn = 2 * ch1.reach + SLACK
    project(0)
    project(1)

    @pl.loop(0, chunks + 3 * turn)
    def _(s):
        pl.when(s + 2 < chunks)(lambda: project(s + 2))
        due(ch1, s)
        serve(ch1, s)

        @pl.when(s == turn)
        def _():
            for load in loads:
                load.wait()

        g = s - turn
        pl.when(within(g, chunks))(functools.partial(feed, g))
        due(ch3, g)
        serve(ch3, g)
        g = s - 2 * turn
        pl.when(within(g, chunks))(functools.partial(back, g))
        due(ch2, g)
        serve(ch2, g)
        i = s - turn - chunks
        pl.when(within(i, groups))(functools.partial(down_block, i))
        j = i - groups
        pl.when(within(j, 4))(functools.partial(up_block, j))
        g = s - 3 * turn
        pl.when(within(g, chunks))(functools.partial(finish, g))

    for j in range(4):
        cols = slice(j * up_rows, (j + 1) * up_rows)
        outw[:, cols] = mm(attn[...], pa[:, cols], TN).astype(bf)

    @pl.loop(0, groups - 1)
    def _(i):
        down_copy(i).wait_recv()
        down_own[...] += down_in[i].astype(jnp.float32)
        down_copy(i).wait_send()

    @pl.loop(0, chunks)
    def _(g):
        r = chunk_rows(g, rows)
        pltpu.make_async_copy(pa.at[r], gmix_h.at[r], gm_s.at[g]).wait()
        pltpu.make_async_copy(pb.at[r], out_h.at[r], save_s.at[g]).wait()

    for j in range(4):
        up_copy(j).wait()


def middle(attn, tokens, cotangent, wo, wu, wd, vec, ub, groups, chunks=8):
    rows, wide = tokens.shape
    heads_wide, hidden = wo.shape[0], wu.shape[1]
    bf, f32 = jnp.bfloat16, jnp.float32
    sds, vm = jax.ShapeDtypeStruct, pltpu.VMEM
    v, a = pl.BlockSpec(memory_space=pltpu.VMEM), pl.BlockSpec(memory_space=pl.ANY)
    dma = pltpu.SemaphoreType.DMA
    return pl.pallas_call(
        functools.partial(middle_kernel, chunks),
        out_shape=(
            sds((rows, wide), bf),
            sds((rows, wide), bf),
            sds((rows, heads_wide), bf),
            sds((hidden, wide // groups), f32),
            sds((wide, hidden), bf),
            sds((heads_wide, wide), bf),
            sds((8, wide), f32),
            sds((1, hidden), f32),
        ),
        in_specs=[v, v, v, v, a, a, a, a],
        out_specs=(a, a, v, v, a, v, v, v),
        scratch_shapes=[
            vm((rows, wide), bf),
            vm((rows, wide), bf),
            vm((wide, hidden), bf),
            vm((hidden, wide), bf),
            vm((rows, hidden), bf),
            vm((rows, wide), bf),
            vm((rows, hidden), bf),
            vm((rows, wide), bf),
            vm((rows, wide), bf),
            vm((rows, wide), bf),
            vm((rows, wide), bf),
            vm((rows // 2, wide), bf),
            vm((rows // 2, wide), bf),
            vm((rows // 2, wide), bf),
            vm((rows // 4, wide), bf),
            vm((rows // (4 * chunks), wide), f32),
            vm((groups - 1, hidden, wide // groups), bf),
            dma((4,)), dma((chunks,)), dma((chunks,)), dma((4,)), dma((groups - 1,)), dma((groups - 1,)),
            *Chain.sems(chunks), *Chain.sems(chunks), *Chain.sems(chunks),
        ],
        compiler_params=pltpu.CompilerParams(
            collective_id=2, has_side_effects=True, vmem_limit_bytes=61 * MIB
        ),
        name="middle",
    )(attn, wo, vec, ub, tokens, cotangent, wu, wd)


def layer_norm(values, gain, bias):
    centre = jnp.mean(values, axis=-1, keepdims=True)
    centred = values - centre
    spread = jnp.mean(centred * centred, axis=-1, keepdims=True)
    return centred * lax.rsqrt(spread + EPSILON) * gain + bias


def positions_of(file_lengths, pad_mask, own_pos, rows, keys):
    files = jnp.arange(file_lengths.shape[0], dtype=jnp.int32)
    doc_ends = jnp.sum(
        jnp.where(files[:, None] <= files[None, :], file_lengths[:, None], 0), axis=0
    )
    row_start = jnp.max(
        jnp.where(doc_ends[None, :] <= own_pos[:, None], doc_ends[None, :], 0), axis=1
    )
    kid = jnp.where(pad_mask == 1, jnp.arange(pad_mask.shape[0], dtype=jnp.int32), -1)
    firsts = jnp.concatenate([row_start[::rows] // keys, own_pos[:1]])
    return firsts, row_start, kid


def shards(
    tokens,
    cotangent,
    first_gain,
    first_bias,
    query_weight,
    query_bias,
    key_weight,
    value_weight,
    value_bias,
    out_weight,
    out_bias,
    second_gain,
    second_bias,
    up_weight,
    up_bias,
    down_weight,
    down_bias,
    file_lengths,
    pad_mask,
):
    local_rows = tokens.shape[0]
    head_size = key_weight.shape[1]
    cp_index = lax.axis_index("cp")
    block_rows, block_keys = 512, 512
    own_pos = cp_index * local_rows + jnp.arange(local_rows, dtype=jnp.int32)
    firsts, row_start, kid = positions_of(file_lengths, pad_mask, own_pos, block_rows, block_keys)
    gain_one = first_gain.astype(jnp.float32)
    bias_one = first_bias.astype(jnp.float32)
    gain_two = second_gain.astype(jnp.float32)
    bias_two = second_bias.astype(jnp.float32)
    stream = tokens.astype(jnp.float32)
    kv_weight = jnp.concatenate([key_weight, value_weight], axis=1)
    kv_bias = jnp.concatenate([jnp.zeros_like(value_bias), value_bias]).astype(jnp.float32)

    def first_half(stream_in):
        normed_in = layer_norm(stream_in, gain_one, bias_one).astype(jnp.bfloat16)
        query_low = (
            jnp.dot(normed_in, query_weight, preferred_element_type=jnp.float32)
            + query_bias.astype(jnp.float32)
        ).astype(jnp.bfloat16)
        return (normed_in, query_low)

    normed, queries = first_half(stream)
    kv_own = (jnp.dot(normed, kv_weight, preferred_element_type=jnp.float32) + kv_bias).astype(
        jnp.bfloat16
    )
    gathered = lax.all_gather(kv_own, "cp", axis=0, tiled=True)
    attn_f32, log_total = attend(
        queries, gathered, firsts, row_start[:, None], kid[None, :], block_rows, block_keys
    )
    attn_low = attn_f32.astype(jnp.bfloat16)
    vec = jnp.concatenate(
        [
            jnp.stack([gain_two, bias_two, out_bias.astype(jnp.float32), down_bias.astype(jnp.float32)]),
            jnp.zeros((4, gain_two.shape[0]), jnp.float32),
        ]
    )
    block_out, grad_mixed, grad_attn, down_grad, up_grad, out_grad, sums, up_sum = middle(
        attn_low, tokens, cotangent, out_weight, up_weight, down_weight, vec,
        up_bias.astype(jnp.float32)[None], lax.axis_size("cp"),
    )
    grad_middle = grad_mixed.astype(jnp.float32)
    down_bias_grad, second_gain_grad, second_bias_grad, out_bias_grad = (sums[i] for i in range(4))
    up_bias_grad = up_sum[0]
    grad_queries, key_value_parts = attend_back(
        queries, grad_attn, attn_f32, log_total, gathered, firsts,
        row_start[None, :], kid[:, None], block_rows, block_keys,
    )
    own_key_value = lax.psum_scatter(
        key_value_parts,
        "cp",
        scatter_dimension=0,
        tiled=True,
    )
    grad_from_queries = jnp.einsum(
        "ta,da->td", grad_queries, query_weight, preferred_element_type=jnp.float32
    )
    summed_input, summed_kv = (
        tp_sum(grad_from_queries.astype(jnp.bfloat16), 4).astype(jnp.float32),
        lax.psum(own_key_value, "tp").astype(jnp.float32),
    )
    grad_kv = summed_kv.astype(jnp.bfloat16)
    grad_normed = summed_input + jnp.einsum(
        "tc,dc->td", grad_kv, kv_weight, preferred_element_type=jnp.float32
    )
    unused, norm_one_back = jax.vjp(layer_norm, stream, gain_one, bias_one)
    grad_stream, first_gain_grad, first_bias_grad = norm_one_back(grad_normed)
    tokens_grad = grad_middle + grad_stream
    query_grad = jnp.einsum("td,ta->da", normed, grad_queries, preferred_element_type=jnp.float32)
    query_bias_grad = jnp.sum(grad_queries.astype(jnp.float32), axis=0)
    kv_grad = jnp.einsum("td,tc->dc", normed, grad_kv, preferred_element_type=jnp.float32)
    value_bias_grad = jnp.sum(grad_kv[:, head_size:].astype(jnp.float32), axis=0)
    query_grad, kv_grad, up_grad = (
        lax.psum_scatter(
            query_grad.astype(jnp.bfloat16), "cp", scatter_dimension=0, tiled=True
        ).astype(jnp.float32),
        lax.psum_scatter(
            kv_grad.astype(jnp.bfloat16), "cp", scatter_dimension=0, tiled=True
        ).astype(jnp.float32),
        lax.psum_scatter(
            up_grad, "cp", scatter_dimension=0, tiled=True
        ).astype(jnp.float32),
    )
    out_grad = lax.psum_scatter(out_grad, "cp", scatter_dimension=1, tiled=True).astype(jnp.float32)
    small_sums = (
        lax.psum(first_gain_grad.astype(jnp.bfloat16), "cp").astype(jnp.float32),
        lax.psum(first_bias_grad.astype(jnp.bfloat16), "cp").astype(jnp.float32),
        lax.psum(query_bias_grad.astype(jnp.bfloat16), "cp").astype(jnp.float32),
        lax.psum(value_bias_grad.astype(jnp.bfloat16), "cp").astype(jnp.float32),
        lax.psum(out_bias_grad.astype(jnp.bfloat16), "cp").astype(jnp.float32),
        lax.psum(second_gain_grad.astype(jnp.bfloat16), "cp").astype(jnp.float32),
        lax.psum(second_bias_grad.astype(jnp.bfloat16), "cp").astype(jnp.float32),
        lax.psum(up_bias_grad.astype(jnp.bfloat16), "cp").astype(jnp.float32),
        lax.psum(down_bias_grad.astype(jnp.bfloat16), "cp").astype(jnp.float32),
    )
    return (
        block_out,
        tokens_grad,
        small_sums[0],
        small_sums[1],
        query_grad,
        small_sums[2],
        kv_grad[:, :head_size],
        kv_grad[:, head_size:],
        small_sums[3],
        out_grad,
        small_sums[4],
        small_sums[5],
        small_sums[6],
        up_grad,
        small_sums[7],
        down_grad,
        small_sums[8],
    )


def solution(mesh):
    placed = (
        P("cp", None),
        P("cp", None),
        P(),
        P(),
        P(None, "tp"),
        P("tp"),
        P(),
        P(),
        P(),
        P("tp", None),
        P(),
        P(),
        P(),
        P(None, "tp"),
        P("tp"),
        P("tp", None),
        P(),
        P(),
        P(),
    )
    return jax.shard_map(
        shards,
        mesh=mesh,
        in_specs=placed,
        out_specs=(
            P("cp", None),
            P("cp", None),
            P(),
            P(),
            P("cp", "tp"),
            P("tp"),
            P("cp", None),
            P("cp", None),
            P(),
            P("tp", "cp"),
            P(),
            P(),
            P(),
            P("cp", "tp"),
            P("tp"),
            P("tp", "cp"),
            P(),
        ),
        check_vma=False,
    )
```

```python
import functools
import math

import jax
import jax.numpy as jnp
from jax import lax
from jax.experimental import pallas as pl
from jax.experimental.pallas import tpu as pltpu
from jax.sharding import PartitionSpec as P

EPSILON = 1e-05
NEGATIVE = -1e30
LOG2E = 1.4426950408889634
LN2 = 0.6931471805599453
NT = (((1,), (1,)), ((), ()))
NN = (((1,), (0,)), ((), ()))
TN = (((0,), (0,)), ((), ()))
MIB = 2**20


def mm(a, b, dims=NN):
    return lax.dot_general(a, b, dims, preferred_element_type=jnp.float32)


def attend_kernel(rows, keys, heads, size, first_ref, q_ref, kv_ref, start_ref, kid_ref, o_ref, lse_ref):
    i = pl.program_id(0)
    scale2 = LOG2E / math.sqrt(size)
    base = first_ref[pl.num_programs(0)] + i * rows
    row_pos = base + lax.broadcasted_iota(jnp.int32, (rows, 1), 0)
    row_start = start_ref[...]
    ones = jnp.ones((keys, size), jnp.bfloat16)

    def block(j, carry, diagonal):
        here = pl.ds(pl.multiple_of(j * keys, keys), keys)
        k = kv_ref[here, :size]
        v1 = jnp.concatenate([kv_ref[here, size:], ones], axis=1)
        kid = kid_ref[:, here]
        ok = kid >= row_start
        if diagonal:
            col = j * keys + lax.broadcasted_iota(jnp.int32, (1, keys), 1)
            ok = (ok & (kid <= row_pos)) | (col == row_pos)
        out = []
        for h in range(heads):
            top, acc = carry[h]
            s = jnp.where(ok, mm(q_ref[:, h * size : (h + 1) * size], k, NT) * scale2, NEGATIVE)
            new = jnp.maximum(top, jnp.max(s, axis=1, keepdims=True))
            w = jnp.exp2(s - new).astype(jnp.bfloat16)
            out.append((new, acc * jnp.exp2(top - new) + mm(w, v1)))
        return tuple(out)

    carry = tuple(
        (jnp.full((rows, 1), NEGATIVE, jnp.float32), jnp.zeros((rows, 2 * size), jnp.float32))
        for _ in range(heads)
    )
    full = base // keys
    carry = lax.fori_loop(first_ref[i], full, lambda j, c: block(j, c, False), carry)
    last = (base + rows + keys - 1) // keys
    carry = lax.fori_loop(full, last, lambda j, c: block(j, c, True), carry)
    for h in range(heads):
        top, acc = carry[h]
        total = acc[:, size:]
        o_ref[:, h * size : (h + 1) * size] = acc[:, :size] / total
        lse_ref[h : h + 1, :] = jnp.transpose(top + jnp.log2(total))[0:1]


def attend(q, kv, firsts, row_start, kid, rows, keys):
    total, wide = q.shape
    size = kv.shape[1] // 2
    heads = wide // size
    return pl.pallas_call(
        functools.partial(attend_kernel, rows, keys, heads, size),
        out_shape=(
            jax.ShapeDtypeStruct((total, wide), jnp.float32),
            jax.ShapeDtypeStruct((heads, total), jnp.float32),
        ),
        grid_spec=pltpu.PrefetchScalarGridSpec(
            num_scalar_prefetch=1,
            grid=(total // rows,),
            in_specs=[
                pl.BlockSpec((rows, wide), lambda i, f: (i, 0)),
                pl.BlockSpec(kv.shape, lambda i, f: (0, 0)),
                pl.BlockSpec((rows, 1), lambda i, f: (i, 0)),
                pl.BlockSpec((1, kid.shape[1]), lambda i, f: (0, 0)),
            ],
            out_specs=[
                pl.BlockSpec((rows, wide), lambda i, f: (i, 0)),
                pl.BlockSpec((heads, rows), lambda i, f: (0, i)),
            ],
        ),
        compiler_params=pltpu.CompilerParams(vmem_limit_bytes=40 * MIB),
        name="attend",
    )(firsts, q, kv, row_start, kid)


def attend_back_kernel(
    rows, keys, heads, size, first_ref, q_ref, do_ref, o_ref, lse_ref, kv_ref, start_ref, kid_ref,
    dq_ref, dkv_ref, acc_ref,
):
    i = pl.program_id(0)
    scale = 1.0 / math.sqrt(size)
    base = first_ref[pl.num_programs(0)] + i * rows
    row_pos = base + lax.broadcasted_iota(jnp.int32, (1, rows), 1)
    row_start = start_ref[...]

    @pl.when(i == 0)
    def _():
        acc_ref[...] = jnp.zeros_like(acc_ref)

    deltas = []
    for h in range(heads):
        cols = slice(h * size, (h + 1) * size)
        both = do_ref[:, cols].astype(jnp.float32) * o_ref[:, cols]
        deltas.append(jnp.sum(jnp.transpose(both), axis=0, keepdims=True))

    def block(j, carry, diagonal):
        here = pl.ds(pl.multiple_of(j * keys, keys), keys)
        k = kv_ref[here, :size]
        v = kv_ref[here, size:]
        kid = kid_ref[here, :]
        ok = kid >= row_start
        if diagonal:
            col = j * keys + lax.broadcasted_iota(jnp.int32, (keys, 1), 0)
            ok = (ok & (kid <= row_pos)) | (col == row_pos)
        out = []
        dk = acc_ref[here, :size]
        dv = acc_ref[here, size:]
        for h in range(heads):
            cols = slice(h * size, (h + 1) * size)
            q = q_ref[:, cols]
            do = do_ref[:, cols]
            s = mm(k, q, NT) * (scale * LOG2E) - lse_ref[h : h + 1, :]
            p = jnp.where(ok, jnp.exp2(s), 0.0)
            ds = (p * (mm(v, do, NT) - deltas[h])).astype(jnp.bfloat16)
            dv = dv + mm(p.astype(jnp.bfloat16), do)
            dk = dk + mm(ds, q)
            out.append(carry[h] + mm(ds, k, TN))
        acc_ref[here, :size] = dk
        acc_ref[here, size:] = dv
        return tuple(out)

    carry = tuple(jnp.zeros((rows, size), jnp.float32) for _ in range(heads))
    full = base // keys
    carry = lax.fori_loop(first_ref[i], full, lambda j, c: block(j, c, False), carry)
    last = (base + rows + keys - 1) // keys
    carry = lax.fori_loop(full, last, lambda j, c: block(j, c, True), carry)
    for h in range(heads):
        dq_ref[:, h * size : (h + 1) * size] = (carry[h] * scale).astype(dq_ref.dtype)

    @pl.when(i == pl.num_programs(0) - 1)
    def _():
        dkv_ref[:, :size] = (acc_ref[:, :size] * scale).astype(dkv_ref.dtype)
        dkv_ref[:, size:] = acc_ref[:, size:].astype(dkv_ref.dtype)


def attend_back(q, do, o, lse, kv, firsts, row_start, kid, rows, keys):
    total, wide = q.shape
    size = kv.shape[1] // 2
    heads = wide // size
    return pl.pallas_call(
        functools.partial(attend_back_kernel, rows, keys, heads, size),
        out_shape=(
            jax.ShapeDtypeStruct((total, wide), jnp.bfloat16),
            jax.ShapeDtypeStruct(kv.shape, jnp.bfloat16),
        ),
        grid_spec=pltpu.PrefetchScalarGridSpec(
            num_scalar_prefetch=1,
            grid=(total // rows,),
            in_specs=[
                pl.BlockSpec((rows, wide), lambda i, f: (i, 0)),
                pl.BlockSpec((rows, wide), lambda i, f: (i, 0)),
                pl.BlockSpec((rows, wide), lambda i, f: (i, 0)),
                pl.BlockSpec((heads, rows), lambda i, f: (0, i)),
                pl.BlockSpec(kv.shape, lambda i, f: (0, 0)),
                pl.BlockSpec((1, rows), lambda i, f: (0, i)),
                pl.BlockSpec((kid.shape[0], 1), lambda i, f: (0, 0)),
            ],
            out_specs=[
                pl.BlockSpec((rows, wide), lambda i, f: (i, 0)),
                pl.BlockSpec(kv.shape, lambda i, f: (0, 0)),
            ],
            scratch_shapes=[pltpu.VMEM(kv.shape, jnp.float32)],
        ),
        compiler_params=pltpu.CompilerParams(vmem_limit_bytes=48 * MIB),
        name="attend_back",
    )(firsts, q, do, o, lse, kv, row_start, kid)


MESH = pl.DeviceIdType.MESH


class Chain:
    def __init__(self, chunks, quarter, part, snd, out, mate, in0, in1, tmp, sems):
        tp = lax.axis_index("tp")
        self.n = lax.axis_size("tp") // 2
        self.p, self.c = tp // 2, tp % 2
        self.chunks, self.q = chunks, quarter
        self.part, self.snd, self.out, self.mate, self.in0, self.in1, self.tmp = part, snd, out, mate, in0, in1, tmp
        (self.mate_s, self.mate_r, self.ch_s, self.in0_r, self.in1_r, self.bl_s, self.br_s, self.bc_r, self.fin_s, self.fin_r) = sems
        self.roots = (self.n // 2 - 1, self.n // 2)
        self.reach = max(self.roots[0], self.n - 1 - self.roots[0])

    @staticmethod
    def sems(chunks):
        one, two = pltpu.SemaphoreType.DMA((chunks,)), pltpu.SemaphoreType.DMA((chunks, 2))
        return [one, one, two, two, one, two, two, two, two, two]

    def at(self, p, c):
        return {"tp": p * 2 + c}

    def rows(self, g, c, part):
        q = self.q
        return pl.ds(pl.multiple_of(g * (4 * q) + c * (2 * q) + part * q, q), q)

    def own(self, g, part):
        q = self.q
        return pl.ds(pl.multiple_of(g * (2 * q) + part * q, q), q)

    def copy(self, src, dst, s, r, p, c):
        return pltpu.make_async_remote_copy(src, dst, s, r, device_id=self.at(p, c), device_id_type=MESH)

    def mate_copy(self, g):
        q = self.q
        src = self.part.at[pl.ds(pl.multiple_of(g * (4 * q) + (1 - self.c) * (2 * q), 2 * q), 2 * q)]
        dst = self.mate.at[pl.ds(pl.multiple_of(g * (2 * q), 2 * q), 2 * q)]
        return self.copy(src, dst, self.mate_s.at[g], self.mate_r.at[g], self.p, 1 - self.c)

    def in_copy(self, g, k, to):
        return self.copy(self.snd.at[self.own(g, k)], self.in0.at[self.own(g, k)], self.ch_s.at[g, k], self.in0_r.at[g, k], to, self.c)

    def in1_copy(self, g, k, to):
        q = self.q
        dst = self.in1.at[pl.ds(pl.multiple_of(g * q, q), q)]
        return self.copy(self.snd.at[self.own(g, k)], dst, self.ch_s.at[g, k], self.in1_r.at[g], to, self.c)

    def out_copy(self, g, k, to, sem):
        here = self.out.at[self.rows(g, self.c, k)]
        return self.copy(here, here, sem.at[g, k], self.bc_r.at[g, k], to, self.c)

    def fin_copy(self, g, k):
        here = self.out.at[self.rows(g, self.c, k)]
        return self.copy(here, here, self.fin_s.at[g, k], self.fin_r.at[g, k], self.p, 1 - self.c)

    def lag_up(self, k):
        root = self.roots[k]
        return jnp.where(self.p == root, self.reach, jnp.where(self.p < root, self.p, self.n - 1 - self.p))

    def lag_down(self, k):
        return self.reach + jnp.abs(self.p - self.roots[k])

    def start_mate(self, g):
        self.mate_copy(g).start()

    def reduce(self, g, k):
        root, p, n, q = self.roots[k], self.p, self.n, self.q
        rows, own, tmp = self.rows(g, self.c, k), self.own(g, k), self.tmp
        if self.mate is None:
            tmp[...] = self.part[rows, :].astype(jnp.float32)
        else:
            tmp[...] = self.part[rows, :].astype(jnp.float32) + self.mate[own, :].astype(jnp.float32)

        @pl.when(((p > 0) & (p <= root)) | ((p > root) & (p < n - 1)))
        def _():
            self.in_copy(g, k, p).wait_recv()
            tmp[...] += self.in0[own, :].astype(jnp.float32)

        @pl.when((p == root) & (p < n - 1))
        def _():
            self.in1_copy(g, k, p).wait_recv()
            tmp[...] += self.in1[pl.ds(pl.multiple_of(g * q, q), q), :].astype(jnp.float32)

        @pl.when(p != root)
        def _():
            self.snd[own, :] = tmp[...].astype(jnp.bfloat16)

        @pl.when(p < root)
        def _():
            self.in_copy(g, k, p + 1).start()

        @pl.when(p > root + 1)
        def _():
            self.in_copy(g, k, p - 1).start()

        @pl.when(p == root + 1)
        def _():
            self.in1_copy(g, k, p - 1).start()

        @pl.when(p == root)
        def _():
            self.out[rows, :] = tmp[...].astype(jnp.bfloat16)
            self.spread(g, k)

    def spread(self, g, k):
        root, p, n = self.roots[k], self.p, self.n

        @pl.when((p <= root) & (p > 0))
        def _():
            self.out_copy(g, k, p - 1, self.bl_s).start()

        @pl.when((p >= root) & (p < n - 1))
        def _():
            self.out_copy(g, k, p + 1, self.br_s).start()

        self.fin_copy(g, k).start()

    def down(self, g, k):
        @pl.when(self.p != self.roots[k])
        def _():
            self.out_copy(g, k, self.p, self.bl_s).wait_recv()
            self.spread(g, k)

    def done(self, g):
        for k in range(2):
            self.fin_copy(g, k).wait_recv()

    def drain(self, g):
        p, n = self.p, self.n
        if self.mate is not None:
            self.mate_copy(g).wait_send()
        for k, root in enumerate(self.roots):

            @pl.when(p != root)
            def _():
                self.in_copy(g, k, p).wait_send()

            @pl.when((p <= root) & (p > 0))
            def _():
                self.out_copy(g, k, p, self.bl_s).wait_send()

            @pl.when((p >= root) & (p < n - 1))
            def _():
                self.out_copy(g, k, p, self.br_s).wait_send()

            self.fin_copy(g, k).wait_send()


def within(g, chunks):
    return (g >= 0) & (g < chunks)


def chunk_rows(g, rows):
    return pl.ds(pl.multiple_of(g * rows, rows), rows)


def norm_parts(values):
    centre = jnp.mean(values, axis=1, keepdims=True)
    centred = values - centre
    inv = lax.rsqrt(jnp.mean(centred * centred, axis=1, keepdims=True) + EPSILON)
    return centred * inv, inv


def norm_back(grad, unit, inv, gain):
    e = grad * gain
    return inv * (
        e - jnp.mean(e, axis=1, keepdims=True) - unit * jnp.mean(e * unit, axis=1, keepdims=True)
    )


def greet(with_cp):
    tp, me = lax.axis_index("tp"), lax.axis_index("cp")
    n, groups = lax.axis_size("tp") // 2, lax.axis_size("cp")
    p, c = tp // 2, tp % 2
    bar = pltpu.get_barrier_semaphore()
    pl.semaphore_signal(bar, 1, device_id={"tp": p * 2 + 1 - c}, device_id_type=MESH)

    @pl.when(p > 0)
    def _():
        pl.semaphore_signal(bar, 1, device_id={"tp": tp - 2}, device_id_type=MESH)

    @pl.when(p < n - 1)
    def _():
        pl.semaphore_signal(bar, 1, device_id={"tp": tp + 2}, device_id_type=MESH)

    count = 1
    if with_cp:
        for i in range(1, groups):
            pl.semaphore_signal(bar, 1, device_id={"cp": lax.rem(me + i, groups)}, device_id_type=MESH)
        count += groups - 1
    pl.semaphore_wait(bar, count + (p > 0).astype(jnp.int32) + (p < n - 1).astype(jnp.int32))


def cp_copy(i, src, dst, send, recv):
    to = lax.rem(lax.axis_index("cp") + i + 1, lax.axis_size("cp"))
    return pltpu.make_async_remote_copy(
        src, dst, send.at[i], recv.at[i], device_id={"cp": to}, device_id_type=MESH
    )


SLACK = 1


def middle_kernel(
    chunks,
    attn, wo, vec, ub, tok_h, cot_h, wu_h, wd_h,
    out_h, gmix_h, gattn, down_own, up_h, outw, sums, usum,
    tok, cot, wu, wd, hid, h2, gup, pa, pb, out1, out2, snd, mate, in0, in1, tmp, down_in,
    load_s, save_s, gm_s, up_s, dn_s, dn_r,
    *sems,
):
    rows = tok.shape[0] // chunks
    groups, me = lax.axis_size("cp"), lax.axis_index("cp")
    wide = tok.shape[1]
    per = wide // groups
    bf = jnp.bfloat16
    third = len(sems) // 3
    shared = (mate, in0, in1, tmp)
    ch1 = Chain(chunks, rows // 4, pa, snd, out1, *shared, sems[:third])
    ch3 = Chain(chunks, rows // 4, pa, snd, out2, *shared, sems[third : 2 * third])
    ch2 = Chain(chunks, rows // 4, pb, snd, out2, *shared, sems[2 * third :])
    loads = [
        pltpu.make_async_copy(src, dst, load_s.at[i])
        for i, (src, dst) in enumerate(((tok_h, tok), (wu_h, wu), (wd_h, wd), (cot_h, cot)))
    ]
    for load in loads:
        load.start()
    greet(True)
    gain, bias, out_bias, down_bias = (vec[i : i + 1, :] for i in range(4))
    sums[...] = jnp.zeros_like(sums)
    usum[...] = jnp.zeros_like(usum)

    def project(g):
        r = chunk_rows(g, rows)
        pa[r, :] = mm(attn[r, :], wo[...]).astype(bf)
        ch1.start_mate(g)

    def middle_of(r):
        return tok[r, :].astype(jnp.float32) + out1[r, :].astype(jnp.float32) + out_bias

    def feed(g):
        r = chunk_rows(g, rows)
        ch1.done(g)
        unit, _ = norm_parts(middle_of(r))
        h2[r, :] = (unit * gain + bias).astype(bf)
        up = mm(h2[r, :], wu[...]) + ub[...]
        sq = up * up
        t = jnp.tanh(0.7978845608028654 * up * (1.0 + 0.044715 * sq))
        half = 0.5 * (1.0 + t)
        hid[r, :] = (half * up).astype(bf)
        slope = half + 0.5 * up * (1.0 - t * t) * (0.7978845608028654 * (1.0 + 3.0 * 0.044715 * sq))
        gu = (slope * mm(cot[r, :], wd[...], NT)).astype(bf)
        gup[r, :] = gu
        usum[...] += jnp.sum(gu.astype(jnp.float32), axis=0, keepdims=True)
        sums[0:1, :] += jnp.sum(cot[r, :].astype(jnp.float32), axis=0, keepdims=True)
        ch1.drain(g)
        pa[r, :] = mm(gup[r, :], wu[...], NT).astype(bf)
        ch3.start_mate(g)
        pb[r, :] = mm(hid[r, :], wd[...]).astype(bf)

    def back(g):
        r = chunk_rows(g, rows)
        ch3.done(g)
        unit, inv = norm_parts(middle_of(r))
        grad = out2[r, :].astype(jnp.float32)
        sums[1:2, :] += jnp.sum(grad * unit, axis=0, keepdims=True)
        sums[2:3, :] += jnp.sum(grad, axis=0, keepdims=True)
        gm = (cot[r, :].astype(jnp.float32) + norm_back(grad, unit, inv, gain)).astype(bf)
        sums[3:4, :] += jnp.sum(gm.astype(jnp.float32), axis=0, keepdims=True)
        ch3.drain(g)
        pa[r, :] = gm
        pltpu.make_async_copy(pa.at[r], gmix_h.at[r], gm_s.at[g]).start()
        gattn[r, :] = mm(gm, wo[...], NT).astype(bf)
        ch2.start_mate(g)

    def finish(g):
        r = chunk_rows(g, rows)
        ch2.done(g)
        ch2.drain(g)
        pb[r, :] = (middle_of(r) + out2[r, :].astype(jnp.float32) + down_bias).astype(bf)
        pltpu.make_async_copy(pb.at[r], out_h.at[r], save_s.at[g]).start()

    def down_copy(i):
        to = lax.rem(me + i + 1, groups)
        cols = pl.ds(pl.multiple_of(to * per, per), per)
        return cp_copy(i, wd.at[:, cols], down_in.at[i], dn_s, dn_r)

    def down_block(i):
        cols = pl.ds(pl.multiple_of(lax.rem(me + i + 1, groups) * per, per), per)
        part = mm(hid[...], cot[:, cols], TN)

        @pl.when(i < groups - 1)
        def _():
            wd[:, cols] = part.astype(bf)
            down_copy(i).start()

        @pl.when(i == groups - 1)
        def _():
            down_own[...] = part

    up_rows = wide // 4

    def up_copy(j):
        r = chunk_rows(j, up_rows)
        return pltpu.make_async_copy(wu.at[r], up_h.at[r], up_s.at[j])

    def up_block(j):
        r = chunk_rows(j, up_rows)
        wu[r, :] = mm(h2[:, r], gup[...], TN).astype(bf)
        up_copy(j).start()

    def serve(ch, s):
        for k in range(2):
            g = s - ch.lag_up(k)
            pl.when(within(g, chunks))(functools.partial(ch.reduce, g, k))
        for k in range(2):
            g = s - ch.lag_down(k) - SLACK
            pl.when(within(g, chunks))(functools.partial(ch.down, g, k))

    def due(ch, s):
        pl.when(within(s, chunks))(lambda: ch.mate_copy(s).wait_recv())

    turn = 2 * ch1.reach + SLACK
    project(0)
    project(1)

    @pl.loop(0, chunks + 3 * turn)
    def _(s):
        pl.when(s + 2 < chunks)(lambda: project(s + 2))
        due(ch1, s)
        serve(ch1, s)

        @pl.when(s == turn)
        def _():
            for load in loads:
                load.wait()

        g = s - turn
        pl.when(within(g, chunks))(functools.partial(feed, g))
        due(ch3, g)
        serve(ch3, g)
        g = s - 2 * turn
        pl.when(within(g, chunks))(functools.partial(back, g))
        due(ch2, g)
        serve(ch2, g)
        i = s - turn - chunks
        pl.when(within(i, groups))(functools.partial(down_block, i))
        j = i - groups
        pl.when(within(j, 4))(functools.partial(up_block, j))
        g = s - 3 * turn
        pl.when(within(g, chunks))(functools.partial(finish, g))

    for j in range(4):
        cols = slice(j * up_rows, (j + 1) * up_rows)
        outw[:, cols] = mm(attn[...], pa[:, cols], TN).astype(bf)

    @pl.loop(0, groups - 1)
    def _(i):
        down_copy(i).wait_recv()
        down_own[...] += down_in[i].astype(jnp.float32)
        down_copy(i).wait_send()

    @pl.loop(0, chunks)
    def _(g):
        r = chunk_rows(g, rows)
        pltpu.make_async_copy(pa.at[r], gmix_h.at[r], gm_s.at[g]).wait()
        pltpu.make_async_copy(pb.at[r], out_h.at[r], save_s.at[g]).wait()

    for j in range(4):
        up_copy(j).wait()


def middle(attn, tokens, cotangent, wo, wu, wd, vec, ub, groups, chunks=8):
    rows, wide = tokens.shape
    heads_wide, hidden = wo.shape[0], wu.shape[1]
    bf, f32 = jnp.bfloat16, jnp.float32
    sds, vm = jax.ShapeDtypeStruct, pltpu.VMEM
    v, a = pl.BlockSpec(memory_space=pltpu.VMEM), pl.BlockSpec(memory_space=pl.ANY)
    dma = pltpu.SemaphoreType.DMA
    return pl.pallas_call(
        functools.partial(middle_kernel, chunks),
        out_shape=(
            sds((rows, wide), bf),
            sds((rows, wide), bf),
            sds((rows, heads_wide), bf),
            sds((hidden, wide // groups), f32),
            sds((wide, hidden), bf),
            sds((heads_wide, wide), bf),
            sds((8, wide), f32),
            sds((1, hidden), f32),
        ),
        in_specs=[v, v, v, v, a, a, a, a],
        out_specs=(a, a, v, v, a, v, v, v),
        scratch_shapes=[
            vm((rows, wide), bf),
            vm((rows, wide), bf),
            vm((wide, hidden), bf),
            vm((hidden, wide), bf),
            vm((rows, hidden), bf),
            vm((rows, wide), bf),
            vm((rows, hidden), bf),
            vm((rows, wide), bf),
            vm((rows, wide), bf),
            vm((rows, wide), bf),
            vm((rows, wide), bf),
            vm((rows // 2, wide), bf),
            vm((rows // 2, wide), bf),
            vm((rows // 2, wide), bf),
            vm((rows // 4, wide), bf),
            vm((rows // (4 * chunks), wide), f32),
            vm((groups - 1, hidden, wide // groups), bf),
            dma((4,)), dma((chunks,)), dma((chunks,)), dma((4,)), dma((groups - 1,)), dma((groups - 1,)),
            *Chain.sems(chunks), *Chain.sems(chunks), *Chain.sems(chunks),
        ],
        compiler_params=pltpu.CompilerParams(
            collective_id=2, has_side_effects=True, vmem_limit_bytes=61 * MIB
        ),
        name="middle",
    )(attn, wo, vec, ub, tokens, cotangent, wu, wd)


KV_STEP = 3


def tail_kernel(
    chunks,
    gq, dkv, wq, wkv, vec, sums, usum, tok_h, gmix_h,
    tgrad_h, own, vout,
    tok, gmix, h1, pa, out1, snd, mate, in0, in1, tmp, kvm, kvs, kv_in, pkv, okv, ksnd, kin0, kin1, ktmp,
    stage, w_in, acc, v_in,
    load_s, save_s, km_s, km_r, kx_s, kx_r, w_s, w_r, v_s, v_r,
    *sems,
):
    local, wide = tok.shape
    rows = local // chunks
    groups, me = lax.axis_size("cp"), lax.axis_index("cp")
    core = lax.axis_index("tp") % 2
    tp = lax.axis_index("tp")
    per = wide // groups
    heads_wide, size = gq.shape[1], wkv.shape[1] // 2
    bf = jnp.bfloat16
    half = len(sems) // 2
    ch1 = Chain(chunks, rows // 4, pa, snd, out1, mate, in0, in1, tmp, sems[:half])
    chk = Chain(1, local // 4, pkv, ksnd, okv, None, kin0, kin1, ktmp, sems[half:])
    loads = [
        pltpu.make_async_copy(src, dst, load_s.at[i])
        for i, (src, dst) in enumerate(((tok_h, tok), (gmix_h, gmix)))
    ]
    for load in loads:
        load.start()
    greet(True)
    own_half = chunk_rows(core, local // 2)
    kv_mate = pltpu.make_async_remote_copy(
        dkv.at[:, chunk_rows(1 - core, local // 2), :], kvm, km_s, km_r,
        device_id={"tp": tp + 1 - 2 * core}, device_id_type=MESH,
    )
    kv_mate.start()
    gain, bias = vec[0:1, :], vec[1:2, :]

    def project(g):
        r = chunk_rows(g, rows)
        pa[r, :] = mm(gq[r, :], wq[...], NT).astype(bf)
        ch1.start_mate(g)

    project(0)
    project(1)
    acc[...] = sums[...]
    kv_mate.wait_recv()

    def kv_copy(i):
        to = lax.rem(me + i + 1, groups)
        return cp_copy(i, kvs.at[to], kv_in.at[i], kx_s, kx_r)

    @pl.loop(0, groups)
    def _(i):
        to = lax.rem(me + i + 1, groups)
        both = dkv[to, own_half, :].astype(jnp.float32) + kvm[to].astype(jnp.float32)
        kvs[to] = both.astype(bf)
        pl.when(i < groups - 1)(lambda: kv_copy(i).start())

    def normed(g):
        r = chunk_rows(g, rows)
        unit, _ = norm_parts(tok[r, :].astype(jnp.float32))
        h1[r, :] = (unit * gain + bias).astype(bf)

    def kv_gather():
        total = kvs[me].astype(jnp.float32)
        for i in range(groups - 1):
            kv_copy(i).wait_recv()
            total += kv_in[i].astype(jnp.float32)
        pkv[own_half, :] = total.astype(bf)

    def serve(ch, s, count, slack):
        for k in range(2):
            g = s - ch.lag_up(k)
            pl.when(within(g, count))(functools.partial(ch.reduce, g, k))
        for k in range(2):
            g = s - ch.lag_down(k) - slack
            pl.when(within(g, count))(functools.partial(ch.down, g, k))

    def w_copy(i):
        return cp_copy(i, stage.at[i], w_in.at[i], w_s, w_r)

    def weights(i):
        cols = pl.ds(pl.multiple_of(lax.rem(me + i + 1, groups) * per, per), per)
        part = mm(h1[:, cols], jnp.concatenate([gq[...], okv[...]], axis=1), TN)

        @pl.when(i < groups - 1)
        def _():
            stage[i] = part.astype(bf)
            w_copy(i).start()

        @pl.when(i == groups - 1)
        def _():
            own[...] = part

    def save(g):
        r = chunk_rows(g, rows)
        return pltpu.make_async_copy(pa.at[r], tgrad_h.at[r], save_s.at[g])

    def finish(g):
        r = chunk_rows(g, rows)
        ch1.done(g)
        ch1.drain(g)
        grad = out1[r, :].astype(jnp.float32) + mm(okv[r, :], wkv[...], NT)
        unit, inv = norm_parts(tok[r, :].astype(jnp.float32))
        acc[4:5, :] += jnp.sum(grad * unit, axis=0, keepdims=True)
        acc[5:6, :] += jnp.sum(grad, axis=0, keepdims=True)
        pa[r, :] = (gmix[r, :].astype(jnp.float32) + norm_back(grad, unit, inv, gain)).astype(bf)
        save(g).start()

    turn = 2 * ch1.reach + SLACK
    ready = KV_STEP + 2 * ch1.reach

    def finished(s):
        return jnp.clip(jnp.minimum(2 * (s - ready), s - turn + 1), 0, chunks)

    @pl.loop(0, max(chunks + turn, ready + 1 + chunks // 2, ready + 1 + groups))
    def _(s):
        pl.when(s + 2 < chunks)(lambda: project(s + 2))
        pl.when(within(s, chunks))(lambda: ch1.mate_copy(s).wait_recv())
        serve(ch1, s, chunks, SLACK)

        @pl.when(s == 0)
        def _():
            for load in loads:
                load.wait()

        pl.when(s < chunks)(lambda: normed(s))
        pl.when(s == KV_STEP)(kv_gather)
        serve(chk, s - KV_STEP, 1, 0)
        pl.when(s == ready)(lambda: chk.done(0))
        i = s - ready - 1
        pl.when(within(i, groups))(lambda: weights(i))
        pl.loop(finished(s - 1), finished(s))(finish)

    acc[6:7, 0 : usum.shape[1]] = usum[...]
    at = usum.shape[1]
    acc[6:7, at : at + heads_wide] = jnp.sum(gq[...].astype(jnp.float32), axis=0, keepdims=True)
    at += heads_wide
    acc[6:7, at : at + size] = jnp.sum(okv[:, size:].astype(jnp.float32), axis=0, keepdims=True)

    def v_copy(i):
        return cp_copy(i, acc, v_in.at[i], v_s, v_r)

    for i in range(groups - 1):
        v_copy(i).start()
    kv_mate.wait_send()
    chk.drain(0)

    @pl.loop(0, groups - 1)
    def _(i):
        w_copy(i).wait_recv()
        own[...] += w_in[i].astype(jnp.float32)
        w_copy(i).wait_send()
        kv_copy(i).wait_send()

    @pl.loop(0, chunks)
    def _(g):
        save(g).wait()

    total = jnp.zeros_like(acc)
    for i in range(groups - 1):
        v_copy(i).wait_recv()
    for source in range(groups):
        slot = lax.rem(me - source - 1 + groups, groups)
        theirs = v_in[jnp.minimum(slot, groups - 2)]
        total += jnp.where(slot == groups - 1, acc[...], theirs)
    vout[...] = total
    for i in range(groups - 1):
        v_copy(i).wait_send()


def tail(gq, dkv, wq, wkv, vec, sums, usum, tokens, grad_mixed, groups, chunks=8):
    rows, wide = tokens.shape
    heads_wide, two = gq.shape[1], wkv.shape[1]
    bf, f32 = jnp.bfloat16, jnp.float32
    sds, vm = jax.ShapeDtypeStruct, pltpu.VMEM
    v, a = pl.BlockSpec(memory_space=pltpu.VMEM), pl.BlockSpec(memory_space=pl.ANY)
    dma = pltpu.SemaphoreType.DMA
    per, both = wide // groups, heads_wide + two
    return pl.pallas_call(
        functools.partial(tail_kernel, chunks),
        out_shape=(sds((rows, wide), bf), sds((per, both), f32), sds((8, wide), f32)),
        in_specs=[v] * 7 + [a, a],
        out_specs=(a, v, v),
        scratch_shapes=[
            vm((rows, wide), bf),
            vm((rows, wide), bf),
            vm((rows, wide), bf),
            vm((rows, wide), bf),
            vm((rows, wide), bf),
            vm((rows // 2, wide), bf),
            vm((rows // 2, wide), bf),
            vm((rows // 2, wide), bf),
            vm((rows // 4, wide), bf),
            vm((rows // (4 * chunks), wide), f32),
            vm((groups, rows // 2, two), bf),
            vm((groups, rows // 2, two), bf),
            vm((groups - 1, rows // 2, two), bf),
            vm((rows, two), bf),
            vm((rows, two), bf),
            vm((rows // 2, two), bf),
            vm((rows // 2, two), bf),
            vm((rows // 4, two), bf),
            vm((rows // 4, two), f32),
            vm((groups - 1, per, both), bf),
            vm((groups - 1, per, both), bf),
            vm((8, wide), f32),
            vm((groups - 1, 8, wide), f32),
            dma((2,)), dma((chunks,)), dma, dma,
            dma((groups - 1,)), dma((groups - 1,)), dma((groups - 1,)), dma((groups - 1,)),
            dma((groups - 1,)), dma((groups - 1,)),
            *Chain.sems(chunks), *Chain.sems(1),
        ],
        compiler_params=pltpu.CompilerParams(
            collective_id=3, has_side_effects=True, vmem_limit_bytes=61 * MIB
        ),
        name="tail",
    )(gq, dkv, wq, wkv, vec, sums, usum, tokens, grad_mixed)


def layer_norm(values, gain, bias):
    centre = jnp.mean(values, axis=-1, keepdims=True)
    centred = values - centre
    spread = jnp.mean(centred * centred, axis=-1, keepdims=True)
    return centred * lax.rsqrt(spread + EPSILON) * gain + bias


def positions_of(file_lengths, pad_mask, own_pos, rows, keys):
    files = jnp.arange(file_lengths.shape[0], dtype=jnp.int32)
    doc_ends = jnp.sum(
        jnp.where(files[:, None] <= files[None, :], file_lengths[:, None], 0), axis=0
    )
    row_start = jnp.max(
        jnp.where(doc_ends[None, :] <= own_pos[:, None], doc_ends[None, :], 0), axis=1
    )
    kid = jnp.where(pad_mask == 1, jnp.arange(pad_mask.shape[0], dtype=jnp.int32), -1)
    firsts = jnp.concatenate([row_start[::rows] // keys, own_pos[:1]])
    return firsts, row_start, kid


def shards(
    tokens,
    cotangent,
    first_gain,
    first_bias,
    query_weight,
    query_bias,
    key_weight,
    value_weight,
    value_bias,
    out_weight,
    out_bias,
    second_gain,
    second_bias,
    up_weight,
    up_bias,
    down_weight,
    down_bias,
    file_lengths,
    pad_mask,
):
    local_rows = tokens.shape[0]
    head_size = key_weight.shape[1]
    cp_index = lax.axis_index("cp")
    block_rows, block_keys = 512, 512
    own_pos = cp_index * local_rows + jnp.arange(local_rows, dtype=jnp.int32)
    firsts, row_start, kid = positions_of(file_lengths, pad_mask, own_pos, block_rows, block_keys)
    gain_one = first_gain.astype(jnp.float32)
    bias_one = first_bias.astype(jnp.float32)
    gain_two = second_gain.astype(jnp.float32)
    bias_two = second_bias.astype(jnp.float32)
    stream = tokens.astype(jnp.float32)
    kv_weight = jnp.concatenate([key_weight, value_weight], axis=1)
    kv_bias = jnp.concatenate([jnp.zeros_like(value_bias), value_bias]).astype(jnp.float32)

    def first_half(stream_in):
        normed_in = layer_norm(stream_in, gain_one, bias_one).astype(jnp.bfloat16)
        query_low = (
            jnp.dot(normed_in, query_weight, preferred_element_type=jnp.float32)
            + query_bias.astype(jnp.float32)
        ).astype(jnp.bfloat16)
        return (normed_in, query_low)

    normed, queries = first_half(stream)
    kv_own = (jnp.dot(normed, kv_weight, preferred_element_type=jnp.float32) + kv_bias).astype(
        jnp.bfloat16
    )
    gathered = lax.all_gather(kv_own, "cp", axis=0, tiled=True)
    attn_f32, log_total = attend(
        queries, gathered, firsts, row_start[:, None], kid[None, :], block_rows, block_keys
    )
    attn_low = attn_f32.astype(jnp.bfloat16)
    vec = jnp.concatenate(
        [
            jnp.stack([gain_two, bias_two, out_bias.astype(jnp.float32), down_bias.astype(jnp.float32)]),
            jnp.zeros((4, gain_two.shape[0]), jnp.float32),
        ]
    )
    block_out, grad_mixed, grad_attn, down_grad, up_grad, out_grad, sums, up_sum = middle(
        attn_low, tokens, cotangent, out_weight, up_weight, down_weight, vec,
        up_bias.astype(jnp.float32)[None], lax.axis_size("cp"),
    )
    grad_queries, key_value_parts = attend_back(
        queries, grad_attn, attn_f32, log_total, gathered, firsts,
        row_start[None, :], kid[:, None], block_rows, block_keys,
    )
    tokens_low, own_grads, sums = tail(
        grad_queries, key_value_parts.reshape(-1, local_rows, 2 * head_size), query_weight, kv_weight,
        jnp.concatenate([jnp.stack([gain_one, bias_one]), jnp.zeros((6, gain_one.shape[0]), jnp.float32)]),
        sums, up_sum, tokens, grad_mixed, lax.axis_size("cp"),
    )
    tokens_grad = tokens_low.astype(jnp.float32)
    down_bias_grad, second_gain_grad, second_bias_grad, out_bias_grad = (sums[i] for i in range(4))
    first_gain_grad, first_bias_grad = sums[4], sums[5]
    hidden, heads_wide = up_weight.shape[1], query_weight.shape[1]
    up_bias_grad = sums[6, :hidden]
    query_bias_grad = sums[6, hidden : hidden + heads_wide]
    value_bias_grad = sums[6, hidden + heads_wide : hidden + heads_wide + head_size]
    query_grad = own_grads[:, :heads_wide]
    key_grad = own_grads[:, heads_wide : heads_wide + head_size]
    value_grad = own_grads[:, heads_wide + head_size :]
    up_grad = lax.psum_scatter(up_grad, "cp", scatter_dimension=0, tiled=True).astype(jnp.float32)
    out_grad = lax.psum_scatter(out_grad, "cp", scatter_dimension=1, tiled=True).astype(jnp.float32)
    return (
        block_out,
        tokens_grad,
        first_gain_grad,
        first_bias_grad,
        query_grad,
        query_bias_grad,
        key_grad,
        value_grad,
        value_bias_grad,
        out_grad,
        out_bias_grad,
        second_gain_grad,
        second_bias_grad,
        up_grad,
        up_bias_grad,
        down_grad,
        down_bias_grad,
    )


def solution(mesh):
    placed = (
        P("cp", None),
        P("cp", None),
        P(),
        P(),
        P(None, "tp"),
        P("tp"),
        P(),
        P(),
        P(),
        P("tp", None),
        P(),
        P(),
        P(),
        P(None, "tp"),
        P("tp"),
        P("tp", None),
        P(),
        P(),
        P(),
    )
    return jax.shard_map(
        shards,
        mesh=mesh,
        in_specs=placed,
        out_specs=(
            P("cp", None),
            P("cp", None),
            P(),
            P(),
            P("cp", "tp"),
            P("tp"),
            P("cp", None),
            P("cp", None),
            P(),
            P("tp", "cp"),
            P(),
            P(),
            P(),
            P("cp", "tp"),
            P("tp"),
            P("tp", "cp"),
            P(),
        ),
        check_vma=False,
    )
```

```python
import functools
import math

import jax
import jax.numpy as jnp
from jax import lax
from jax.experimental import pallas as pl
from jax.experimental.pallas import tpu as pltpu
from jax.sharding import PartitionSpec as P

EPSILON = 1e-05
NEGATIVE = -1e30
LOG2E = 1.4426950408889634
LN2 = 0.6931471805599453
NT = (((1,), (1,)), ((), ()))
NN = (((1,), (0,)), ((), ()))
TN = (((0,), (0,)), ((), ()))
MIB = 2**20


def mm(a, b, dims=NN):
    return lax.dot_general(a, b, dims, preferred_element_type=jnp.float32)


def file_start(lengths, pos):
    end, start = 0, jnp.zeros_like(pos)
    for i in range(lengths.shape[0]):
        end = end + lengths[i]
        start = jnp.where(pos >= end, end, start)
    return start


def key_ids(pad, j, keys):
    pos = j * keys + lax.broadcasted_iota(jnp.int32, (1, keys), 1)
    return jnp.where(pad[pl.ds(pl.multiple_of(j * keys, keys), keys)].reshape(1, -1) == 1, pos, -1)


def as_column(row):
    return jnp.transpose(jnp.broadcast_to(row, (128, row.shape[1])))[:, :1]


def attend_kernel(rows, keys, heads, size, len_ref, q_ref, kv_ref, pad_ref, o_ref, low_ref, lse_ref):
    scale2 = LOG2E / math.sqrt(size)
    base = (lax.axis_index("cp") * pl.num_programs(0) + pl.program_id(0)) * rows
    row_pos = base + lax.broadcasted_iota(jnp.int32, (rows, 1), 0)
    row_start = as_column(file_start(len_ref, base + lax.broadcasted_iota(jnp.int32, (1, rows), 1)))
    ones = jnp.ones((keys, size), jnp.bfloat16)

    def block(j, carry, diagonal):
        here = pl.ds(pl.multiple_of(j * keys, keys), keys)
        k = kv_ref[here, :size]
        v1 = jnp.concatenate([kv_ref[here, size:], ones], axis=1)
        kid = key_ids(pad_ref, j, keys)
        ok = kid >= row_start
        if diagonal:
            col = j * keys + lax.broadcasted_iota(jnp.int32, (1, keys), 1)
            ok = (ok & (kid <= row_pos)) | (col == row_pos)
        out = []
        for h in range(heads):
            top, acc = carry[h]
            s = jnp.where(ok, mm(q_ref[:, h * size : (h + 1) * size], k, NT) * scale2, NEGATIVE)
            new = jnp.maximum(top, jnp.max(s, axis=1, keepdims=True))
            w = jnp.exp2(s - new).astype(jnp.bfloat16)
            out.append((new, acc * jnp.exp2(top - new) + mm(w, v1)))
        return tuple(out)

    carry = tuple(
        (jnp.full((rows, 1), NEGATIVE, jnp.float32), jnp.zeros((rows, 2 * size), jnp.float32))
        for _ in range(heads)
    )
    full = base // keys
    carry = lax.fori_loop(file_start(len_ref, base) // keys, full, lambda j, c: block(j, c, False), carry)
    last = (base + rows + keys - 1) // keys
    carry = lax.fori_loop(full, last, lambda j, c: block(j, c, True), carry)
    for h in range(heads):
        top, acc = carry[h]
        total = acc[:, size:]
        out = acc[:, :size] / total
        o_ref[:, h * size : (h + 1) * size] = out
        low_ref[:, h * size : (h + 1) * size] = out.astype(jnp.bfloat16)
        lse_ref[h : h + 1, :] = jnp.transpose(top + jnp.log2(total))[0:1]


def attend(q, kv, lengths, pad, rows=512, keys=512):
    total, wide = q.shape
    size = kv.shape[1] // 2
    heads = wide // size
    by_row = pl.BlockSpec((rows, wide), lambda i, f: (i, 0))
    return pl.pallas_call(
        functools.partial(attend_kernel, rows, keys, heads, size),
        out_shape=(
            jax.ShapeDtypeStruct((total, wide), jnp.float32),
            jax.ShapeDtypeStruct((total, wide), jnp.bfloat16),
            jax.ShapeDtypeStruct((heads, total), jnp.float32),
        ),
        grid_spec=pltpu.PrefetchScalarGridSpec(
            num_scalar_prefetch=1,
            grid=(total // rows,),
            in_specs=[
                by_row,
                pl.BlockSpec(kv.shape, lambda i, f: (0, 0)),
                pl.BlockSpec(pad.shape, lambda i, f: (0,)),
            ],
            out_specs=[by_row, by_row, pl.BlockSpec((heads, rows), lambda i, f: (0, i))],
        ),
        compiler_params=pltpu.CompilerParams(vmem_limit_bytes=61 * MIB),
        name="attend",
    )(lengths, q, kv, pad)


def attend_back_kernel(
    rows, keys, heads, size, len_ref, q_ref, do_ref, o_ref, lse_ref, kv_ref, pad_ref, one_h, two_h,
    dq_ref, dkv_ref, one_o, two_o, acc_ref, one_v, two_v, pass_s,
):
    i = pl.program_id(0)
    scale = 1.0 / math.sqrt(size)
    base = (lax.axis_index("cp") * pl.num_programs(0) + i) * rows
    row_pos = base + lax.broadcasted_iota(jnp.int32, (1, rows), 1)
    row_start = file_start(len_ref, row_pos)
    fetched = [
        pltpu.make_async_copy(one_h, one_v, pass_s.at[0]),
        pltpu.make_async_copy(two_h, two_v, pass_s.at[1]),
    ]
    passed = [
        pltpu.make_async_copy(one_v, one_o, pass_s.at[2]),
        pltpu.make_async_copy(two_v, two_o, pass_s.at[3]),
    ]

    @pl.when(i == 0)
    def _():
        for copy in fetched:
            copy.start()
        acc_ref[...] = jnp.zeros_like(acc_ref)

    @pl.when(i == pl.num_programs(0) - 1)
    def _():
        for copy, onward in zip(fetched, passed):
            copy.wait()
            onward.start()

    deltas = []
    for h in range(heads):
        cols = slice(h * size, (h + 1) * size)
        both = do_ref[:, cols].astype(jnp.float32) * o_ref[:, cols]
        deltas.append(jnp.sum(jnp.transpose(both), axis=0, keepdims=True))

    def block(j, carry, diagonal):
        here = pl.ds(pl.multiple_of(j * keys, keys), keys)
        k = kv_ref[here, :size]
        v = kv_ref[here, size:]
        kid = as_column(key_ids(pad_ref, j, keys))
        ok = kid >= row_start
        if diagonal:
            col = j * keys + lax.broadcasted_iota(jnp.int32, (keys, 1), 0)
            ok = (ok & (kid <= row_pos)) | (col == row_pos)
        out = []
        dk = acc_ref[here, :size]
        dv = acc_ref[here, size:]
        for h in range(heads):
            cols = slice(h * size, (h + 1) * size)
            q = q_ref[:, cols]
            do = do_ref[:, cols]
            s = mm(k, q, NT) * (scale * LOG2E) - lse_ref[h : h + 1, :]
            p = jnp.where(ok, jnp.exp2(s), 0.0)
            ds = (p * (mm(v, do, NT) - deltas[h])).astype(jnp.bfloat16)
            dv = dv + mm(p.astype(jnp.bfloat16), do)
            dk = dk + mm(ds, q)
            out.append(carry[h] + mm(ds, k, TN))
        acc_ref[here, :size] = dk
        acc_ref[here, size:] = dv
        return tuple(out)

    carry = tuple(jnp.zeros((rows, size), jnp.float32) for _ in range(heads))
    full = base // keys
    carry = lax.fori_loop(file_start(len_ref, base) // keys, full, lambda j, c: block(j, c, False), carry)
    last = (base + rows + keys - 1) // keys
    carry = lax.fori_loop(full, last, lambda j, c: block(j, c, True), carry)
    for h in range(heads):
        dq_ref[:, h * size : (h + 1) * size] = (carry[h] * scale).astype(dq_ref.dtype)

    @pl.when(i == pl.num_programs(0) - 1)
    def _():
        dkv_ref[:, :size] = (acc_ref[:, :size] * scale).astype(dkv_ref.dtype)
        dkv_ref[:, size:] = acc_ref[:, size:].astype(dkv_ref.dtype)
        for copy in passed:
            copy.wait()


def attend_back(q, do, o, lse, kv, lengths, pad, one, two, rows=512, keys=512):
    total, wide = q.shape
    size = kv.shape[1] // 2
    heads = wide // size
    by_row = pl.BlockSpec((rows, wide), lambda i, f: (i, 0))
    whole = pl.BlockSpec(kv.shape, lambda i, f: (0, 0))
    far = pl.BlockSpec(memory_space=pl.ANY)
    return pl.pallas_call(
        functools.partial(attend_back_kernel, rows, keys, heads, size),
        out_shape=(
            jax.ShapeDtypeStruct((total, wide), jnp.bfloat16),
            jax.ShapeDtypeStruct(kv.shape, jnp.bfloat16),
            jax.ShapeDtypeStruct(one.shape, one.dtype),
            jax.ShapeDtypeStruct(two.shape, two.dtype),
        ),
        grid_spec=pltpu.PrefetchScalarGridSpec(
            num_scalar_prefetch=1,
            grid=(total // rows,),
            in_specs=[
                by_row,
                by_row,
                by_row,
                pl.BlockSpec((heads, rows), lambda i, f: (0, i)),
                whole,
                pl.BlockSpec(pad.shape, lambda i, f: (0,)),
                far,
                far,
            ],
            out_specs=[by_row, whole, far, far],
            scratch_shapes=[
                pltpu.VMEM(kv.shape, jnp.float32),
                pltpu.VMEM(one.shape, one.dtype),
                pltpu.VMEM(two.shape, two.dtype),
                pltpu.SemaphoreType.DMA((4,)),
            ],
        ),
        compiler_params=pltpu.CompilerParams(vmem_limit_bytes=61 * MIB),
        name="attend_back",
    )(lengths, q, do, o, lse, kv, pad, one, two)


def emit_kernel(heads_wide, hidden, low, up, out, own, sums, tokens_o, up_o, out_o, q_o, k_o, v_o, *vectors):
    tokens_o[...] = low[...].astype(jnp.float32)
    up_o[...] = up[...].astype(jnp.float32)
    out_o[...] = out[...].astype(jnp.float32)
    size = k_o.shape[1]
    q_o[...] = own[:, :heads_wide]
    k_o[...] = own[:, heads_wide : heads_wide + size]
    v_o[...] = own[:, heads_wide + size :]

    @pl.when(pl.program_id(0) == 0)
    def _():
        for i in range(6):
            vectors[i][...] = sums[i : i + 1, :].reshape(-1)
        at = 0
        for ref in vectors[6:]:
            ref[...] = sums[6:7, at : at + ref.shape[0]].reshape(-1)
            at += ref.shape[0]


def emit(low, up, out, own, sums, heads_wide, steps=8):
    size = (own.shape[1] - heads_wide) // 2
    wide, hidden = low.shape[1], up.shape[1]
    f32 = jnp.float32

    def rows_of(array, columns):
        return pl.BlockSpec((array.shape[0] // steps, columns), lambda i: (i, 0))

    lengths = (wide,) * 6 + (hidden, heads_wide, size)
    return pl.pallas_call(
        functools.partial(emit_kernel, heads_wide, hidden),
        out_shape=(
            jax.ShapeDtypeStruct(low.shape, f32),
            jax.ShapeDtypeStruct(up.shape, f32),
            jax.ShapeDtypeStruct(out.shape, f32),
            jax.ShapeDtypeStruct((own.shape[0], heads_wide), f32),
            jax.ShapeDtypeStruct((own.shape[0], size), f32),
            jax.ShapeDtypeStruct((own.shape[0], size), f32),
            *(jax.ShapeDtypeStruct((n,), f32) for n in lengths),
        ),
        grid=(steps,),
        in_specs=[
            *(rows_of(x, x.shape[1]) for x in (low, up, out, own)),
            pl.BlockSpec(sums.shape, lambda i: (0, 0)),
        ],
        out_specs=(
            *(rows_of(x, x.shape[1]) for x in (low, up, out)),
            rows_of(own, heads_wide),
            rows_of(own, size),
            rows_of(own, size),
            *(pl.BlockSpec((n,), lambda i: (0,)) for n in lengths),
        ),
        compiler_params=pltpu.CompilerParams(vmem_limit_bytes=61 * MIB),
        name="emit",
    )(low, up, out, own, sums)


def as_row(ref):
    return ref[...].astype(jnp.float32).reshape(1, -1)


MESH = pl.DeviceIdType.MESH


class Chain:
    def __init__(self, chunks, quarter, part, snd, out, mate, in0, in1, tmp, sems):
        tp = lax.axis_index("tp")
        self.n = lax.axis_size("tp") // 2
        self.p, self.c = tp // 2, tp % 2
        self.chunks, self.q = chunks, quarter
        self.part, self.snd, self.out, self.mate, self.in0, self.in1, self.tmp = part, snd, out, mate, in0, in1, tmp
        (self.mate_s, self.mate_r, self.ch_s, self.in0_r, self.in1_r, self.bl_s, self.br_s, self.bc_r, self.fin_s, self.fin_r) = sems
        self.roots = (self.n // 2 - 1, self.n // 2)
        self.reach = max(self.roots[0], self.n - 1 - self.roots[0])

    @staticmethod
    def sems(chunks):
        one, two = pltpu.SemaphoreType.DMA((chunks,)), pltpu.SemaphoreType.DMA((chunks, 2))
        return [one, one, two, two, one, two, two, two, two, two]

    def at(self, p, c):
        return {"tp": p * 2 + c}

    def rows(self, g, c, part):
        q = self.q
        return pl.ds(pl.multiple_of(g * (4 * q) + c * (2 * q) + part * q, q), q)

    def own(self, g, part):
        q = self.q
        return pl.ds(pl.multiple_of(g * (2 * q) + part * q, q), q)

    def copy(self, src, dst, s, r, p, c):
        return pltpu.make_async_remote_copy(src, dst, s, r, device_id=self.at(p, c), device_id_type=MESH)

    def mate_copy(self, g):
        q = self.q
        src = self.part.at[pl.ds(pl.multiple_of(g * (4 * q) + (1 - self.c) * (2 * q), 2 * q), 2 * q)]
        dst = self.mate.at[pl.ds(pl.multiple_of(g * (2 * q), 2 * q), 2 * q)]
        return self.copy(src, dst, self.mate_s.at[g], self.mate_r.at[g], self.p, 1 - self.c)

    def in_copy(self, g, k, to):
        return self.copy(self.snd.at[self.own(g, k)], self.in0.at[self.own(g, k)], self.ch_s.at[g, k], self.in0_r.at[g, k], to, self.c)

    def in1_copy(self, g, k, to):
        q = self.q
        dst = self.in1.at[pl.ds(pl.multiple_of(g * q, q), q)]
        return self.copy(self.snd.at[self.own(g, k)], dst, self.ch_s.at[g, k], self.in1_r.at[g], to, self.c)

    def out_copy(self, g, k, to, sem):
        here = self.out.at[self.rows(g, self.c, k)]
        return self.copy(here, here, sem.at[g, k], self.bc_r.at[g, k], to, self.c)

    def fin_copy(self, g, k):
        here = self.out.at[self.rows(g, self.c, k)]
        return self.copy(here, here, self.fin_s.at[g, k], self.fin_r.at[g, k], self.p, 1 - self.c)

    def lag_up(self, k):
        root = self.roots[k]
        return jnp.where(self.p == root, self.reach, jnp.where(self.p < root, self.p, self.n - 1 - self.p))

    def lag_down(self, k):
        return self.reach + jnp.abs(self.p - self.roots[k])

    def start_mate(self, g):
        self.mate_copy(g).start()

    def reduce(self, g, k):
        root, p, n, q = self.roots[k], self.p, self.n, self.q
        rows, own, tmp = self.rows(g, self.c, k), self.own(g, k), self.tmp
        if self.mate is None:
            tmp[...] = self.part[rows, :].astype(jnp.float32)
        else:
            tmp[...] = self.part[rows, :].astype(jnp.float32) + self.mate[own, :].astype(jnp.float32)

        @pl.when(((p > 0) & (p <= root)) | ((p > root) & (p < n - 1)))
        def _():
            self.in_copy(g, k, p).wait_recv()
            tmp[...] += self.in0[own, :].astype(jnp.float32)

        @pl.when((p == root) & (p < n - 1))
        def _():
            self.in1_copy(g, k, p).wait_recv()
            tmp[...] += self.in1[pl.ds(pl.multiple_of(g * q, q), q), :].astype(jnp.float32)

        @pl.when(p != root)
        def _():
            self.snd[own, :] = tmp[...].astype(jnp.bfloat16)

        @pl.when(p < root)
        def _():
            self.in_copy(g, k, p + 1).start()

        @pl.when(p > root + 1)
        def _():
            self.in_copy(g, k, p - 1).start()

        @pl.when(p == root + 1)
        def _():
            self.in1_copy(g, k, p - 1).start()

        @pl.when(p == root)
        def _():
            self.out[rows, :] = tmp[...].astype(jnp.bfloat16)
            self.spread(g, k)

    def spread(self, g, k):
        root, p, n = self.roots[k], self.p, self.n

        @pl.when((p <= root) & (p > 0))
        def _():
            self.out_copy(g, k, p - 1, self.bl_s).start()

        @pl.when((p >= root) & (p < n - 1))
        def _():
            self.out_copy(g, k, p + 1, self.br_s).start()

        self.fin_copy(g, k).start()

    def down(self, g, k):
        @pl.when(self.p != self.roots[k])
        def _():
            self.out_copy(g, k, self.p, self.bl_s).wait_recv()
            self.spread(g, k)

    def done(self, g):
        for k in range(2):
            self.fin_copy(g, k).wait_recv()

    def drain(self, g):
        p, n = self.p, self.n
        if self.mate is not None:
            self.mate_copy(g).wait_send()
        for k, root in enumerate(self.roots):

            @pl.when(p != root)
            def _():
                self.in_copy(g, k, p).wait_send()

            @pl.when((p <= root) & (p > 0))
            def _():
                self.out_copy(g, k, p, self.bl_s).wait_send()

            @pl.when((p >= root) & (p < n - 1))
            def _():
                self.out_copy(g, k, p, self.br_s).wait_send()

            self.fin_copy(g, k).wait_send()


def within(g, chunks):
    return (g >= 0) & (g < chunks)


def chunk_rows(g, rows):
    return pl.ds(pl.multiple_of(g * rows, rows), rows)


def norm_parts(values):
    centre = jnp.mean(values, axis=1, keepdims=True)
    centred = values - centre
    inv = lax.rsqrt(jnp.mean(centred * centred, axis=1, keepdims=True) + EPSILON)
    return centred * inv, inv


def norm_back(grad, unit, inv, gain):
    e = grad * gain
    return inv * (
        e - jnp.mean(e, axis=1, keepdims=True) - unit * jnp.mean(e * unit, axis=1, keepdims=True)
    )


def greet(chips, peers):
    tp, me = lax.axis_index("tp"), lax.axis_index("cp")
    n, groups = lax.axis_size("tp") // 2, lax.axis_size("cp")
    p, c = tp // 2, tp % 2
    bar = pltpu.get_barrier_semaphore()
    count = 1
    pl.semaphore_signal(bar, 1, device_id={"tp": p * 2 + 1 - c}, device_id_type=MESH)
    if chips:

        @pl.when(p > 0)
        def _():
            pl.semaphore_signal(bar, 1, device_id={"tp": tp - 2}, device_id_type=MESH)

        @pl.when(p < n - 1)
        def _():
            pl.semaphore_signal(bar, 1, device_id={"tp": tp + 2}, device_id_type=MESH)

        count += (p > 0).astype(jnp.int32) + (p < n - 1).astype(jnp.int32)
    if peers:
        for i in range(1, groups):
            pl.semaphore_signal(bar, 1, device_id={"cp": lax.rem(me + i, groups)}, device_id_type=MESH)
        count += groups - 1
    return lambda: pl.semaphore_wait(bar, count)


def cp_copy(i, src, dst, send, recv):
    to = lax.rem(lax.axis_index("cp") + i + 1, lax.axis_size("cp"))
    return pltpu.make_async_remote_copy(
        src, dst, send.at[i], recv.at[i], device_id={"cp": to}, device_id_type=MESH
    )


SLACK = 1


def middle_kernel(
    chunks,
    attn, wo, gain_v, bias_v, ob_v, db_v, ub_v, tok_h, cot_h, wu_h, wd_h,
    out_h, gmix_h, gattn, down_own, up_h, outw, sums, usum,
    tok, cot, wu, wd, hid, h2, gup, pa, pb, out1, out2, snd, mate, in0, in1, tmp, down_in,
    load_s, save_s, gm_s, up_s, dn_s, dn_r,
    *sems,
):
    rows = tok.shape[0] // chunks
    groups, me = lax.axis_size("cp"), lax.axis_index("cp")
    wide = tok.shape[1]
    per = wide // groups
    bf = jnp.bfloat16
    third = len(sems) // 3
    shared = (mate, in0, in1, tmp)
    ch1 = Chain(chunks, rows // 4, pa, snd, out1, *shared, sems[:third])
    ch3 = Chain(chunks, rows // 4, pa, snd, out2, *shared, sems[third : 2 * third])
    ch2 = Chain(chunks, rows // 4, pb, snd, out2, *shared, sems[2 * third :])
    loads = [
        pltpu.make_async_copy(src, dst, load_s.at[i])
        for i, (src, dst) in enumerate(((tok_h, tok), (wu_h, wu), (wd_h, wd), (cot_h, cot)))
    ]
    for load in loads:
        load.start()
    greet(True, True)()
    gain, bias, out_bias, down_bias, up_bias = (as_row(x) for x in (gain_v, bias_v, ob_v, db_v, ub_v))
    sums[...] = jnp.zeros_like(sums)
    usum[...] = jnp.zeros_like(usum)

    def project(g):
        r = chunk_rows(g, rows)
        pa[r, :] = mm(attn[r, :], wo[...]).astype(bf)
        ch1.start_mate(g)

    def middle_of(r):
        return tok[r, :].astype(jnp.float32) + out1[r, :].astype(jnp.float32) + out_bias

    def feed(g):
        r = chunk_rows(g, rows)
        ch1.done(g)
        unit, _ = norm_parts(middle_of(r))
        h2[r, :] = (unit * gain + bias).astype(bf)
        up = mm(h2[r, :], wu[...]) + up_bias
        sq = up * up
        t = jnp.tanh(0.7978845608028654 * up * (1.0 + 0.044715 * sq))
        half = 0.5 * (1.0 + t)
        hid[r, :] = (half * up).astype(bf)
        slope = half + 0.5 * up * (1.0 - t * t) * (0.7978845608028654 * (1.0 + 3.0 * 0.044715 * sq))
        gu = (slope * mm(cot[r, :], wd[...], NT)).astype(bf)
        gup[r, :] = gu
        usum[...] += jnp.sum(gu.astype(jnp.float32), axis=0, keepdims=True)
        sums[0:1, :] += jnp.sum(cot[r, :].astype(jnp.float32), axis=0, keepdims=True)
        ch1.drain(g)
        pa[r, :] = mm(gup[r, :], wu[...], NT).astype(bf)
        ch3.start_mate(g)
        pb[r, :] = mm(hid[r, :], wd[...]).astype(bf)

    def back(g):
        r = chunk_rows(g, rows)
        ch3.done(g)
        unit, inv = norm_parts(middle_of(r))
        grad = out2[r, :].astype(jnp.float32)
        sums[1:2, :] += jnp.sum(grad * unit, axis=0, keepdims=True)
        sums[2:3, :] += jnp.sum(grad, axis=0, keepdims=True)
        gm = (cot[r, :].astype(jnp.float32) + norm_back(grad, unit, inv, gain)).astype(bf)
        sums[3:4, :] += jnp.sum(gm.astype(jnp.float32), axis=0, keepdims=True)
        ch3.drain(g)
        pa[r, :] = gm
        pltpu.make_async_copy(pa.at[r], gmix_h.at[r], gm_s.at[g]).start()
        gattn[r, :] = mm(gm, wo[...], NT).astype(bf)
        ch2.start_mate(g)

    def finish(g):
        r = chunk_rows(g, rows)
        ch2.done(g)
        ch2.drain(g)
        pb[r, :] = (middle_of(r) + out2[r, :].astype(jnp.float32) + down_bias).astype(bf)
        pltpu.make_async_copy(pb.at[r], out_h.at[r], save_s.at[g]).start()

    def down_copy(i):
        to = lax.rem(me + i + 1, groups)
        cols = pl.ds(pl.multiple_of(to * per, per), per)
        return cp_copy(i, wd.at[:, cols], down_in.at[i], dn_s, dn_r)

    def down_block(i):
        cols = pl.ds(pl.multiple_of(lax.rem(me + i + 1, groups) * per, per), per)
        part = mm(hid[...], cot[:, cols], TN)

        @pl.when(i < groups - 1)
        def _():
            wd[:, cols] = part.astype(bf)
            down_copy(i).start()

        @pl.when(i == groups - 1)
        def _():
            down_own[...] = part

    up_rows = wide // 4

    def up_copy(j):
        r = chunk_rows(j, up_rows)
        return pltpu.make_async_copy(wu.at[r], up_h.at[r], up_s.at[j])

    def up_block(j):
        r = chunk_rows(j, up_rows)
        wu[r, :] = mm(h2[:, r], gup[...], TN).astype(bf)
        up_copy(j).start()

    def serve(ch, s):
        for k in range(2):
            g = s - ch.lag_up(k)
            pl.when(within(g, chunks))(functools.partial(ch.reduce, g, k))
        for k in range(2):
            g = s - ch.lag_down(k) - SLACK
            pl.when(within(g, chunks))(functools.partial(ch.down, g, k))

    def due(ch, s):
        pl.when(within(s, chunks))(lambda: ch.mate_copy(s).wait_recv())

    turn = 2 * ch1.reach + SLACK
    project(0)
    project(1)

    @pl.loop(0, chunks + 3 * turn)
    def _(s):
        pl.when(s + 2 < chunks)(lambda: project(s + 2))
        due(ch1, s)
        serve(ch1, s)

        @pl.when(s == turn)
        def _():
            for load in loads:
                load.wait()

        g = s - turn
        pl.when(within(g, chunks))(functools.partial(feed, g))
        due(ch3, g)
        serve(ch3, g)
        g = s - 2 * turn
        pl.when(within(g, chunks))(functools.partial(back, g))
        due(ch2, g)
        serve(ch2, g)
        i = s - turn - chunks
        pl.when(within(i, groups))(functools.partial(down_block, i))
        j = i - groups
        pl.when(within(j, 4))(functools.partial(up_block, j))
        g = s - 3 * turn
        pl.when(within(g, chunks))(functools.partial(finish, g))

    for j in range(4):
        cols = slice(j * up_rows, (j + 1) * up_rows)
        outw[:, cols] = mm(attn[...], pa[:, cols], TN).astype(bf)

    @pl.loop(0, groups - 1)
    def _(i):
        down_copy(i).wait_recv()
        down_own[...] += down_in[i].astype(jnp.float32)
        down_copy(i).wait_send()

    @pl.loop(0, chunks)
    def _(g):
        r = chunk_rows(g, rows)
        pltpu.make_async_copy(pa.at[r], gmix_h.at[r], gm_s.at[g]).wait()
        pltpu.make_async_copy(pb.at[r], out_h.at[r], save_s.at[g]).wait()

    for j in range(4):
        up_copy(j).wait()


def middle(attn, tokens, cotangent, wo, wu, wd, vectors, groups, chunks=8):
    rows, wide = tokens.shape
    heads_wide, hidden = wo.shape[0], wu.shape[1]
    bf, f32 = jnp.bfloat16, jnp.float32
    sds, vm = jax.ShapeDtypeStruct, pltpu.VMEM
    v, a = pl.BlockSpec(memory_space=pltpu.VMEM), pl.BlockSpec(memory_space=pl.ANY)
    dma = pltpu.SemaphoreType.DMA
    return pl.pallas_call(
        functools.partial(middle_kernel, chunks),
        out_shape=(
            sds((rows, wide), bf),
            sds((rows, wide), bf),
            sds((rows, heads_wide), bf),
            sds((hidden, wide // groups), f32),
            sds((wide, hidden), bf),
            sds((heads_wide, wide), bf),
            sds((8, wide), f32),
            sds((1, hidden), f32),
        ),
        in_specs=[v] * 7 + [a] * 4,
        out_specs=(a, a, v, v, a, v, v, v),
        scratch_shapes=[
            vm((rows, wide), bf),
            vm((rows, wide), bf),
            vm((wide, hidden), bf),
            vm((hidden, wide), bf),
            vm((rows, hidden), bf),
            vm((rows, wide), bf),
            vm((rows, hidden), bf),
            vm((rows, wide), bf),
            vm((rows, wide), bf),
            vm((rows, wide), bf),
            vm((rows, wide), bf),
            vm((rows // 2, wide), bf),
            vm((rows // 2, wide), bf),
            vm((rows // 2, wide), bf),
            vm((rows // 4, wide), bf),
            vm((rows // (4 * chunks), wide), f32),
            vm((groups - 1, hidden, wide // groups), bf),
            dma((4,)), dma((chunks,)), dma((chunks,)), dma((4,)), dma((groups - 1,)), dma((groups - 1,)),
            *Chain.sems(chunks), *Chain.sems(chunks), *Chain.sems(chunks),
        ],
        compiler_params=pltpu.CompilerParams(
            collective_id=2, has_side_effects=True, vmem_limit_bytes=61 * MIB
        ),
        name="middle",
    )(attn, wo, *vectors, tokens, cotangent, wu, wd)


HEAD_PARTS = 4


def head_kernel(
    gain_v, bias_v, qb_v, vb_v, tok_h, wq_h, wk_h, wv_h, q, kv, tok, h1, wq, wkv, load_s, w_s, x_s, x_r, f_s, f_r
):
    local = tok.shape[0]
    rows = local // HEAD_PARTS
    mine = HEAD_PARTS // 2
    groups, me = lax.axis_size("cp"), lax.axis_index("cp")
    tp = lax.axis_index("tp")
    core = tp % 2
    bf = jnp.bfloat16

    def load(part):
        r = chunk_rows(part, rows)
        return pltpu.make_async_copy(tok_h.at[r], tok.at[r], load_s.at[part])

    def part_at(i):
        return lax.rem(mine * core + i, HEAD_PARTS)

    def block(source, part):
        return pl.ds(pl.multiple_of(source * local + part * rows, rows), rows)

    def spread(j, i):
        here = kv.at[block(me, part_at(i))]
        to = lax.rem(me + j + 1, groups)
        return pltpu.make_async_remote_copy(
            here, here, x_s.at[j, i], x_r.at[j, i], device_id={"cp": to}, device_id_type=MESH
        )

    def forward(j, i):
        here = kv.at[block(lax.rem(me - j - 1 + groups, groups), part_at(i))]
        return pltpu.make_async_remote_copy(
            here, here, f_s.at[j, i], f_r.at[j, i], device_id={"tp": tp + 1 - 2 * core}, device_id_type=MESH
        )

    size = wk_h.shape[1]
    weights = [
        pltpu.make_async_copy(wk_h, wkv.at[:, pl.ds(0, size)], w_s.at[0]),
        pltpu.make_async_copy(wv_h, wkv.at[:, pl.ds(size, size)], w_s.at[1]),
        pltpu.make_async_copy(wq_h, wq, w_s.at[2]),
    ]
    load(part_at(0)).start()
    weights[0].start()
    weights[1].start()
    for i in range(1, HEAD_PARTS):
        load(part_at(i)).start()
    weights[2].start()
    greeted = greet(False, True)
    gain, bias, q_bias, v_bias = (as_row(x) for x in (gain_v, bias_v, qb_v, vb_v))
    kv_bias = jnp.concatenate([jnp.zeros_like(v_bias), v_bias], axis=1)
    for i in range(HEAD_PARTS):
        load(part_at(i)).wait()
        r = chunk_rows(part_at(i), rows)
        unit, _ = norm_parts(tok[r, :].astype(jnp.float32))
        h1[r, :] = (unit * gain + bias).astype(bf)
        if i == 0:
            weights[0].wait()
            weights[1].wait()
        kv[block(me, part_at(i)), :] = (mm(h1[r, :], wkv[...]) + kv_bias).astype(bf)
        if i == 0:
            greeted()
        if i < mine:
            for j in range(groups - 1):
                spread(j, i).start()
    weights[2].wait()
    for i in range(HEAD_PARTS):
        r = chunk_rows(part_at(i), rows)
        q[r, :] = (mm(h1[r, :], wq[...]) + q_bias).astype(bf)
    for i in range(mine):
        for j in range(groups - 1):
            spread(j, i).wait_recv()
            forward(j, i).start()
    for i in range(mine):
        for j in range(groups - 1):
            forward(j, i).wait()
            spread(j, i).wait_send()


def head(tokens, wq, wk, wv, vectors, groups):
    rows, wide = tokens.shape
    bf = jnp.bfloat16
    sds, vm = jax.ShapeDtypeStruct, pltpu.VMEM
    v, a = pl.BlockSpec(memory_space=pltpu.VMEM), pl.BlockSpec(memory_space=pl.ANY)
    dma, two = pltpu.SemaphoreType.DMA, 2 * wk.shape[1]
    pairs = dma((groups - 1, HEAD_PARTS // 2))
    return pl.pallas_call(
        head_kernel,
        out_shape=(sds((rows, wq.shape[1]), bf), sds((groups * rows, two), bf)),
        in_specs=[v] * 4 + [a] * 4,
        out_specs=(v, v),
        scratch_shapes=[
            vm((rows, wide), bf), vm((rows, wide), bf), vm(wq.shape, bf), vm((wide, two), bf),
            dma((HEAD_PARTS,)), dma((3,)), pairs, pairs, pairs, pairs,
        ],
        compiler_params=pltpu.CompilerParams(
            collective_id=1, has_side_effects=True, vmem_limit_bytes=61 * MIB
        ),
        name="head",
    )(*vectors, tokens, wq, wk, wv)


KV_STEP = 3


def tail_kernel(
    chunks,
    gq, dkv, wq, wk, wv, gain_v, bias_v, sums, usum, tok_h, gmix_h,
    tgrad_h, own, vout,
    tok, gmix, h1, pa, out1, snd, mate, in0, in1, tmp, kvm, kvs, kv_in, pkv, okv, ksnd, kin0, kin1, ktmp,
    stage, w_in, acc, v_in,
    load_s, save_s, km_s, km_r, kx_s, kx_r, w_s, w_r, v_s, v_r,
    *sems,
):
    local, wide = tok.shape
    rows = local // chunks
    groups, me = lax.axis_size("cp"), lax.axis_index("cp")
    core = lax.axis_index("tp") % 2
    tp = lax.axis_index("tp")
    per = wide // groups
    heads_wide, size = gq.shape[1], wk.shape[1]
    bf = jnp.bfloat16
    half = len(sems) // 2
    ch1 = Chain(chunks, rows // 4, pa, snd, out1, mate, in0, in1, tmp, sems[:half])
    chk = Chain(1, local // 4, pkv, ksnd, okv, None, kin0, kin1, ktmp, sems[half:])
    loads = [
        pltpu.make_async_copy(src, dst, load_s.at[i])
        for i, (src, dst) in enumerate(((tok_h, tok), (gmix_h, gmix)))
    ]
    for load in loads:
        load.start()
    greet(True, True)()
    own_half = chunk_rows(core, local // 2)
    kv_mate = pltpu.make_async_remote_copy(
        dkv.at[:, chunk_rows(1 - core, local // 2), :], kvm, km_s, km_r,
        device_id={"tp": tp + 1 - 2 * core}, device_id_type=MESH,
    )
    kv_mate.start()
    gain, bias = as_row(gain_v), as_row(bias_v)

    def project(g):
        r = chunk_rows(g, rows)
        pa[r, :] = mm(gq[r, :], wq[...], NT).astype(bf)
        ch1.start_mate(g)

    project(0)
    project(1)
    acc[...] = sums[...]
    kv_mate.wait_recv()

    def kv_copy(i):
        to = lax.rem(me + i + 1, groups)
        return cp_copy(i, kvs.at[to], kv_in.at[i], kx_s, kx_r)

    @pl.loop(0, groups)
    def _(i):
        to = lax.rem(me + i + 1, groups)
        both = dkv[to, own_half, :].astype(jnp.float32) + kvm[to].astype(jnp.float32)
        kvs[to] = both.astype(bf)
        pl.when(i < groups - 1)(lambda: kv_copy(i).start())

    def normed(g):
        r = chunk_rows(g, rows)
        unit, _ = norm_parts(tok[r, :].astype(jnp.float32))
        h1[r, :] = (unit * gain + bias).astype(bf)

    def kv_gather():
        total = kvs[me].astype(jnp.float32)
        for i in range(groups - 1):
            kv_copy(i).wait_recv()
            total += kv_in[i].astype(jnp.float32)
        pkv[own_half, :] = total.astype(bf)

    def serve(ch, s, count, slack):
        for k in range(2):
            g = s - ch.lag_up(k)
            pl.when(within(g, count))(functools.partial(ch.reduce, g, k))
        for k in range(2):
            g = s - ch.lag_down(k) - slack
            pl.when(within(g, count))(functools.partial(ch.down, g, k))

    def w_copy(i):
        return cp_copy(i, stage.at[i], w_in.at[i], w_s, w_r)

    def weights(i):
        cols = pl.ds(pl.multiple_of(lax.rem(me + i + 1, groups) * per, per), per)
        part = mm(h1[:, cols], jnp.concatenate([gq[...], okv[...]], axis=1), TN)

        @pl.when(i < groups - 1)
        def _():
            stage[i] = part.astype(bf)
            w_copy(i).start()

        @pl.when(i == groups - 1)
        def _():
            own[...] = part

    def save(g):
        r = chunk_rows(g, rows)
        return pltpu.make_async_copy(pa.at[r], tgrad_h.at[r], save_s.at[g])

    def finish(g):
        r = chunk_rows(g, rows)
        ch1.done(g)
        ch1.drain(g)
        grad = out1[r, :].astype(jnp.float32) + mm(okv[r, :], jnp.concatenate([wk[...], wv[...]], axis=1), NT)
        unit, inv = norm_parts(tok[r, :].astype(jnp.float32))
        acc[4:5, :] += jnp.sum(grad * unit, axis=0, keepdims=True)
        acc[5:6, :] += jnp.sum(grad, axis=0, keepdims=True)
        pa[r, :] = (gmix[r, :].astype(jnp.float32) + norm_back(grad, unit, inv, gain)).astype(bf)
        save(g).start()

    turn = 2 * ch1.reach + SLACK
    ready = KV_STEP + 2 * ch1.reach

    def finished(s):
        return jnp.clip(jnp.minimum(2 * (s - ready), s - turn + 1), 0, chunks)

    @pl.loop(0, max(chunks + turn, ready + 1 + chunks // 2, ready + 1 + groups))
    def _(s):
        pl.when(s + 2 < chunks)(lambda: project(s + 2))
        pl.when(within(s, chunks))(lambda: ch1.mate_copy(s).wait_recv())
        serve(ch1, s, chunks, SLACK)

        @pl.when(s == 0)
        def _():
            for load in loads:
                load.wait()

        pl.when(s < chunks)(lambda: normed(s))
        pl.when(s == KV_STEP)(kv_gather)
        serve(chk, s - KV_STEP, 1, 0)
        pl.when(s == ready)(lambda: chk.done(0))
        i = s - ready - 1
        pl.when(within(i, groups))(lambda: weights(i))
        pl.loop(finished(s - 1), finished(s))(finish)

    acc[6:7, 0 : usum.shape[1]] = usum[...]
    at = usum.shape[1]
    acc[6:7, at : at + heads_wide] = jnp.sum(gq[...].astype(jnp.float32), axis=0, keepdims=True)
    at += heads_wide
    acc[6:7, at : at + size] = jnp.sum(okv[:, size:].astype(jnp.float32), axis=0, keepdims=True)

    def v_copy(i):
        return cp_copy(i, acc, v_in.at[i], v_s, v_r)

    for i in range(groups - 1):
        v_copy(i).start()
    kv_mate.wait_send()
    chk.drain(0)

    @pl.loop(0, groups - 1)
    def _(i):
        w_copy(i).wait_recv()
        own[...] += w_in[i].astype(jnp.float32)
        w_copy(i).wait_send()
        kv_copy(i).wait_send()

    @pl.loop(0, chunks)
    def _(g):
        save(g).wait()

    total = jnp.zeros_like(acc)
    for i in range(groups - 1):
        v_copy(i).wait_recv()
    for source in range(groups):
        slot = lax.rem(me - source - 1 + groups, groups)
        theirs = v_in[jnp.minimum(slot, groups - 2)]
        total += jnp.where(slot == groups - 1, acc[...], theirs)
    vout[...] = total
    for i in range(groups - 1):
        v_copy(i).wait_send()


def tail(gq, dkv, wq, wk, wv, vectors, sums, usum, tokens, grad_mixed, groups, chunks=8):
    rows, wide = tokens.shape
    heads_wide, two = gq.shape[1], 2 * wk.shape[1]
    bf, f32 = jnp.bfloat16, jnp.float32
    sds, vm = jax.ShapeDtypeStruct, pltpu.VMEM
    v, a = pl.BlockSpec(memory_space=pltpu.VMEM), pl.BlockSpec(memory_space=pl.ANY)
    dma = pltpu.SemaphoreType.DMA
    per, both = wide // groups, heads_wide + two
    return pl.pallas_call(
        functools.partial(tail_kernel, chunks),
        out_shape=(sds((rows, wide), bf), sds((per, both), f32), sds((8, wide), f32)),
        in_specs=[v] * 9 + [a, a],
        out_specs=(a, v, v),
        scratch_shapes=[
            vm((rows, wide), bf),
            vm((rows, wide), bf),
            vm((rows, wide), bf),
            vm((rows, wide), bf),
            vm((rows, wide), bf),
            vm((rows // 2, wide), bf),
            vm((rows // 2, wide), bf),
            vm((rows // 2, wide), bf),
            vm((rows // 4, wide), bf),
            vm((rows // (4 * chunks), wide), f32),
            vm((groups, rows // 2, two), bf),
            vm((groups, rows // 2, two), bf),
            vm((groups - 1, rows // 2, two), bf),
            vm((rows, two), bf),
            vm((rows, two), bf),
            vm((rows // 2, two), bf),
            vm((rows // 2, two), bf),
            vm((rows // 4, two), bf),
            vm((rows // 4, two), f32),
            vm((groups - 1, per, both), bf),
            vm((groups - 1, per, both), bf),
            vm((8, wide), f32),
            vm((groups - 1, 8, wide), f32),
            dma((2,)), dma((chunks,)), dma, dma,
            dma((groups - 1,)), dma((groups - 1,)), dma((groups - 1,)), dma((groups - 1,)),
            dma((groups - 1,)), dma((groups - 1,)),
            *Chain.sems(chunks), *Chain.sems(1),
        ],
        compiler_params=pltpu.CompilerParams(
            collective_id=3, has_side_effects=True, vmem_limit_bytes=61 * MIB
        ),
        name="tail",
    )(gq, dkv, wq, wk, wv, *vectors, sums, usum, tokens, grad_mixed)


def shards(
    tokens,
    cotangent,
    first_gain,
    first_bias,
    query_weight,
    query_bias,
    key_weight,
    value_weight,
    value_bias,
    out_weight,
    out_bias,
    second_gain,
    second_bias,
    up_weight,
    up_bias,
    down_weight,
    down_bias,
    file_lengths,
    pad_mask,
):
    groups = lax.axis_size("cp")
    queries, gathered = head(
        tokens, query_weight, key_weight, value_weight, (first_gain, first_bias, query_bias, value_bias), groups
    )
    attended, attended_low, log_total = attend(queries, gathered, file_lengths, pad_mask)
    block_out, grad_mixed, grad_attended, down_grad, up_grad, out_grad, sums, up_sum = middle(
        attended_low, tokens, cotangent, out_weight, up_weight, down_weight,
        (second_gain, second_bias, out_bias, down_bias, up_bias), groups,
    )
    up_grad = lax.psum_scatter(up_grad, "cp", scatter_dimension=0, tiled=True)
    out_grad = lax.psum_scatter(out_grad, "cp", scatter_dimension=1, tiled=True)
    grad_queries, key_value_parts, block_out, down_grad = attend_back(
        queries, grad_attended, attended, log_total, gathered, file_lengths, pad_mask, block_out, down_grad
    )
    tokens_low, own_grads, sums = tail(
        grad_queries, key_value_parts.reshape(groups, -1, gathered.shape[1]), query_weight,
        key_weight, value_weight, (first_gain, first_bias), sums, up_sum, tokens, grad_mixed, groups,
    )
    (
        tokens_grad, up_grad, out_grad, query_grad, key_grad, value_grad,
        down_bias_grad, second_gain_grad, second_bias_grad, out_bias_grad, first_gain_grad, first_bias_grad,
        up_bias_grad, query_bias_grad, value_bias_grad,
    ) = emit(tokens_low, up_grad, out_grad, own_grads, sums, query_weight.shape[1])
    return (
        block_out,
        tokens_grad,
        first_gain_grad,
        first_bias_grad,
        query_grad,
        query_bias_grad,
        key_grad,
        value_grad,
        value_bias_grad,
        out_grad,
        out_bias_grad,
        second_gain_grad,
        second_bias_grad,
        up_grad,
        up_bias_grad,
        down_grad,
        down_bias_grad,
    )


def solution(mesh):
    placed = (
        P("cp", None),
        P("cp", None),
        P(),
        P(),
        P(None, "tp"),
        P("tp"),
        P(),
        P(),
        P(),
        P("tp", None),
        P(),
        P(),
        P(),
        P(None, "tp"),
        P("tp"),
        P("tp", None),
        P(),
        P(),
        P(),
    )
    return jax.shard_map(
        shards,
        mesh=mesh,
        in_specs=placed,
        out_specs=(
            P("cp", None),
            P("cp", None),
            P(),
            P(),
            P("cp", "tp"),
            P("tp"),
            P("cp", None),
            P("cp", None),
            P(),
            P("tp", "cp"),
            P(),
            P(),
            P(),
            P("cp", "tp"),
            P("tp"),
            P("tp", "cp"),
            P(),
        ),
        check_vma=False,
    )
```

```python
import functools
import math

import jax
import jax.numpy as jnp
from jax import lax
from jax.experimental import pallas as pl
from jax.experimental.pallas import tpu as pltpu
from jax.sharding import PartitionSpec as P

EPSILON = 1e-05
NEGATIVE = -1e30
LOG2E = 1.4426950408889634
LN2 = 0.6931471805599453
NT = (((1,), (1,)), ((), ()))
NN = (((1,), (0,)), ((), ()))
TN = (((0,), (0,)), ((), ()))
MIB = 2**20


def mm(a, b, dims=NN):
    return lax.dot_general(a, b, dims, preferred_element_type=jnp.float32)


def file_start(lengths, pos):
    end, start = 0, jnp.zeros_like(pos)
    for i in range(lengths.shape[0]):
        end = end + lengths[i]
        start = jnp.where(pos >= end, end, start)
    return start


def key_ids(pad, j, keys):
    pos = j * keys + lax.broadcasted_iota(jnp.int32, (1, keys), 1)
    return jnp.where(pad[pl.ds(pl.multiple_of(j * keys, keys), keys)].reshape(1, -1) == 1, pos, -1)


def as_column(row):
    return jnp.transpose(jnp.broadcast_to(row, (128, row.shape[1])))[:, :1]


def attend_kernel(rows, keys, heads, size, len_ref, q_ref, kv_ref, pad_ref, o_ref, low_ref, lse_ref):
    scale2 = LOG2E / math.sqrt(size)
    base = (lax.axis_index("cp") * pl.num_programs(0) + pl.program_id(0)) * rows
    row_pos = base + lax.broadcasted_iota(jnp.int32, (rows, 1), 0)
    row_start = as_column(file_start(len_ref, base + lax.broadcasted_iota(jnp.int32, (1, rows), 1)))
    ones = jnp.ones((keys, size), jnp.bfloat16)

    def block(j, carry, diagonal):
        here = pl.ds(pl.multiple_of(j * keys, keys), keys)
        k = kv_ref[here, :size]
        v1 = jnp.concatenate([kv_ref[here, size:], ones], axis=1)
        kid = key_ids(pad_ref, j, keys)
        ok = kid >= row_start
        if diagonal:
            col = j * keys + lax.broadcasted_iota(jnp.int32, (1, keys), 1)
            ok = (ok & (kid <= row_pos)) | (col == row_pos)
        out = []
        for h in range(heads):
            top, acc = carry[h]
            s = jnp.where(ok, mm(q_ref[:, h * size : (h + 1) * size], k, NT) * scale2, NEGATIVE)
            new = jnp.maximum(top, jnp.max(s, axis=1, keepdims=True))
            w = jnp.exp2(s - new).astype(jnp.bfloat16)
            out.append((new, acc * jnp.exp2(top - new) + mm(w, v1)))
        return tuple(out)

    carry = tuple(
        (jnp.full((rows, 1), NEGATIVE, jnp.float32), jnp.zeros((rows, 2 * size), jnp.float32))
        for _ in range(heads)
    )
    full = base // keys
    carry = lax.fori_loop(file_start(len_ref, base) // keys, full, lambda j, c: block(j, c, False), carry)
    last = (base + rows + keys - 1) // keys
    carry = lax.fori_loop(full, last, lambda j, c: block(j, c, True), carry)
    for h in range(heads):
        top, acc = carry[h]
        total = acc[:, size:]
        out = acc[:, :size] / total
        o_ref[:, h * size : (h + 1) * size] = out
        low_ref[:, h * size : (h + 1) * size] = out.astype(jnp.bfloat16)
        lse_ref[h : h + 1, :] = jnp.transpose(top + jnp.log2(total))[0:1]


def attend(q, kv, lengths, pad, rows=512, keys=512):
    total, wide = q.shape
    size = kv.shape[1] // 2
    heads = wide // size
    by_row = pl.BlockSpec((rows, wide), lambda i, f: (i, 0))
    return pl.pallas_call(
        functools.partial(attend_kernel, rows, keys, heads, size),
        out_shape=(
            jax.ShapeDtypeStruct((total, wide), jnp.float32),
            jax.ShapeDtypeStruct((total, wide), jnp.bfloat16),
            jax.ShapeDtypeStruct((heads, total), jnp.float32),
        ),
        grid_spec=pltpu.PrefetchScalarGridSpec(
            num_scalar_prefetch=1,
            grid=(total // rows,),
            in_specs=[
                by_row,
                pl.BlockSpec(kv.shape, lambda i, f: (0, 0)),
                pl.BlockSpec(pad.shape, lambda i, f: (0,)),
            ],
            out_specs=[by_row, by_row, pl.BlockSpec((heads, rows), lambda i, f: (0, i))],
        ),
        compiler_params=pltpu.CompilerParams(vmem_limit_bytes=61 * MIB),
        name="attend",
    )(lengths, q, kv, pad)


def attend_back_kernel(
    rows, keys, heads, size, len_ref, q_ref, do_ref, o_ref, lse_ref, kv_ref, pad_ref, block_h, down_h, in_h,
    dq_ref, dkv_ref, block_o, down_o, acc_ref, block_v, down_v, in_v, pass_s,
):
    i = pl.program_id(0)
    scale = 1.0 / math.sqrt(size)
    base = (lax.axis_index("cp") * pl.num_programs(0) + i) * rows
    row_pos = base + lax.broadcasted_iota(jnp.int32, (1, rows), 1)
    row_start = file_start(len_ref, row_pos)
    fetched = [
        pltpu.make_async_copy(src, dst, pass_s.at[k])
        for k, (src, dst) in enumerate(((block_h, block_v), (down_h, down_v), (in_h, in_v)))
    ]
    passed = [
        pltpu.make_async_copy(block_v, block_o, pass_s.at[3]),
        pltpu.make_async_copy(down_v, down_o, pass_s.at[4]),
    ]

    @pl.when(i == 0)
    def _():
        for copy in fetched:
            copy.start()
        acc_ref[...] = jnp.zeros_like(acc_ref)

    @pl.when(i == pl.num_programs(0) - 1)
    def _():
        for copy in fetched:
            copy.wait()
        passed[0].start()

        @pl.loop(0, 8)
        def _(j):
            r = chunk_rows(j, down_v.shape[0] // 8)
            total = down_v[r, :]
            for k in range(in_v.shape[0]):
                total += in_v[k, r, :].astype(jnp.float32)
            down_v[r, :] = total

        passed[1].start()

    deltas = []
    for h in range(heads):
        cols = slice(h * size, (h + 1) * size)
        both = do_ref[:, cols].astype(jnp.float32) * o_ref[:, cols]
        deltas.append(jnp.sum(jnp.transpose(both), axis=0, keepdims=True))

    def block(j, carry, diagonal):
        here = pl.ds(pl.multiple_of(j * keys, keys), keys)
        k = kv_ref[here, :size]
        v = kv_ref[here, size:]
        kid = as_column(key_ids(pad_ref, j, keys))
        ok = kid >= row_start
        if diagonal:
            col = j * keys + lax.broadcasted_iota(jnp.int32, (keys, 1), 0)
            ok = (ok & (kid <= row_pos)) | (col == row_pos)
        out = []
        dk = acc_ref[here, :size]
        dv = acc_ref[here, size:]
        for h in range(heads):
            cols = slice(h * size, (h + 1) * size)
            q = q_ref[:, cols]
            do = do_ref[:, cols]
            s = mm(k, q, NT) * (scale * LOG2E) - lse_ref[h : h + 1, :]
            p = jnp.where(ok, jnp.exp2(s), 0.0)
            ds = (p * (mm(v, do, NT) - deltas[h])).astype(jnp.bfloat16)
            dv = dv + mm(p.astype(jnp.bfloat16), do)
            dk = dk + mm(ds, q)
            out.append(carry[h] + mm(ds, k, TN))
        acc_ref[here, :size] = dk
        acc_ref[here, size:] = dv
        return tuple(out)

    carry = tuple(jnp.zeros((rows, size), jnp.float32) for _ in range(heads))
    full = base // keys
    carry = lax.fori_loop(file_start(len_ref, base) // keys, full, lambda j, c: block(j, c, False), carry)
    last = (base + rows + keys - 1) // keys
    carry = lax.fori_loop(full, last, lambda j, c: block(j, c, True), carry)
    for h in range(heads):
        dq_ref[:, h * size : (h + 1) * size] = (carry[h] * scale).astype(dq_ref.dtype)

    @pl.when(i == pl.num_programs(0) - 1)
    def _():
        dkv_ref[:, :size] = (acc_ref[:, :size] * scale).astype(dkv_ref.dtype)
        dkv_ref[:, size:] = acc_ref[:, size:].astype(dkv_ref.dtype)
        for copy in passed:
            copy.wait()


def attend_back(q, do, o, lse, kv, lengths, pad, block, down, down_in, rows=512, keys=512):
    total, wide = q.shape
    size = kv.shape[1] // 2
    heads = wide // size
    by_row = pl.BlockSpec((rows, wide), lambda i, f: (i, 0))
    whole = pl.BlockSpec(kv.shape, lambda i, f: (0, 0))
    far = pl.BlockSpec(memory_space=pl.ANY)
    return pl.pallas_call(
        functools.partial(attend_back_kernel, rows, keys, heads, size),
        out_shape=(
            jax.ShapeDtypeStruct((total, wide), jnp.bfloat16),
            jax.ShapeDtypeStruct(kv.shape, jnp.bfloat16),
            jax.ShapeDtypeStruct(block.shape, block.dtype),
            jax.ShapeDtypeStruct(down.shape, down.dtype),
        ),
        grid_spec=pltpu.PrefetchScalarGridSpec(
            num_scalar_prefetch=1,
            grid=(total // rows,),
            in_specs=[
                by_row,
                by_row,
                by_row,
                pl.BlockSpec((heads, rows), lambda i, f: (0, i)),
                whole,
                pl.BlockSpec(pad.shape, lambda i, f: (0,)),
                far,
                far,
                far,
            ],
            out_specs=[by_row, whole, far, far],
            scratch_shapes=[
                pltpu.VMEM(kv.shape, jnp.float32),
                pltpu.VMEM(block.shape, block.dtype),
                pltpu.VMEM(down.shape, down.dtype),
                pltpu.VMEM(down_in.shape, down_in.dtype),
                pltpu.SemaphoreType.DMA((5,)),
            ],
        ),
        compiler_params=pltpu.CompilerParams(vmem_limit_bytes=61 * MIB),
        name="attend_back",
    )(lengths, q, do, o, lse, kv, pad, block, down, down_in)


def emit_kernel(
    heads_wide, low, own, up, out, out_in, sums, tokens_o, q_o, k_o, v_o, up_o, out_o, *vectors
):
    up_o[...] = up[...].astype(jnp.float32)
    tokens_o[...] = low[...].astype(jnp.float32)
    size = k_o.shape[1]
    q_o[...] = own[:, :heads_wide]
    k_o[...] = own[:, heads_wide : heads_wide + size]
    v_o[...] = own[:, heads_wide + size :]
    total = out[...]
    for i in range(out_in.shape[0]):
        total += out_in[i].astype(jnp.float32)
    out_o[...] = total

    @pl.when(pl.program_id(0) == 0)
    def _():
        for i in range(6):
            vectors[i][...] = sums[i : i + 1, :].reshape(-1)
        at = 0
        for ref in vectors[6:]:
            ref[...] = sums[6:7, at : at + ref.shape[0]].reshape(-1)
            at += ref.shape[0]


def emit(low, own, up, out, out_in, sums, heads_wide, steps=4):
    size = (own.shape[1] - heads_wide) // 2
    wide, hidden = low.shape[1], up.shape[1]
    f32 = jnp.float32

    def rows_of(shape):
        if len(shape) == 3:
            return pl.BlockSpec((shape[0], shape[1] // steps, shape[2]), lambda i: (0, i, 0))
        return pl.BlockSpec((shape[0] // steps, shape[1]), lambda i: (i, 0))

    lengths = (wide,) * 6 + (hidden, heads_wide, size)
    per = own.shape[0]
    shapes = (low.shape, (per, heads_wide), (per, size), (per, size), up.shape, out.shape)
    blocks = (low, own, up, out, out_in)
    return pl.pallas_call(
        functools.partial(emit_kernel, heads_wide),
        out_shape=tuple(jax.ShapeDtypeStruct(x, f32) for x in (*shapes, *((n,) for n in lengths))),
        grid=(steps,),
        in_specs=[*(rows_of(x.shape) for x in blocks), pl.BlockSpec(sums.shape, lambda i: (0, 0))],
        out_specs=(*(rows_of(x) for x in shapes), *(pl.BlockSpec((n,), lambda i: (0,)) for n in lengths)),
        compiler_params=pltpu.CompilerParams(vmem_limit_bytes=61 * MIB),
        name="emit",
    )(*blocks, sums)


def as_row(ref):
    return ref[...].astype(jnp.float32).reshape(1, -1)


MESH = pl.DeviceIdType.MESH


class Chain:
    def __init__(self, chunks, quarter, part, out, mate, in0, in1, tmp, sems, hop=1):
        tp = lax.axis_index("tp")
        self.n = lax.axis_size("tp") // 2
        self.p, self.c = tp // 2, tp % 2
        self.chunks, self.q = chunks, quarter
        self.part, self.out, self.mate, self.in0, self.in1, self.tmp = part, out, mate, in0, in1, tmp
        (self.mate_s, self.mate_r, self.ch_s, self.in0_r, self.in1_r, self.bl_s, self.br_s, self.bc_r, self.fin_s, self.fin_r) = sems
        self.roots = (self.n // 2 - 1, self.n // 2)
        self.hop = hop
        self.reach = hop * max(self.roots[0], self.n - 1 - self.roots[0])

    @staticmethod
    def sems(chunks):
        one, two = pltpu.SemaphoreType.DMA((chunks,)), pltpu.SemaphoreType.DMA((chunks, 2))
        return [one, one, two, two, one, two, two, two, two, two]

    def at(self, p, c):
        return {"tp": p * 2 + c}

    def rows(self, g, c, part):
        q = self.q
        return pl.ds(pl.multiple_of(g * (4 * q) + c * (2 * q) + part * q, q), q)

    def own(self, g, part):
        q = self.q
        return pl.ds(pl.multiple_of(g * (2 * q) + part * q, q), q)

    def copy(self, src, dst, s, r, p, c):
        return pltpu.make_async_remote_copy(src, dst, s, r, device_id=self.at(p, c), device_id_type=MESH)

    def mate_copy(self, g):
        q = self.q
        src = self.part.at[pl.ds(pl.multiple_of(g * (4 * q) + (1 - self.c) * (2 * q), 2 * q), 2 * q)]
        dst = self.mate.at[pl.ds(pl.multiple_of(g * (2 * q), 2 * q), 2 * q)]
        return self.copy(src, dst, self.mate_s.at[g], self.mate_r.at[g], self.p, 1 - self.c)

    def in_copy(self, g, k, to):
        return self.copy(self.part.at[self.rows(g, self.c, k)], self.in0.at[self.own(g, k)], self.ch_s.at[g, k], self.in0_r.at[g, k], to, self.c)

    def in1_copy(self, g, k, to):
        q = self.q
        dst = self.in1.at[pl.ds(pl.multiple_of(g * q, q), q)]
        return self.copy(self.part.at[self.rows(g, self.c, k)], dst, self.ch_s.at[g, k], self.in1_r.at[g], to, self.c)

    def out_copy(self, g, k, to, sem):
        here = self.out.at[self.rows(g, self.c, k)]
        return self.copy(here, here, sem.at[g, k], self.bc_r.at[g, k], to, self.c)

    def fin_copy(self, g, k):
        here = self.out.at[self.rows(g, self.c, k)]
        return self.copy(here, here, self.fin_s.at[g, k], self.fin_r.at[g, k], self.p, 1 - self.c)

    def lag_up(self, k):
        root = self.roots[k]
        return jnp.where(
            self.p == root, self.reach, self.hop * jnp.where(self.p < root, self.p, self.n - 1 - self.p)
        )

    def lag_down(self, k):
        return self.reach + self.hop * jnp.abs(self.p - self.roots[k])

    def start_mate(self, g):
        self.mate_copy(g).start()

    def reduce(self, g, k):
        root, p, n, q = self.roots[k], self.p, self.n, self.q
        rows, own, tmp = self.rows(g, self.c, k), self.own(g, k), self.tmp
        if self.mate is None:
            tmp[...] = self.part[rows, :].astype(jnp.float32)
        else:
            tmp[...] = self.part[rows, :].astype(jnp.float32) + self.mate[own, :].astype(jnp.float32)

        @pl.when(((p > 0) & (p <= root)) | ((p > root) & (p < n - 1)))
        def _():
            self.in_copy(g, k, p).wait_recv()
            tmp[...] += self.in0[own, :].astype(jnp.float32)

        @pl.when((p == root) & (p < n - 1))
        def _():
            self.in1_copy(g, k, p).wait_recv()
            tmp[...] += self.in1[pl.ds(pl.multiple_of(g * q, q), q), :].astype(jnp.float32)

        @pl.when(p != root)
        def _():
            self.part[rows, :] = tmp[...].astype(jnp.bfloat16)

        @pl.when(p < root)
        def _():
            self.in_copy(g, k, p + 1).start()

        @pl.when(p > root + 1)
        def _():
            self.in_copy(g, k, p - 1).start()

        @pl.when(p == root + 1)
        def _():
            self.in1_copy(g, k, p - 1).start()

        @pl.when(p == root)
        def _():
            self.out[rows, :] = tmp[...].astype(jnp.bfloat16)
            self.spread(g, k)

    def spread(self, g, k):
        root, p, n = self.roots[k], self.p, self.n

        @pl.when((p <= root) & (p > 0))
        def _():
            self.out_copy(g, k, p - 1, self.bl_s).start()

        @pl.when((p >= root) & (p < n - 1))
        def _():
            self.out_copy(g, k, p + 1, self.br_s).start()

        self.fin_copy(g, k).start()

    def down(self, g, k):
        @pl.when(self.p != self.roots[k])
        def _():
            self.out_copy(g, k, self.p, self.bl_s).wait_recv()
            self.spread(g, k)

    def done(self, g):
        for k in range(2):
            self.fin_copy(g, k).wait_recv()

    def drain(self, g):
        p, n = self.p, self.n
        if self.mate is not None:
            self.mate_copy(g).wait_send()
        for k, root in enumerate(self.roots):

            @pl.when(p != root)
            def _():
                self.in_copy(g, k, p).wait_send()

            @pl.when((p <= root) & (p > 0))
            def _():
                self.out_copy(g, k, p, self.bl_s).wait_send()

            @pl.when((p >= root) & (p < n - 1))
            def _():
                self.out_copy(g, k, p, self.br_s).wait_send()

            self.fin_copy(g, k).wait_send()


def within(g, chunks):
    return (g >= 0) & (g < chunks)


def chunk_rows(g, rows):
    return pl.ds(pl.multiple_of(g * rows, rows), rows)


def norm_parts(values):
    centre = jnp.mean(values, axis=1, keepdims=True)
    centred = values - centre
    inv = lax.rsqrt(jnp.mean(centred * centred, axis=1, keepdims=True) + EPSILON)
    return centred * inv, inv


def norm_back(grad, unit, inv, gain):
    e = grad * gain
    return inv * (
        e - jnp.mean(e, axis=1, keepdims=True) - unit * jnp.mean(e * unit, axis=1, keepdims=True)
    )


def greet(chips, peers):
    tp, me = lax.axis_index("tp"), lax.axis_index("cp")
    n, groups = lax.axis_size("tp") // 2, lax.axis_size("cp")
    p, c = tp // 2, tp % 2
    bar = pltpu.get_barrier_semaphore()
    count = 1
    pl.semaphore_signal(bar, 1, device_id={"tp": p * 2 + 1 - c}, device_id_type=MESH)
    if chips:

        @pl.when(p > 0)
        def _():
            pl.semaphore_signal(bar, 1, device_id={"tp": tp - 2}, device_id_type=MESH)

        @pl.when(p < n - 1)
        def _():
            pl.semaphore_signal(bar, 1, device_id={"tp": tp + 2}, device_id_type=MESH)

        count += (p > 0).astype(jnp.int32) + (p < n - 1).astype(jnp.int32)
    if peers:
        for i in range(1, groups):
            pl.semaphore_signal(bar, 1, device_id={"cp": lax.rem(me + i, groups)}, device_id_type=MESH)
        count += groups - 1
    return lambda: pl.semaphore_wait(bar, count)


def cp_copy(i, src, dst, send, recv):
    to = lax.rem(lax.axis_index("cp") + i + 1, lax.axis_size("cp"))
    return pltpu.make_async_remote_copy(
        src, dst, send.at[i], recv.at[i], device_id={"cp": to}, device_id_type=MESH
    )


SLACK = 0
HOP = 1


def middle_kernel(
    chunks,
    attn, wo, gain_v, bias_v, ob_v, db_v, ub_v, tok_h, cot_h, wu_h, wd_h,
    out_h, gmix_h, gattn, down_own, down_in, up_h, outw_h, out_own, sums, usum,
    tok, cot, wu, wd, hid, h2, gup, pa, pc, pb, out1, out2, out3, mate, in0, in1, tmp,
    load_s, save_s, gm_s, up_s, ow_s, dn_s, dn_r,
    *sems,
):
    rows = tok.shape[0] // chunks
    groups, me = lax.axis_size("cp"), lax.axis_index("cp")
    wide = tok.shape[1]
    per = wide // groups
    bf = jnp.bfloat16
    third = len(sems) // 3
    ch1 = Chain(chunks, rows // 4, pa, out1, mate, in0, in1, tmp, sems[:third], HOP)
    ch3 = Chain(chunks, rows // 4, pc, out3, mate, in0, in1, tmp, sems[third : 2 * third], HOP)
    ch2 = Chain(chunks, rows // 4, pb, out2, mate, in0, in1, tmp, sems[2 * third :], HOP)
    first = (lax.axis_index("tp") == 0).astype(jnp.float32)
    loads = [
        pltpu.make_async_copy(src, dst, load_s.at[i])
        for i, (src, dst) in enumerate(((tok_h, tok), (wu_h, wu), (wd_h, wd), (cot_h, cot)))
    ]
    for load in loads:
        load.start()
    greet(True, True)()
    gain, bias, out_bias, down_bias, up_bias = (as_row(x) for x in (gain_v, bias_v, ob_v, db_v, ub_v))
    sums[...] = jnp.zeros_like(sums)
    usum[...] = jnp.zeros_like(usum)

    def project(g):
        r = chunk_rows(g, rows)
        pa[r, :] = mm(attn[r, :], wo[...]).astype(bf)
        ch1.start_mate(g)

    def halves(g):
        return [chunk_rows(2 * g + i, rows // 2) for i in range(2)]

    def middle_of(r):
        return tok[r, :].astype(jnp.float32) + out1[r, :].astype(jnp.float32) + out_bias

    def feed(g):
        r = chunk_rows(g, rows)
        ch1.done(g)
        for part in halves(g):
            unit, _ = norm_parts(middle_of(part))
            h2[part, :] = (unit * gain + bias).astype(bf)
        up = mm(h2[r, :], wu[...]) + up_bias
        sq = up * up
        t = jnp.tanh(0.7978845608028654 * up * (1.0 + 0.044715 * sq))
        half = 0.5 * (1.0 + t)
        hid[r, :] = (half * up).astype(bf)
        slope = half + 0.5 * up * (1.0 - t * t) * (0.7978845608028654 * (1.0 + 3.0 * 0.044715 * sq))
        gu = (slope * mm(cot[r, :], wd[...], NT)).astype(bf)
        gup[r, :] = gu
        usum[...] += jnp.sum(gu.astype(jnp.float32), axis=0, keepdims=True)
        sums[0:1, :] += jnp.sum(cot[r, :].astype(jnp.float32), axis=0, keepdims=True)
        pc[r, :] = mm(gup[r, :], wu[...], NT).astype(bf)
        ch3.start_mate(g)
        for part in halves(g):
            base = first * (middle_of(part) + down_bias)
            pb[part, :] = (mm(hid[part, :], wd[...]) + base).astype(bf)

    def back(g):
        r = chunk_rows(g, rows)
        ch3.done(g)
        ch1.drain(g)
        for part in halves(g):
            unit, inv = norm_parts(middle_of(part))
            grad = out3[part, :].astype(jnp.float32)
            sums[1:2, :] += jnp.sum(grad * unit, axis=0, keepdims=True)
            sums[2:3, :] += jnp.sum(grad, axis=0, keepdims=True)
            gm = (cot[part, :].astype(jnp.float32) + norm_back(grad, unit, inv, gain)).astype(bf)
            sums[3:4, :] += jnp.sum(gm.astype(jnp.float32), axis=0, keepdims=True)
            pa[part, :] = gm
        pltpu.make_async_copy(pa.at[r], gmix_h.at[r], gm_s.at[g]).start()
        gattn[r, :] = mm(pa[r, :], wo[...], NT).astype(bf)
        ch2.start_mate(g)

    def finish(g):
        r = chunk_rows(g, rows)
        ch2.done(g)
        pltpu.make_async_copy(out2.at[r], out_h.at[r], save_s.at[g]).start()

    def down_copy(i):
        to = lax.rem(me + i + 1, groups)
        cols = pl.ds(pl.multiple_of(to * per, per), per)
        return cp_copy(i, wd.at[:, cols], down_in.at[i], dn_s, dn_r)

    def down_block(i):
        cols = pl.ds(pl.multiple_of(lax.rem(me + i + 1, groups) * per, per), per)
        half = hid.shape[1] // 2
        for j in range(2):
            part = mm(hid[:, j * half : (j + 1) * half], cot[:, cols], TN)

            @pl.when(i < groups - 1)
            def _():
                wd[j * half : (j + 1) * half, cols] = part.astype(bf)

            @pl.when(i == groups - 1)
            def _():
                down_own[j * half : (j + 1) * half, :] = part

        pl.when(i < groups - 1)(lambda: down_copy(i).start())

    up_rows = wide // 4

    def up_copy(j):
        r = chunk_rows(j, up_rows)
        return pltpu.make_async_copy(wu.at[r], up_h.at[r], up_s.at[j])

    def up_block(j):
        for k in range(2):
            r = chunk_rows(2 * j + k, up_rows // 2)
            wu[r, :] = mm(h2[:, r], gup[...], TN).astype(bf)
        up_copy(j).start()

    def serve(ch, s):
        for k in range(2):
            g = s - ch.lag_up(k)
            pl.when(within(g, chunks))(functools.partial(ch.reduce, g, k))
        for k in range(2):
            g = s - ch.lag_down(k) - SLACK
            pl.when(within(g, chunks))(functools.partial(ch.down, g, k))

    def due(ch, s):
        pl.when(within(s, chunks))(lambda: ch.mate_copy(s).wait_recv())

    turn = 2 * ch1.reach + SLACK
    project(0)
    project(1)

    @pl.loop(0, chunks + max(3 * turn, turn + groups + 4))
    def _(s):
        pl.when(s + 2 < chunks)(lambda: project(s + 2))
        due(ch1, s)
        serve(ch1, s)

        @pl.when(s == turn)
        def _():
            for load in loads:
                load.wait()

        g = s - turn
        pl.when(within(g, chunks))(functools.partial(feed, g))
        due(ch3, g)
        serve(ch3, g)
        g = s - 2 * turn
        pl.when(within(g, chunks))(functools.partial(back, g))
        i = s - turn - chunks
        pl.when(within(i, groups))(functools.partial(down_block, i))
        due(ch2, g)
        serve(ch2, g)
        j = i - groups
        pl.when(within(j, 4))(functools.partial(up_block, j))
        g = s - 3 * turn
        pl.when(within(g, chunks))(functools.partial(finish, g))

    for j in range(4):
        cols = slice(j * (wide // 4), (j + 1) * (wide // 4))
        mate[0 : attn.shape[1], cols] = mm(attn[...], pa[:, cols], TN).astype(bf)
    out_save = pltpu.make_async_copy(mate.at[pl.ds(0, attn.shape[1])], outw_h, ow_s)
    out_save.start()
    out_own[...] = mate[0 : attn.shape[1], pl.ds(pl.multiple_of(me * per, per), per)].astype(jnp.float32)

    @pl.loop(0, groups - 1)
    def _(i):
        down_copy(i).wait()

    @pl.loop(0, chunks)
    def _(g):
        r = chunk_rows(g, rows)
        pltpu.make_async_copy(pa.at[r], gmix_h.at[r], gm_s.at[g]).wait()
        pltpu.make_async_copy(out2.at[r], out_h.at[r], save_s.at[g]).wait()
        ch3.drain(g)
        ch2.drain(g)

    for j in range(4):
        up_copy(j).wait()
    out_save.wait()


def middle(attn, tokens, cotangent, wo, wu, wd, vectors, groups, chunks=8):
    rows, wide = tokens.shape
    heads_wide, hidden = wo.shape[0], wu.shape[1]
    bf, f32 = jnp.bfloat16, jnp.float32
    sds, vm = jax.ShapeDtypeStruct, pltpu.VMEM
    v, a = pl.BlockSpec(memory_space=pltpu.VMEM), pl.BlockSpec(memory_space=pl.ANY)
    dma = pltpu.SemaphoreType.DMA
    return pl.pallas_call(
        functools.partial(middle_kernel, chunks),
        out_shape=(
            sds((rows, wide), bf),
            sds((rows, wide), bf),
            sds((rows, heads_wide), bf),
            sds((hidden, wide // groups), f32),
            sds((groups - 1, hidden, wide // groups), bf),
            sds((wide, hidden), bf),
            sds((heads_wide, wide), bf),
            sds((heads_wide, wide // groups), f32),
            sds((8, wide), f32),
            sds((1, hidden), f32),
        ),
        in_specs=[v] * 7 + [a] * 4,
        out_specs=(a, a, v, v, a, a, a, v, v, v),
        scratch_shapes=[
            vm((rows, wide), bf), vm((rows, wide), bf), vm((wide, hidden), bf), vm((hidden, wide), bf),
            vm((rows, hidden), bf), vm((rows, wide), bf), vm((rows, hidden), bf),
            *[vm((rows, wide), bf)] * 6,
            vm((rows // 2, wide), bf), vm((rows // 2, wide), bf), vm((rows // 4, wide), bf),
            vm((rows // (4 * chunks), wide), f32),
            dma((4,)), dma((chunks,)), dma((chunks,)), dma((4,)), dma, dma((groups - 1,)), dma((groups - 1,)),
            *Chain.sems(chunks), *Chain.sems(chunks), *Chain.sems(chunks),
        ],
        compiler_params=pltpu.CompilerParams(
            collective_id=2, has_side_effects=True, vmem_limit_bytes=61 * MIB
        ),
        name="middle",
    )(attn, wo, *vectors, tokens, cotangent, wu, wd)


HEAD_PARTS = 4


def head_kernel(
    gain_v, bias_v, qb_v, vb_v, tok_h, wq_h, wk_h, wv_h, q, kv, tok, h1, wq, wkv, load_s, w_s, x_s, x_r, f_s, f_r
):
    local = tok.shape[0]
    rows = local // HEAD_PARTS
    mine = HEAD_PARTS // 2
    groups, me = lax.axis_size("cp"), lax.axis_index("cp")
    tp = lax.axis_index("tp")
    core = tp % 2
    bf = jnp.bfloat16

    def load(part):
        r = chunk_rows(part, rows)
        return pltpu.make_async_copy(tok_h.at[r], tok.at[r], load_s.at[part])

    def part_at(i):
        return lax.rem(mine * core + i, HEAD_PARTS)

    def block(source, part):
        return pl.ds(pl.multiple_of(source * local + part * rows, rows), rows)

    def spread(j, i):
        here = kv.at[block(me, part_at(i))]
        to = lax.rem(me + j + 1, groups)
        return pltpu.make_async_remote_copy(
            here, here, x_s.at[j, i], x_r.at[j, i], device_id={"cp": to}, device_id_type=MESH
        )

    def forward(j, i):
        here = kv.at[block(lax.rem(me - j - 1 + groups, groups), part_at(i))]
        return pltpu.make_async_remote_copy(
            here, here, f_s.at[j, i], f_r.at[j, i], device_id={"tp": tp + 1 - 2 * core}, device_id_type=MESH
        )

    size = wk_h.shape[1]
    weights = [
        pltpu.make_async_copy(wk_h, wkv.at[:, pl.ds(0, size)], w_s.at[0]),
        pltpu.make_async_copy(wv_h, wkv.at[:, pl.ds(size, size)], w_s.at[1]),
        pltpu.make_async_copy(wq_h, wq, w_s.at[2]),
    ]
    load(part_at(0)).start()
    weights[0].start()
    weights[1].start()
    for i in range(1, HEAD_PARTS):
        load(part_at(i)).start()
    weights[2].start()
    greeted = greet(False, True)
    gain, bias, q_bias, v_bias = (as_row(x) for x in (gain_v, bias_v, qb_v, vb_v))
    kv_bias = jnp.concatenate([jnp.zeros_like(v_bias), v_bias], axis=1)
    for i in range(HEAD_PARTS):
        load(part_at(i)).wait()
        r = chunk_rows(part_at(i), rows)
        unit, _ = norm_parts(tok[r, :].astype(jnp.float32))
        h1[r, :] = (unit * gain + bias).astype(bf)
        if i == 0:
            weights[0].wait()
            weights[1].wait()
        kv[block(me, part_at(i)), :] = (mm(h1[r, :], wkv[...]) + kv_bias).astype(bf)
        if i == 0:
            greeted()
        if i < mine:
            for j in range(groups - 1):
                spread(j, i).start()
    weights[2].wait()
    for i in range(HEAD_PARTS):
        r = chunk_rows(part_at(i), rows)
        q[r, :] = (mm(h1[r, :], wq[...]) + q_bias).astype(bf)
    for i in range(mine):
        for j in range(groups - 1):
            spread(j, i).wait_recv()
            forward(j, i).start()
    for i in range(mine):
        for j in range(groups - 1):
            forward(j, i).wait()
            spread(j, i).wait_send()


def head(tokens, wq, wk, wv, vectors, groups):
    rows, wide = tokens.shape
    bf = jnp.bfloat16
    sds, vm = jax.ShapeDtypeStruct, pltpu.VMEM
    v, a = pl.BlockSpec(memory_space=pltpu.VMEM), pl.BlockSpec(memory_space=pl.ANY)
    dma, two = pltpu.SemaphoreType.DMA, 2 * wk.shape[1]
    pairs = dma((groups - 1, HEAD_PARTS // 2))
    return pl.pallas_call(
        head_kernel,
        out_shape=(sds((rows, wq.shape[1]), bf), sds((groups * rows, two), bf)),
        in_specs=[v] * 4 + [a] * 4,
        out_specs=(v, v),
        scratch_shapes=[
            vm((rows, wide), bf), vm((rows, wide), bf), vm(wq.shape, bf), vm((wide, two), bf),
            dma((HEAD_PARTS,)), dma((3,)), pairs, pairs, pairs, pairs,
        ],
        compiler_params=pltpu.CompilerParams(
            collective_id=1, has_side_effects=True, vmem_limit_bytes=61 * MIB
        ),
        name="head",
    )(*vectors, tokens, wq, wk, wv)


KV_STEP = 2
TAIL_HOP = 1


def tail_kernel(
    chunks,
    gq, dkv, wq, wk, wv, gain_v, bias_v, sums, usum, tok_h, gmix_h, outw_h,
    tgrad_h, out_in, own, vout,
    tok, gmix, h1, pa, out1, mate, in0, in1, tmp, kvm, kvs, kv_in, pkv, okv, kin0, kin1, ktmp,
    stage, w_in, acc, v_in,
    load_s, save_s, o_s, o_r, km_s, km_r, kx_s, kx_r, w_s, w_r, v_s, v_r,
    *sems,
):
    local, wide = tok.shape
    rows = local // chunks
    groups, me = lax.axis_size("cp"), lax.axis_index("cp")
    core = lax.axis_index("tp") % 2
    tp = lax.axis_index("tp")
    per = wide // groups
    heads_wide, size = gq.shape[1], wk.shape[1]
    bf = jnp.bfloat16
    half_sems = len(sems) // 2
    ch1 = Chain(chunks, rows // 4, pa, out1, mate, in0, in1, tmp, sems[:half_sems], TAIL_HOP)
    chk = Chain(1, local // 4, pkv, okv, None, kin0, kin1, ktmp, sems[half_sems:])
    loads = [
        pltpu.make_async_copy(src, dst, load_s.at[i])
        for i, (src, dst) in enumerate(((tok_h, tok), (gmix_h, gmix)))
    ]
    for load in loads:
        load.start()
    greet(True, True)()
    own_half = chunk_rows(core, local // 2)
    kv_mate = pltpu.make_async_remote_copy(
        dkv.at[:, chunk_rows(1 - core, local // 2), :], kvm, km_s, km_r,
        device_id={"tp": tp + 1 - 2 * core}, device_id_type=MESH,
    )
    kv_mate.start()
    gain, bias = as_row(gain_v), as_row(bias_v)

    def project(g):
        r = chunk_rows(g, rows)
        pa[r, :] = mm(gq[r, :], wq[...], NT).astype(bf)
        ch1.start_mate(g)

    project(0)
    project(1)
    acc[...] = sums[...]

    def kv_copy(i):
        to = lax.rem(me + i + 1, groups)
        return cp_copy(i, kvs.at[to], kv_in.at[i], kx_s, kx_r)

    def kv_send():
        kv_mate.wait_recv()

        @pl.loop(0, groups)
        def _(i):
            to = lax.rem(me + i + 1, groups)
            both = dkv[to, own_half, :].astype(jnp.float32) + kvm[to].astype(jnp.float32)
            kvs[to] = both.astype(bf)
            pl.when(i < groups - 1)(lambda: kv_copy(i).start())

        for i in range(groups - 1):
            out_copy(i).start()

    def normed(g):
        r = chunk_rows(g, rows)
        unit, _ = norm_parts(tok[r, :].astype(jnp.float32))
        h1[r, :] = (unit * gain + bias).astype(bf)

    def kv_gather():
        total = kvs[me].astype(jnp.float32)
        for i in range(groups - 1):
            kv_copy(i).wait_recv()
            total += kv_in[i].astype(jnp.float32)
        pkv[own_half, :] = total.astype(bf)

    def serve(ch, s, count, slack):
        for k in range(2):
            g = s - ch.lag_up(k)
            pl.when(within(g, count))(functools.partial(ch.reduce, g, k))
        for k in range(2):
            g = s - ch.lag_down(k) - slack
            pl.when(within(g, count))(functools.partial(ch.down, g, k))

    def w_copy(i):
        return cp_copy(i, stage.at[i], w_in.at[i], w_s, w_r)

    def weights(i):
        cols = pl.ds(pl.multiple_of(lax.rem(me + i + 1, groups) * per, per), per)
        part = mm(h1[:, cols], jnp.concatenate([gq[...], okv[...]], axis=1), TN)

        @pl.when(i < groups - 1)
        def _():
            stage[i] = part.astype(bf)
            w_copy(i).start()

        @pl.when(i == groups - 1)
        def _():
            own[...] = part

    def save(g):
        r = chunk_rows(g, rows)
        return pltpu.make_async_copy(gmix.at[r], tgrad_h.at[r], save_s.at[g])

    def finish(g):
        r = chunk_rows(g, rows)
        ch1.done(g)
        grad = out1[r, :].astype(jnp.float32) + mm(okv[r, :], jnp.concatenate([wk[...], wv[...]], axis=1), NT)
        unit, inv = norm_parts(tok[r, :].astype(jnp.float32))
        acc[4:5, :] += jnp.sum(grad * unit, axis=0, keepdims=True)
        acc[5:6, :] += jnp.sum(grad, axis=0, keepdims=True)
        gmix[r, :] = (gmix[r, :].astype(jnp.float32) + norm_back(grad, unit, inv, gain)).astype(bf)
        save(g).start()

    turn = 2 * ch1.reach + SLACK
    ready = KV_STEP + chk.reach

    def finished(s):
        return jnp.clip(jnp.minimum(2 * (s - ready), s - turn + 1), 0, chunks)

    def out_copy(i):
        to = lax.rem(me + i + 1, groups)
        return cp_copy(i, outw_h.at[:, pl.ds(pl.multiple_of(to * per, per), per)], out_in.at[i], o_s, o_r)

    @pl.loop(0, max(chunks + turn, ready + 1 + chunks // 2, ready + 1 + groups))
    def _(s):
        pl.when(s + 2 < chunks)(lambda: project(s + 2))
        pl.when(within(s, chunks))(lambda: ch1.mate_copy(s).wait_recv())
        serve(ch1, s, chunks, SLACK)

        @pl.when(s == 0)
        def _():
            kv_send()
            for load in loads:
                load.wait()

        @pl.when(s < chunks // 2)
        def _():
            normed(2 * s)
            normed(2 * s + 1)

        pl.when(s == KV_STEP)(kv_gather)
        serve(chk, 2 * (s - KV_STEP), 1, 0)
        serve(chk, 2 * (s - KV_STEP) + 1, 1, 0)
        pl.when(s == ready)(lambda: chk.done(0))
        i = s - ready - 1
        pl.when(within(i, groups))(lambda: weights(i))
        pl.loop(finished(s - 1), finished(s))(finish)

    acc[6:7, 0 : usum.shape[1]] = usum[...]
    at = usum.shape[1]
    acc[6:7, at : at + heads_wide] = jnp.sum(gq[...].astype(jnp.float32), axis=0, keepdims=True)
    at += heads_wide
    acc[6:7, at : at + size] = jnp.sum(okv[:, size:].astype(jnp.float32), axis=0, keepdims=True)

    def v_copy(i):
        return cp_copy(i, acc, v_in.at[i], v_s, v_r)

    for i in range(groups - 1):
        v_copy(i).start()
    kv_mate.wait_send()
    chk.drain(0)

    @pl.loop(0, groups - 1)
    def _(i):
        w_copy(i).wait_recv()
        own[...] += w_in[i].astype(jnp.float32)
        w_copy(i).wait_send()
        kv_copy(i).wait_send()
        out_copy(i).wait()

    @pl.loop(0, chunks)
    def _(g):
        save(g).wait()
        ch1.drain(g)

    total = jnp.zeros_like(acc)
    for i in range(groups - 1):
        v_copy(i).wait_recv()
    for source in range(groups):
        slot = lax.rem(me - source - 1 + groups, groups)
        theirs = v_in[jnp.minimum(slot, groups - 2)]
        total += jnp.where(slot == groups - 1, acc[...], theirs)
    vout[...] = total
    for i in range(groups - 1):
        v_copy(i).wait_send()


def tail(gq, dkv, wq, wk, wv, vectors, sums, usum, tokens, grad_mixed, outw, groups, chunks=8):
    rows, wide = tokens.shape
    heads_wide, two = gq.shape[1], 2 * wk.shape[1]
    bf, f32 = jnp.bfloat16, jnp.float32
    sds, vm = jax.ShapeDtypeStruct, pltpu.VMEM
    v, a = pl.BlockSpec(memory_space=pltpu.VMEM), pl.BlockSpec(memory_space=pl.ANY)
    dma = pltpu.SemaphoreType.DMA
    per, both = wide // groups, heads_wide + two
    return pl.pallas_call(
        functools.partial(tail_kernel, chunks),
        out_shape=(
            sds((rows, wide), bf),
            sds((groups - 1, heads_wide, per), bf),
            sds((per, both), f32),
            sds((8, wide), f32),
        ),
        in_specs=[v] * 9 + [a, a, a],
        out_specs=(a, a, v, v),
        scratch_shapes=[
            *[vm((rows, wide), bf)] * 5,
            vm((rows // 2, wide), bf), vm((rows // 2, wide), bf), vm((rows // 4, wide), bf),
            vm((rows // (4 * chunks), wide), f32),
            vm((groups, rows // 2, two), bf),
            vm((groups, rows // 2, two), bf),
            vm((groups - 1, rows // 2, two), bf),
            vm((rows, two), bf),
            vm((rows, two), bf),
            vm((rows // 2, two), bf),
            vm((rows // 4, two), bf),
            vm((rows // 4, two), f32),
            vm((groups - 1, per, both), bf),
            vm((groups - 1, per, both), bf),
            vm((8, wide), f32),
            vm((groups - 1, 8, wide), f32),
            dma((2,)), dma((chunks,)), dma((groups - 1,)), dma((groups - 1,)), dma, dma,
            dma((groups - 1,)), dma((groups - 1,)), dma((groups - 1,)), dma((groups - 1,)),
            dma((groups - 1,)), dma((groups - 1,)),
            *Chain.sems(chunks), *Chain.sems(1),
        ],
        compiler_params=pltpu.CompilerParams(
            collective_id=3, has_side_effects=True, vmem_limit_bytes=61 * MIB
        ),
        name="tail",
    )(gq, dkv, wq, wk, wv, *vectors, sums, usum, tokens, grad_mixed, outw)


def shards(
    tokens,
    cotangent,
    first_gain,
    first_bias,
    query_weight,
    query_bias,
    key_weight,
    value_weight,
    value_bias,
    out_weight,
    out_bias,
    second_gain,
    second_bias,
    up_weight,
    up_bias,
    down_weight,
    down_bias,
    file_lengths,
    pad_mask,
):
    groups = lax.axis_size("cp")
    queries, gathered = head(
        tokens, query_weight, key_weight, value_weight, (first_gain, first_bias, query_bias, value_bias), groups
    )
    attended, attended_low, log_total = attend(queries, gathered, file_lengths, pad_mask)
    block_low, grad_mixed, grad_attended, down_own, down_in, up_grad, out_part, out_own, sums, up_sum = middle(
        attended_low, tokens, cotangent, out_weight, up_weight, down_weight,
        (second_gain, second_bias, out_bias, down_bias, up_bias), groups,
    )
    up_grad = lax.psum_scatter(up_grad, "cp", scatter_dimension=0, tiled=True)
    grad_queries, key_value_parts, block_out, down_grad = attend_back(
        queries, grad_attended, attended, log_total, gathered, file_lengths, pad_mask,
        block_low, down_own, down_in,
    )
    tokens_low, out_in, own_grads, sums = tail(
        grad_queries, key_value_parts.reshape(groups, -1, gathered.shape[1]), query_weight,
        key_weight, value_weight, (first_gain, first_bias), sums, up_sum, tokens, grad_mixed, out_part, groups,
    )
    (
        tokens_grad, query_grad, key_grad, value_grad, up_grad, out_grad,
        down_bias_grad, second_gain_grad, second_bias_grad, out_bias_grad, first_gain_grad, first_bias_grad,
        up_bias_grad, query_bias_grad, value_bias_grad,
    ) = emit(tokens_low, own_grads, up_grad, out_own, out_in, sums, query_weight.shape[1])
    return (
        block_out,
        tokens_grad,
        first_gain_grad,
        first_bias_grad,
        query_grad,
        query_bias_grad,
        key_grad,
        value_grad,
        value_bias_grad,
        out_grad,
        out_bias_grad,
        second_gain_grad,
        second_bias_grad,
        up_grad,
        up_bias_grad,
        down_grad,
        down_bias_grad,
    )


def solution(mesh):
    placed = (
        P("cp", None),
        P("cp", None),
        P(),
        P(),
        P(None, "tp"),
        P("tp"),
        P(),
        P(),
        P(),
        P("tp", None),
        P(),
        P(),
        P(),
        P(None, "tp"),
        P("tp"),
        P("tp", None),
        P(),
        P(),
        P(),
    )
    return jax.shard_map(
        shards,
        mesh=mesh,
        in_specs=placed,
        out_specs=(
            P("cp", None),
            P("cp", None),
            P(),
            P(),
            P("cp", "tp"),
            P("tp"),
            P("cp", None),
            P("cp", None),
            P(),
            P("tp", "cp"),
            P(),
            P(),
            P(),
            P("cp", "tp"),
            P("tp"),
            P("tp", "cp"),
            P(),
        ),
        check_vma=False,
    )
```

```python
import functools
import math

import jax
import jax.numpy as jnp
from jax import lax
from jax.experimental import pallas as pl
from jax.experimental.pallas import tpu as pltpu
from jax.sharding import PartitionSpec as P

EPSILON = 1e-05
NEGATIVE = -1e30
LOG2E = 1.4426950408889634
LN2 = 0.6931471805599453
NT = (((1,), (1,)), ((), ()))
NN = (((1,), (0,)), ((), ()))
TN = (((0,), (0,)), ((), ()))
MIB = 2**20


def mm(a, b, dims=NN):
    return lax.dot_general(a, b, dims, preferred_element_type=jnp.float32)


def file_start(lengths, pos):
    end, start = 0, jnp.zeros_like(pos)
    for i in range(lengths.shape[0]):
        end = end + lengths[i]
        start = jnp.where(pos >= end, end, start)
    return start


def key_ids(pad, j, keys):
    pos = j * keys + lax.broadcasted_iota(jnp.int32, (1, keys), 1)
    return jnp.where(pad[pl.ds(pl.multiple_of(j * keys, keys), keys)].reshape(1, -1) == 1, pos, -1)


def as_column(row):
    return jnp.transpose(jnp.broadcast_to(row, (128, row.shape[1])))[:, :1]


def attend_kernel(rows, keys, heads, size, len_ref, q_ref, kv_ref, pad_ref, o_ref, low_ref, lse_ref):
    scale2 = LOG2E / math.sqrt(size)
    base = (lax.axis_index("cp") * pl.num_programs(0) + pl.program_id(0)) * rows
    row_pos = base + lax.broadcasted_iota(jnp.int32, (rows, 1), 0)
    row_start = as_column(file_start(len_ref, base + lax.broadcasted_iota(jnp.int32, (1, rows), 1)))
    ones = jnp.ones((keys, size), jnp.bfloat16)

    def block(j, carry, diagonal):
        here = pl.ds(pl.multiple_of(j * keys, keys), keys)
        k = kv_ref[here, :size]
        v1 = jnp.concatenate([kv_ref[here, size:], ones], axis=1)
        kid = key_ids(pad_ref, j, keys)
        ok = kid >= row_start
        if diagonal:
            col = j * keys + lax.broadcasted_iota(jnp.int32, (1, keys), 1)
            ok = (ok & (kid <= row_pos)) | (col == row_pos)
        out = []
        for h in range(heads):
            top, acc = carry[h]
            s = jnp.where(ok, mm(q_ref[:, h * size : (h + 1) * size], k, NT) * scale2, NEGATIVE)
            new = jnp.maximum(top, jnp.max(s, axis=1, keepdims=True))
            w = jnp.exp2(s - new).astype(jnp.bfloat16)
            out.append((new, acc * jnp.exp2(top - new) + mm(w, v1)))
        return tuple(out)

    carry = tuple(
        (jnp.full((rows, 1), NEGATIVE, jnp.float32), jnp.zeros((rows, 2 * size), jnp.float32))
        for _ in range(heads)
    )
    full = base // keys
    carry = lax.fori_loop(file_start(len_ref, base) // keys, full, lambda j, c: block(j, c, False), carry)
    last = (base + rows + keys - 1) // keys
    carry = lax.fori_loop(full, last, lambda j, c: block(j, c, True), carry)
    for h in range(heads):
        top, acc = carry[h]
        total = acc[:, size:]
        out = acc[:, :size] / total
        o_ref[:, h * size : (h + 1) * size] = out
        low_ref[:, h * size : (h + 1) * size] = out.astype(jnp.bfloat16)
        lse_ref[h : h + 1, :] = jnp.transpose(top + jnp.log2(total))[0:1]


def attend(q, kv, lengths, pad, rows=512, keys=512):
    total, wide = q.shape
    size = kv.shape[1] // 2
    heads = wide // size
    by_row = pl.BlockSpec((rows, wide), lambda i, f: (i, 0))
    return pl.pallas_call(
        functools.partial(attend_kernel, rows, keys, heads, size),
        out_shape=(
            jax.ShapeDtypeStruct((total, wide), jnp.float32),
            jax.ShapeDtypeStruct((total, wide), jnp.bfloat16),
            jax.ShapeDtypeStruct((heads, total), jnp.float32),
        ),
        grid_spec=pltpu.PrefetchScalarGridSpec(
            num_scalar_prefetch=1,
            grid=(total // rows,),
            in_specs=[
                by_row,
                pl.BlockSpec(kv.shape, lambda i, f: (0, 0)),
                pl.BlockSpec(pad.shape, lambda i, f: (0,)),
            ],
            out_specs=[by_row, by_row, pl.BlockSpec((heads, rows), lambda i, f: (0, i))],
        ),
        compiler_params=pltpu.CompilerParams(vmem_limit_bytes=61 * MIB),
        name="attend",
    )(lengths, q, kv, pad)


def attend_back_kernel(
    rows, keys, heads, size, len_ref, q_ref, do_ref, o_ref, lse_ref, kv_ref, pad_ref, block_h, down_h, in_h,
    dq_ref, dkv_ref, block_o, down_o, acc_ref, block_v, down_v, in_v, pass_s,
):
    i = pl.program_id(0)
    scale = 1.0 / math.sqrt(size)
    base = (lax.axis_index("cp") * pl.num_programs(0) + i) * rows
    row_pos = base + lax.broadcasted_iota(jnp.int32, (1, rows), 1)
    row_start = file_start(len_ref, row_pos)
    fetched = [
        pltpu.make_async_copy(src, dst, pass_s.at[k])
        for k, (src, dst) in enumerate(((block_h, block_v), (down_h, down_v), (in_h, in_v)))
    ]
    passed = [
        pltpu.make_async_copy(block_v, block_o, pass_s.at[3]),
        pltpu.make_async_copy(down_v, down_o, pass_s.at[4]),
    ]

    @pl.when(i == 0)
    def _():
        for copy in fetched:
            copy.start()
        acc_ref[...] = jnp.zeros_like(acc_ref)

    @pl.when(i == pl.num_programs(0) - 1)
    def _():
        for copy in fetched:
            copy.wait()
        passed[0].start()

        @pl.loop(0, 8)
        def _(j):
            r = chunk_rows(j, down_v.shape[0] // 8)
            total = down_v[r, :]
            for k in range(in_v.shape[0]):
                total += in_v[k, r, :].astype(jnp.float32)
            down_v[r, :] = total

        passed[1].start()

    deltas = []
    for h in range(heads):
        cols = slice(h * size, (h + 1) * size)
        both = do_ref[:, cols].astype(jnp.float32) * o_ref[:, cols]
        deltas.append(jnp.sum(jnp.transpose(both), axis=0, keepdims=True))

    def block(j, carry, diagonal):
        here = pl.ds(pl.multiple_of(j * keys, keys), keys)
        k = kv_ref[here, :size]
        v = kv_ref[here, size:]
        kid = as_column(key_ids(pad_ref, j, keys))
        ok = kid >= row_start
        if diagonal:
            col = j * keys + lax.broadcasted_iota(jnp.int32, (keys, 1), 0)
            ok = (ok & (kid <= row_pos)) | (col == row_pos)
        out = []
        dk = acc_ref[here, :size]
        dv = acc_ref[here, size:]
        for h in range(heads):
            cols = slice(h * size, (h + 1) * size)
            q = q_ref[:, cols]
            do = do_ref[:, cols]
            s = mm(k, q, NT) * (scale * LOG2E) - lse_ref[h : h + 1, :]
            p = jnp.where(ok, jnp.exp2(s), 0.0)
            ds = (p * (mm(v, do, NT) - deltas[h])).astype(jnp.bfloat16)
            dv = dv + mm(p.astype(jnp.bfloat16), do)
            dk = dk + mm(ds, q)
            out.append(carry[h] + mm(ds, k, TN))
        acc_ref[here, :size] = dk
        acc_ref[here, size:] = dv
        return tuple(out)

    carry = tuple(jnp.zeros((rows, size), jnp.float32) for _ in range(heads))
    full = base // keys
    carry = lax.fori_loop(file_start(len_ref, base) // keys, full, lambda j, c: block(j, c, False), carry)
    last = (base + rows + keys - 1) // keys
    carry = lax.fori_loop(full, last, lambda j, c: block(j, c, True), carry)
    for h in range(heads):
        dq_ref[:, h * size : (h + 1) * size] = (carry[h] * scale).astype(dq_ref.dtype)

    @pl.when(i == pl.num_programs(0) - 1)
    def _():
        dkv_ref[:, :size] = (acc_ref[:, :size] * scale).astype(dkv_ref.dtype)
        dkv_ref[:, size:] = acc_ref[:, size:].astype(dkv_ref.dtype)
        for copy in passed:
            copy.wait()


def attend_back(q, do, o, lse, kv, lengths, pad, block, down, down_in, rows=512, keys=512):
    total, wide = q.shape
    size = kv.shape[1] // 2
    heads = wide // size
    by_row = pl.BlockSpec((rows, wide), lambda i, f: (i, 0))
    whole = pl.BlockSpec(kv.shape, lambda i, f: (0, 0))
    far = pl.BlockSpec(memory_space=pl.ANY)
    return pl.pallas_call(
        functools.partial(attend_back_kernel, rows, keys, heads, size),
        out_shape=(
            jax.ShapeDtypeStruct((total, wide), jnp.bfloat16),
            jax.ShapeDtypeStruct(kv.shape, jnp.bfloat16),
            jax.ShapeDtypeStruct(block.shape, block.dtype),
            jax.ShapeDtypeStruct(down.shape, down.dtype),
        ),
        grid_spec=pltpu.PrefetchScalarGridSpec(
            num_scalar_prefetch=1,
            grid=(total // rows,),
            in_specs=[
                by_row,
                by_row,
                by_row,
                pl.BlockSpec((heads, rows), lambda i, f: (0, i)),
                whole,
                pl.BlockSpec(pad.shape, lambda i, f: (0,)),
                far,
                far,
                far,
            ],
            out_specs=[by_row, whole, far, far],
            scratch_shapes=[
                pltpu.VMEM(kv.shape, jnp.float32),
                pltpu.VMEM(block.shape, block.dtype),
                pltpu.VMEM(down.shape, down.dtype),
                pltpu.VMEM(down_in.shape, down_in.dtype),
                pltpu.SemaphoreType.DMA((5,)),
            ],
        ),
        compiler_params=pltpu.CompilerParams(vmem_limit_bytes=61 * MIB),
        name="attend_back",
    )(lengths, q, do, o, lse, kv, pad, block, down, down_in)


def emit_kernel(
    heads_wide, low, own, up, up_in, out, out_in, sums, tokens_o, q_o, k_o, v_o, up_o, out_o, *vectors
):
    total = up[...].astype(jnp.float32)
    for i in range(up_in.shape[0]):
        total += up_in[i].astype(jnp.float32)
    up_o[...] = total
    tokens_o[...] = low[...].astype(jnp.float32)
    size = k_o.shape[1]
    q_o[...] = own[:, :heads_wide]
    k_o[...] = own[:, heads_wide : heads_wide + size]
    v_o[...] = own[:, heads_wide + size :]
    total = out[...]
    for i in range(out_in.shape[0]):
        total += out_in[i].astype(jnp.float32)
    out_o[...] = total

    @pl.when(pl.program_id(0) == 0)
    def _():
        for i in range(6):
            vectors[i][...] = sums[i : i + 1, :].reshape(-1)
        at = 0
        for ref in vectors[6:]:
            ref[...] = sums[6:7, at : at + ref.shape[0]].reshape(-1)
            at += ref.shape[0]


def emit(low, own, up, up_in, out, out_in, sums, heads_wide, steps=4):
    size = (own.shape[1] - heads_wide) // 2
    wide, hidden = low.shape[1], up.shape[1]
    f32 = jnp.float32

    def rows_of(shape):
        if len(shape) == 3:
            return pl.BlockSpec((shape[0], shape[1] // steps, shape[2]), lambda i: (0, i, 0))
        return pl.BlockSpec((shape[0] // steps, shape[1]), lambda i: (i, 0))

    lengths = (wide,) * 6 + (hidden, heads_wide, size)
    per = own.shape[0]
    shapes = (low.shape, (per, heads_wide), (per, size), (per, size), up.shape, out.shape)
    blocks = (low, own, up, up_in, out, out_in)
    return pl.pallas_call(
        functools.partial(emit_kernel, heads_wide),
        out_shape=tuple(jax.ShapeDtypeStruct(x, f32) for x in (*shapes, *((n,) for n in lengths))),
        grid=(steps,),
        in_specs=[*(rows_of(x.shape) for x in blocks), pl.BlockSpec(sums.shape, lambda i: (0, 0))],
        out_specs=(*(rows_of(x) for x in shapes), *(pl.BlockSpec((n,), lambda i: (0,)) for n in lengths)),
        compiler_params=pltpu.CompilerParams(vmem_limit_bytes=61 * MIB),
        name="emit",
    )(*blocks, sums)


def as_row(ref):
    return ref[...].astype(jnp.float32).reshape(1, -1)


MESH = pl.DeviceIdType.MESH


class Chain:
    def __init__(self, chunks, quarter, part, out, mate, in0, in1, tmp, sems, hop=1):
        tp = lax.axis_index("tp")
        self.n = lax.axis_size("tp") // 2
        self.p, self.c = tp // 2, tp % 2
        self.chunks, self.q = chunks, quarter
        self.part, self.out, self.mate, self.in0, self.in1, self.tmp = part, out, mate, in0, in1, tmp
        (self.mate_s, self.mate_r, self.ch_s, self.in0_r, self.in1_r, self.bl_s, self.br_s, self.bc_r, self.fin_s, self.fin_r) = sems
        self.roots = (self.n // 2 - 1, self.n // 2)
        self.hop = hop
        self.reach = hop * max(self.roots[0], self.n - 1 - self.roots[0])

    @staticmethod
    def sems(chunks):
        one, two = pltpu.SemaphoreType.DMA((chunks,)), pltpu.SemaphoreType.DMA((chunks, 2))
        return [one, one, two, two, one, two, two, two, two, two]

    def at(self, p, c):
        return {"tp": p * 2 + c}

    def rows(self, g, c, part):
        q = self.q
        return pl.ds(pl.multiple_of(g * (4 * q) + c * (2 * q) + part * q, q), q)

    def own(self, g, part):
        q = self.q
        return pl.ds(pl.multiple_of(g * (2 * q) + part * q, q), q)

    def copy(self, src, dst, s, r, p, c):
        return pltpu.make_async_remote_copy(src, dst, s, r, device_id=self.at(p, c), device_id_type=MESH)

    def mate_copy(self, g):
        q = self.q
        src = self.part.at[pl.ds(pl.multiple_of(g * (4 * q) + (1 - self.c) * (2 * q), 2 * q), 2 * q)]
        dst = self.mate.at[pl.ds(pl.multiple_of(g * (2 * q), 2 * q), 2 * q)]
        return self.copy(src, dst, self.mate_s.at[g], self.mate_r.at[g], self.p, 1 - self.c)

    def in_copy(self, g, k, to):
        return self.copy(self.part.at[self.rows(g, self.c, k)], self.in0.at[self.own(g, k)], self.ch_s.at[g, k], self.in0_r.at[g, k], to, self.c)

    def in1_copy(self, g, k, to):
        q = self.q
        dst = self.in1.at[pl.ds(pl.multiple_of(g * q, q), q)]
        return self.copy(self.part.at[self.rows(g, self.c, k)], dst, self.ch_s.at[g, k], self.in1_r.at[g], to, self.c)

    def out_copy(self, g, k, to, sem):
        here = self.out.at[self.rows(g, self.c, k)]
        return self.copy(here, here, sem.at[g, k], self.bc_r.at[g, k], to, self.c)

    def fin_copy(self, g, k):
        here = self.out.at[self.rows(g, self.c, k)]
        return self.copy(here, here, self.fin_s.at[g, k], self.fin_r.at[g, k], self.p, 1 - self.c)

    def lag_up(self, k):
        root = self.roots[k]
        return jnp.where(
            self.p == root, self.reach, self.hop * jnp.where(self.p < root, self.p, self.n - 1 - self.p)
        )

    def lag_down(self, k):
        return self.reach + self.hop * jnp.abs(self.p - self.roots[k])

    def start_mate(self, g):
        self.mate_copy(g).start()

    def reduce(self, g, k):
        root, p, n, q = self.roots[k], self.p, self.n, self.q
        rows, own, tmp = self.rows(g, self.c, k), self.own(g, k), self.tmp
        if self.mate is None:
            tmp[...] = self.part[rows, :].astype(jnp.float32)
        else:
            tmp[...] = self.part[rows, :].astype(jnp.float32) + self.mate[own, :].astype(jnp.float32)

        @pl.when(((p > 0) & (p <= root)) | ((p > root) & (p < n - 1)))
        def _():
            self.in_copy(g, k, p).wait_recv()
            tmp[...] += self.in0[own, :].astype(jnp.float32)

        @pl.when((p == root) & (p < n - 1))
        def _():
            self.in1_copy(g, k, p).wait_recv()
            tmp[...] += self.in1[pl.ds(pl.multiple_of(g * q, q), q), :].astype(jnp.float32)

        @pl.when(p != root)
        def _():
            self.part[rows, :] = tmp[...].astype(jnp.bfloat16)

        @pl.when(p < root)
        def _():
            self.in_copy(g, k, p + 1).start()

        @pl.when(p > root + 1)
        def _():
            self.in_copy(g, k, p - 1).start()

        @pl.when(p == root + 1)
        def _():
            self.in1_copy(g, k, p - 1).start()

        @pl.when(p == root)
        def _():
            self.out[rows, :] = tmp[...].astype(jnp.bfloat16)
            self.spread(g, k)

    def spread(self, g, k):
        root, p, n = self.roots[k], self.p, self.n

        @pl.when((p <= root) & (p > 0))
        def _():
            self.out_copy(g, k, p - 1, self.bl_s).start()

        @pl.when((p >= root) & (p < n - 1))
        def _():
            self.out_copy(g, k, p + 1, self.br_s).start()

        self.fin_copy(g, k).start()

    def down(self, g, k):
        @pl.when(self.p != self.roots[k])
        def _():
            self.out_copy(g, k, self.p, self.bl_s).wait_recv()
            self.spread(g, k)

    def done(self, g):
        for k in range(2):
            self.fin_copy(g, k).wait_recv()

    def drain(self, g):
        p, n = self.p, self.n
        if self.mate is not None:
            self.mate_copy(g).wait_send()
        for k, root in enumerate(self.roots):

            @pl.when(p != root)
            def _():
                self.in_copy(g, k, p).wait_send()

            @pl.when((p <= root) & (p > 0))
            def _():
                self.out_copy(g, k, p, self.bl_s).wait_send()

            @pl.when((p >= root) & (p < n - 1))
            def _():
                self.out_copy(g, k, p, self.br_s).wait_send()

            self.fin_copy(g, k).wait_send()


def within(g, chunks):
    return (g >= 0) & (g < chunks)


def chunk_rows(g, rows):
    return pl.ds(pl.multiple_of(g * rows, rows), rows)


def norm_parts(values):
    centre = jnp.mean(values, axis=1, keepdims=True)
    centred = values - centre
    inv = lax.rsqrt(jnp.mean(centred * centred, axis=1, keepdims=True) + EPSILON)
    return centred * inv, inv


def norm_back(grad, unit, inv, gain):
    e = grad * gain
    return inv * (
        e - jnp.mean(e, axis=1, keepdims=True) - unit * jnp.mean(e * unit, axis=1, keepdims=True)
    )


def greet(chips, peers):
    tp, me = lax.axis_index("tp"), lax.axis_index("cp")
    n, groups = lax.axis_size("tp") // 2, lax.axis_size("cp")
    p, c = tp // 2, tp % 2
    bar = pltpu.get_barrier_semaphore()
    count = 1
    pl.semaphore_signal(bar, 1, device_id={"tp": p * 2 + 1 - c}, device_id_type=MESH)
    if chips:

        @pl.when(p > 0)
        def _():
            pl.semaphore_signal(bar, 1, device_id={"tp": tp - 2}, device_id_type=MESH)

        @pl.when(p < n - 1)
        def _():
            pl.semaphore_signal(bar, 1, device_id={"tp": tp + 2}, device_id_type=MESH)

        count += (p > 0).astype(jnp.int32) + (p < n - 1).astype(jnp.int32)
    if peers:
        for i in range(1, groups):
            pl.semaphore_signal(bar, 1, device_id={"cp": lax.rem(me + i, groups)}, device_id_type=MESH)
        count += groups - 1
    return lambda: pl.semaphore_wait(bar, count)


def cp_copy(i, src, dst, send, recv):
    to = lax.rem(lax.axis_index("cp") + i + 1, lax.axis_size("cp"))
    return pltpu.make_async_remote_copy(
        src, dst, send.at[i], recv.at[i], device_id={"cp": to}, device_id_type=MESH
    )


SLACK = 0
HOP = 1


def middle_kernel(
    chunks,
    attn_h, wo_h, gain_v, bias_v, ob_v, db_v, ub_v, tok_h, cot_h, wu_h, wd_h,
    out_h, gmix_h, gattn, down_own, down_in, up_own_h, up_h, outw_h, out_own, sums, usum,
    attn, wo, tok, cot, wu, wd, hid, h2, gup, pa, pc, pb, out1, out2, out3, mate, in0, in1, tmp,
    load_s, save_s, gm_s, up_o, ow_s, dn_s, dn_r,
    *sems,
):
    rows = tok.shape[0] // chunks
    groups, me = lax.axis_size("cp"), lax.axis_index("cp")
    wide = tok.shape[1]
    per = wide // groups
    bf = jnp.bfloat16
    third = len(sems) // 3
    ch1 = Chain(chunks, rows // 4, pa, out1, mate, in0, in1, tmp, sems[:third], HOP)
    ch3 = Chain(chunks, rows // 4, pc, out3, mate, in0, in1, tmp, sems[third : 2 * third], HOP)
    ch2 = Chain(chunks, rows // 4, pb, out2, mate, in0, in1, tmp, sems[2 * third :], HOP)
    first = (lax.axis_index("tp") == 0).astype(jnp.float32)
    loads = [
        pltpu.make_async_copy(src, dst, load_s.at[i])
        for i, (src, dst) in enumerate(
            ((attn_h, attn), (wo_h, wo), (tok_h, tok), (wu_h, wu), (wd_h, wd), (cot_h, cot))
        )
    ]
    for load in loads:
        load.start()
    greet(True, True)()
    gain, bias, out_bias, down_bias, up_bias = (as_row(x) for x in (gain_v, bias_v, ob_v, db_v, ub_v))
    sums[...] = jnp.zeros_like(sums)
    usum[...] = jnp.zeros_like(usum)

    def project(g):
        r = chunk_rows(g, rows)
        pa[r, :] = mm(attn[r, :], wo[...]).astype(bf)
        ch1.start_mate(g)

    def halves(g):
        return [chunk_rows(2 * g + i, rows // 2) for i in range(2)]

    def middle_of(r):
        return tok[r, :].astype(jnp.float32) + out1[r, :].astype(jnp.float32) + out_bias

    def feed(g):
        r = chunk_rows(g, rows)
        ch1.done(g)
        for part in halves(g):
            unit, _ = norm_parts(middle_of(part))
            h2[part, :] = (unit * gain + bias).astype(bf)
        up = mm(h2[r, :], wu[...]) + up_bias
        sq = up * up
        t = jnp.tanh(0.7978845608028654 * up * (1.0 + 0.044715 * sq))
        half = 0.5 * (1.0 + t)
        hid[r, :] = (half * up).astype(bf)
        slope = half + 0.5 * up * (1.0 - t * t) * (0.7978845608028654 * (1.0 + 3.0 * 0.044715 * sq))
        gu = (slope * mm(cot[r, :], wd[...], NT)).astype(bf)
        gup[r, :] = gu
        usum[...] += jnp.sum(gu.astype(jnp.float32), axis=0, keepdims=True)
        sums[0:1, :] += jnp.sum(cot[r, :].astype(jnp.float32), axis=0, keepdims=True)
        pc[r, :] = mm(gup[r, :], wu[...], NT).astype(bf)
        ch3.start_mate(g)
        for part in halves(g):
            base = first * (middle_of(part) + down_bias)
            pb[part, :] = (mm(hid[part, :], wd[...]) + base).astype(bf)

    def back(g):
        r = chunk_rows(g, rows)
        ch3.done(g)
        ch1.drain(g)
        for part in halves(g):
            unit, inv = norm_parts(middle_of(part))
            grad = out3[part, :].astype(jnp.float32)
            sums[1:2, :] += jnp.sum(grad * unit, axis=0, keepdims=True)
            sums[2:3, :] += jnp.sum(grad, axis=0, keepdims=True)
            gm = (cot[part, :].astype(jnp.float32) + norm_back(grad, unit, inv, gain)).astype(bf)
            sums[3:4, :] += jnp.sum(gm.astype(jnp.float32), axis=0, keepdims=True)
            pa[part, :] = gm
        pltpu.make_async_copy(pa.at[r], gmix_h.at[r], gm_s.at[g]).start()
        gattn[r, :] = mm(pa[r, :], wo[...], NT).astype(bf)
        ch2.start_mate(g)

    def finish(g):
        r = chunk_rows(g, rows)
        ch2.done(g)
        pltpu.make_async_copy(out2.at[r], out_h.at[r], save_s.at[g]).start()

    def down_copy(i):
        to = lax.rem(me + i + 1, groups)
        cols = pl.ds(pl.multiple_of(to * per, per), per)
        return cp_copy(i, wd.at[:, cols], down_in.at[i], dn_s, dn_r)

    def down_block(i):
        cols = pl.ds(pl.multiple_of(lax.rem(me + i + 1, groups) * per, per), per)
        half = hid.shape[1] // 2
        for j in range(2):
            part = mm(hid[:, j * half : (j + 1) * half], cot[:, cols], TN)

            @pl.when(i < groups - 1)
            def _():
                wd[j * half : (j + 1) * half, cols] = part.astype(bf)

            @pl.when(i == groups - 1)
            def _():
                down_own[j * half : (j + 1) * half, :] = part

        pl.when(i < groups - 1)(lambda: down_copy(i).start())

    def up_rows(i):
        return chunk_rows(lax.rem(me + i + 1, groups), per)

    def up_save(i):
        return pltpu.make_async_copy(wu.at[up_rows(i)], up_h.at[up_rows(i)], up_o.at[i])

    up_keep = pltpu.make_async_copy(wu.at[chunk_rows(me, per)], up_own_h, up_o.at[groups - 1])

    def up_block(i):
        for k in range(2):
            r = chunk_rows(2 * lax.rem(me + i + 1, groups) + k, per // 2)
            wu[r, :] = mm(h2[:, r], gup[...], TN).astype(bf)
        pl.when(i < groups - 1)(lambda: up_save(i).start())
        pl.when(i == groups - 1)(lambda: up_keep.start())

    def serve(ch, s):
        for k in range(2):
            g = s - ch.lag_up(k)
            pl.when(within(g, chunks))(functools.partial(ch.reduce, g, k))
        for k in range(2):
            g = s - ch.lag_down(k) - SLACK
            pl.when(within(g, chunks))(functools.partial(ch.down, g, k))

    def due(ch, s):
        pl.when(within(s, chunks))(lambda: ch.mate_copy(s).wait_recv())

    turn = 2 * ch1.reach + SLACK
    for load in loads[:2]:
        load.wait()
    project(0)
    project(1)

    @pl.loop(0, chunks + max(3 * turn, turn + 2 * groups))
    def _(s):
        pl.when(s + 2 < chunks)(lambda: project(s + 2))
        due(ch1, s)
        serve(ch1, s)

        @pl.when(s == turn)
        def _():
            for load in loads[2:]:
                load.wait()

        g = s - turn
        pl.when(within(g, chunks))(functools.partial(feed, g))
        due(ch3, g)
        serve(ch3, g)
        g = s - 2 * turn
        pl.when(within(g, chunks))(functools.partial(back, g))
        i = s - turn - chunks
        pl.when(within(i, groups))(functools.partial(down_block, i))
        due(ch2, g)
        serve(ch2, g)
        j = i - groups
        pl.when(within(j, groups))(functools.partial(up_block, j))
        g = s - 3 * turn
        pl.when(within(g, chunks))(functools.partial(finish, g))

    for j in range(4):
        cols = slice(j * (wide // 4), (j + 1) * (wide // 4))
        mate[0 : attn.shape[1], cols] = mm(attn[...], pa[:, cols], TN).astype(bf)
    out_save = pltpu.make_async_copy(mate.at[pl.ds(0, attn.shape[1])], outw_h, ow_s)
    out_save.start()
    out_own[...] = mate[0 : attn.shape[1], pl.ds(pl.multiple_of(me * per, per), per)].astype(jnp.float32)

    @pl.loop(0, groups - 1)
    def _(i):
        down_copy(i).wait()

    @pl.loop(0, chunks)
    def _(g):
        r = chunk_rows(g, rows)
        pltpu.make_async_copy(pa.at[r], gmix_h.at[r], gm_s.at[g]).wait()
        pltpu.make_async_copy(out2.at[r], out_h.at[r], save_s.at[g]).wait()
        ch3.drain(g)
        ch2.drain(g)

    for i in range(groups - 1):
        up_save(i).wait()
    up_keep.wait()
    out_save.wait()


def middle(attn, tokens, cotangent, wo, wu, wd, vectors, groups, chunks=8):
    rows, wide = tokens.shape
    heads_wide, hidden = wo.shape[0], wu.shape[1]
    bf, f32 = jnp.bfloat16, jnp.float32
    sds, vm = jax.ShapeDtypeStruct, pltpu.VMEM
    v, a = pl.BlockSpec(memory_space=pltpu.VMEM), pl.BlockSpec(memory_space=pl.ANY)
    dma = pltpu.SemaphoreType.DMA
    return pl.pallas_call(
        functools.partial(middle_kernel, chunks),
        out_shape=(
            sds((rows, wide), bf),
            sds((rows, wide), bf),
            sds((rows, heads_wide), bf),
            sds((hidden, wide // groups), f32),
            sds((groups - 1, hidden, wide // groups), bf),
            sds((wide // groups, hidden), bf),
            sds((wide, hidden), bf),
            sds((heads_wide, wide), bf),
            sds((heads_wide, wide // groups), f32),
            sds((8, wide), f32),
            sds((1, hidden), f32),
        ),
        in_specs=[a] * 2 + [v] * 5 + [a] * 4,
        out_specs=(a, a, v, v, a, a, a, a, v, v, v),
        scratch_shapes=[
            vm(attn.shape, bf), vm(wo.shape, bf),
            vm((rows, wide), bf), vm((rows, wide), bf), vm((wide, hidden), bf), vm((hidden, wide), bf),
            vm((rows, hidden), bf), vm((rows, wide), bf), vm((rows, hidden), bf),
            *[vm((rows, wide), bf)] * 6,
            vm((rows // 2, wide), bf), vm((rows // 2, wide), bf), vm((rows // 4, wide), bf),
            vm((rows // (4 * chunks), wide), f32),
            dma((6,)), dma((chunks,)), dma((chunks,)), dma((groups,)), dma, dma((groups - 1,)), dma((groups - 1,)),
            *Chain.sems(chunks), *Chain.sems(chunks), *Chain.sems(chunks),
        ],
        compiler_params=pltpu.CompilerParams(
            collective_id=2, has_side_effects=True, vmem_limit_bytes=61 * MIB
        ),
        name="middle",
    )(attn, wo, *vectors, tokens, cotangent, wu, wd)


HEAD_PARTS = 4


def head_kernel(
    gain_v, bias_v, qb_v, vb_v, tok_h, wq_h, wk_h, wv_h, q, kv, tok, h1, wq, wkv, load_s, w_s, x_s, x_r, f_s, f_r
):
    local = tok.shape[0]
    rows = local // HEAD_PARTS
    mine = HEAD_PARTS // 2
    groups, me = lax.axis_size("cp"), lax.axis_index("cp")
    tp = lax.axis_index("tp")
    core = tp % 2
    bf = jnp.bfloat16

    def load(part):
        r = chunk_rows(part, rows)
        return pltpu.make_async_copy(tok_h.at[r], tok.at[r], load_s.at[part])

    def part_at(i):
        return lax.rem(mine * core + i, HEAD_PARTS)

    def block(source, part):
        return pl.ds(pl.multiple_of(source * local + part * rows, rows), rows)

    def spread(j, i):
        here = kv.at[block(me, part_at(i))]
        to = lax.rem(me + j + 1, groups)
        return pltpu.make_async_remote_copy(
            here, here, x_s.at[j, i], x_r.at[j, i], device_id={"cp": to}, device_id_type=MESH
        )

    def forward(j, i):
        here = kv.at[block(lax.rem(me - j - 1 + groups, groups), part_at(i))]
        return pltpu.make_async_remote_copy(
            here, here, f_s.at[j, i], f_r.at[j, i], device_id={"tp": tp + 1 - 2 * core}, device_id_type=MESH
        )

    size = wk_h.shape[1]
    weights = [
        pltpu.make_async_copy(wk_h, wkv.at[:, pl.ds(0, size)], w_s.at[0]),
        pltpu.make_async_copy(wv_h, wkv.at[:, pl.ds(size, size)], w_s.at[1]),
        pltpu.make_async_copy(wq_h, wq, w_s.at[2]),
    ]
    load(part_at(0)).start()
    weights[0].start()
    weights[1].start()
    for i in range(1, HEAD_PARTS):
        load(part_at(i)).start()
    weights[2].start()
    greeted = greet(False, True)
    gain, bias, q_bias, v_bias = (as_row(x) for x in (gain_v, bias_v, qb_v, vb_v))
    kv_bias = jnp.concatenate([jnp.zeros_like(v_bias), v_bias], axis=1)
    for i in range(HEAD_PARTS):
        load(part_at(i)).wait()
        r = chunk_rows(part_at(i), rows)
        unit, _ = norm_parts(tok[r, :].astype(jnp.float32))
        h1[r, :] = (unit * gain + bias).astype(bf)
        if i == 0:
            weights[0].wait()
            weights[1].wait()
        kv[block(me, part_at(i)), :] = (mm(h1[r, :], wkv[...]) + kv_bias).astype(bf)
        if i == 0:
            greeted()
        if i < mine:
            for j in range(groups - 1):
                spread(j, i).start()
    weights[2].wait()
    for i in range(HEAD_PARTS):
        r = chunk_rows(part_at(i), rows)
        q[r, :] = (mm(h1[r, :], wq[...]) + q_bias).astype(bf)
    for i in range(mine):
        for j in range(groups - 1):
            spread(j, i).wait_recv()
            forward(j, i).start()
    for i in range(mine):
        for j in range(groups - 1):
            forward(j, i).wait()
            spread(j, i).wait_send()


def head(tokens, wq, wk, wv, vectors, groups):
    rows, wide = tokens.shape
    bf = jnp.bfloat16
    sds, vm = jax.ShapeDtypeStruct, pltpu.VMEM
    v, a = pl.BlockSpec(memory_space=pltpu.VMEM), pl.BlockSpec(memory_space=pl.ANY)
    dma, two = pltpu.SemaphoreType.DMA, 2 * wk.shape[1]
    pairs = dma((groups - 1, HEAD_PARTS // 2))
    return pl.pallas_call(
        head_kernel,
        out_shape=(sds((rows, wq.shape[1]), bf), sds((groups * rows, two), bf)),
        in_specs=[v] * 4 + [a] * 4,
        out_specs=(v, v),
        scratch_shapes=[
            vm((rows, wide), bf), vm((rows, wide), bf), vm(wq.shape, bf), vm((wide, two), bf),
            dma((HEAD_PARTS,)), dma((3,)), pairs, pairs, pairs, pairs,
        ],
        compiler_params=pltpu.CompilerParams(
            collective_id=1, has_side_effects=True, vmem_limit_bytes=61 * MIB
        ),
        name="head",
    )(*vectors, tokens, wq, wk, wv)


KV_STEP = 2
TAIL_HOP = 1


def tail_kernel(
    chunks,
    gq_h, dkv_h, wq_h, wk_h, wv_h, gain_v, bias_v, sums, usum, tok_h, gmix_h, outw_h, up_h,
    tgrad_h, out_in, up_in, own, vout,
    gq, dkv, wq, wkv, tok, gmix, h1, pa, out1, mate, in0, in1, tmp, kvm, kvs, kv_in, pkv, okv, kin0, kin1, ktmp,
    stage, w_in, acc, v_in,
    load_s, save_s, o_s, o_r, u_s, u_r, km_s, km_r, kx_s, kx_r, w_s, w_r, v_s, v_r,
    *sems,
):
    local, wide = tok.shape
    rows = local // chunks
    groups, me = lax.axis_size("cp"), lax.axis_index("cp")
    core = lax.axis_index("tp") % 2
    tp = lax.axis_index("tp")
    per = wide // groups
    heads_wide, size = gq.shape[1], wk_h.shape[1]
    bf = jnp.bfloat16
    half_sems = len(sems) // 2
    ch1 = Chain(chunks, rows // 4, pa, out1, mate, in0, in1, tmp, sems[:half_sems], TAIL_HOP)
    chk = Chain(1, local // 4, pkv, okv, None, kin0, kin1, ktmp, sems[half_sems:])
    loads = [
        pltpu.make_async_copy(src, dst, load_s.at[i])
        for i, (src, dst) in enumerate(
            (
                (gq_h, gq), (wq_h, wq), (dkv_h, dkv), (tok_h, tok), (gmix_h, gmix),
                (wk_h, wkv.at[:, pl.ds(0, size)]), (wv_h, wkv.at[:, pl.ds(size, size)]),
            )
        )
    ]
    for load in loads:
        load.start()
    greet(True, True)()
    own_half = chunk_rows(core, local // 2)
    kv_mate = pltpu.make_async_remote_copy(
        dkv_h.at[:, chunk_rows(1 - core, local // 2), :], kvm, km_s, km_r,
        device_id={"tp": tp + 1 - 2 * core}, device_id_type=MESH,
    )
    kv_mate.start()
    gain, bias = as_row(gain_v), as_row(bias_v)

    def project(g):
        r = chunk_rows(g, rows)
        pa[r, :] = mm(gq[r, :], wq[...], NT).astype(bf)
        ch1.start_mate(g)

    for load in loads[:2]:
        load.wait()
    project(0)
    project(1)
    acc[...] = sums[...]

    def kv_copy(i):
        to = lax.rem(me + i + 1, groups)
        return cp_copy(i, kvs.at[to], kv_in.at[i], kx_s, kx_r)

    def kv_send():
        kv_mate.wait_recv()

        @pl.loop(0, groups)
        def _(i):
            to = lax.rem(me + i + 1, groups)
            both = dkv[to, own_half, :].astype(jnp.float32) + kvm[to].astype(jnp.float32)
            kvs[to] = both.astype(bf)
            pl.when(i < groups - 1)(lambda: kv_copy(i).start())

        for i in range(groups - 1):
            out_copy(i).start()
        for i in range(groups - 1):
            up_copy(i).start()

    def normed(g):
        r = chunk_rows(g, rows)
        unit, _ = norm_parts(tok[r, :].astype(jnp.float32))
        h1[r, :] = (unit * gain + bias).astype(bf)

    def kv_gather():
        total = kvs[me].astype(jnp.float32)
        for i in range(groups - 1):
            kv_copy(i).wait_recv()
            total += kv_in[i].astype(jnp.float32)
        pkv[own_half, :] = total.astype(bf)

    def serve(ch, s, count, slack):
        for k in range(2):
            g = s - ch.lag_up(k)
            pl.when(within(g, count))(functools.partial(ch.reduce, g, k))
        for k in range(2):
            g = s - ch.lag_down(k) - slack
            pl.when(within(g, count))(functools.partial(ch.down, g, k))

    def w_copy(i):
        return cp_copy(i, stage.at[i], w_in.at[i], w_s, w_r)

    def weights(i):
        cols = pl.ds(pl.multiple_of(lax.rem(me + i + 1, groups) * per, per), per)
        part = mm(h1[:, cols], jnp.concatenate([gq[...], okv[...]], axis=1), TN)

        @pl.when(i < groups - 1)
        def _():
            stage[i] = part.astype(bf)
            w_copy(i).start()

        @pl.when(i == groups - 1)
        def _():
            own[...] = part

    def save(g):
        r = chunk_rows(g, rows)
        return pltpu.make_async_copy(gmix.at[r], tgrad_h.at[r], save_s.at[g])

    def finish(g):
        r = chunk_rows(g, rows)
        ch1.done(g)
        grad = out1[r, :].astype(jnp.float32) + mm(okv[r, :], wkv[...], NT)
        unit, inv = norm_parts(tok[r, :].astype(jnp.float32))
        acc[4:5, :] += jnp.sum(grad * unit, axis=0, keepdims=True)
        acc[5:6, :] += jnp.sum(grad, axis=0, keepdims=True)
        gmix[r, :] = (gmix[r, :].astype(jnp.float32) + norm_back(grad, unit, inv, gain)).astype(bf)
        save(g).start()

    turn = 2 * ch1.reach + SLACK
    ready = KV_STEP + chk.reach

    def finished(s):
        return jnp.clip(jnp.minimum(2 * (s - ready), s - turn + 1), 0, chunks)

    def up_copy(i):
        r = chunk_rows(lax.rem(me + i + 1, groups), per)
        return cp_copy(i, up_h.at[r], up_in.at[i], u_s, u_r)

    def out_copy(i):
        to = lax.rem(me + i + 1, groups)
        return cp_copy(i, outw_h.at[:, pl.ds(pl.multiple_of(to * per, per), per)], out_in.at[i], o_s, o_r)

    @pl.loop(0, max(chunks + turn, ready + 1 + chunks // 2, ready + 1 + groups))
    def _(s):
        pl.when(s + 2 < chunks)(lambda: project(s + 2))
        pl.when(within(s, chunks))(lambda: ch1.mate_copy(s).wait_recv())
        serve(ch1, s, chunks, SLACK)

        @pl.when(s == 0)
        def _():
            loads[2].wait()
            kv_send()
            for load in loads[3:]:
                load.wait()

        @pl.when(s < chunks // 2)
        def _():
            normed(2 * s)
            normed(2 * s + 1)

        pl.when(s == KV_STEP)(kv_gather)
        serve(chk, 2 * (s - KV_STEP), 1, 0)
        serve(chk, 2 * (s - KV_STEP) + 1, 1, 0)
        pl.when(s == ready)(lambda: chk.done(0))
        i = s - ready - 1
        pl.when(within(i, groups))(lambda: weights(i))
        pl.loop(finished(s - 1), finished(s))(finish)

    acc[6:7, 0 : usum.shape[1]] = usum[...]
    at = usum.shape[1]
    acc[6:7, at : at + heads_wide] = jnp.sum(gq[...].astype(jnp.float32), axis=0, keepdims=True)
    at += heads_wide
    acc[6:7, at : at + size] = jnp.sum(okv[:, size:].astype(jnp.float32), axis=0, keepdims=True)

    def v_copy(i):
        return cp_copy(i, acc, v_in.at[i], v_s, v_r)

    for i in range(groups - 1):
        v_copy(i).start()
    kv_mate.wait_send()
    chk.drain(0)
    for i in range(groups - 1):
        up_copy(i).wait()

    @pl.loop(0, groups - 1)
    def _(i):
        w_copy(i).wait_recv()
        own[...] += w_in[i].astype(jnp.float32)
        w_copy(i).wait_send()
        kv_copy(i).wait_send()
        out_copy(i).wait()

    @pl.loop(0, chunks)
    def _(g):
        save(g).wait()
        ch1.drain(g)

    total = jnp.zeros_like(acc)
    for i in range(groups - 1):
        v_copy(i).wait_recv()
    for source in range(groups):
        slot = lax.rem(me - source - 1 + groups, groups)
        theirs = v_in[jnp.minimum(slot, groups - 2)]
        total += jnp.where(slot == groups - 1, acc[...], theirs)
    vout[...] = total
    for i in range(groups - 1):
        v_copy(i).wait_send()


def tail(gq, dkv, wq, wk, wv, vectors, sums, usum, tokens, grad_mixed, outw, up, groups, chunks=8):
    rows, wide = tokens.shape
    heads_wide, two = gq.shape[1], 2 * wk.shape[1]
    bf, f32 = jnp.bfloat16, jnp.float32
    sds, vm = jax.ShapeDtypeStruct, pltpu.VMEM
    v, a = pl.BlockSpec(memory_space=pltpu.VMEM), pl.BlockSpec(memory_space=pl.ANY)
    dma = pltpu.SemaphoreType.DMA
    per, both = wide // groups, heads_wide + two
    return pl.pallas_call(
        functools.partial(tail_kernel, chunks),
        out_shape=(
            sds((rows, wide), bf),
            sds((groups - 1, heads_wide, per), bf),
            sds((groups - 1, per, up.shape[1]), bf),
            sds((per, both), f32),
            sds((8, wide), f32),
        ),
        in_specs=[a] * 5 + [v] * 4 + [a] * 4,
        out_specs=(a, a, a, v, v),
        scratch_shapes=[
            vm(gq.shape, bf), vm(dkv.shape, bf), vm(wq.shape, bf), vm((wide, two), bf),
            *[vm((rows, wide), bf)] * 5,
            vm((rows // 2, wide), bf), vm((rows // 2, wide), bf), vm((rows // 4, wide), bf),
            vm((rows // (4 * chunks), wide), f32),
            vm((groups, rows // 2, two), bf),
            vm((groups, rows // 2, two), bf),
            vm((groups - 1, rows // 2, two), bf),
            vm((rows, two), bf),
            vm((rows, two), bf),
            vm((rows // 2, two), bf),
            vm((rows // 4, two), bf),
            vm((rows // 4, two), f32),
            vm((groups - 1, per, both), bf),
            vm((groups - 1, per, both), bf),
            vm((8, wide), f32),
            vm((groups - 1, 8, wide), f32),
            dma((7,)), dma((chunks,)), *[dma((groups - 1,))] * 4, dma, dma,
            dma((groups - 1,)), dma((groups - 1,)), dma((groups - 1,)), dma((groups - 1,)),
            dma((groups - 1,)), dma((groups - 1,)),
            *Chain.sems(chunks), *Chain.sems(1),
        ],
        compiler_params=pltpu.CompilerParams(
            collective_id=3, has_side_effects=True, vmem_limit_bytes=61 * MIB
        ),
        name="tail",
    )(gq, dkv, wq, wk, wv, *vectors, sums, usum, tokens, grad_mixed, outw, up)


def shards(
    tokens,
    cotangent,
    first_gain,
    first_bias,
    query_weight,
    query_bias,
    key_weight,
    value_weight,
    value_bias,
    out_weight,
    out_bias,
    second_gain,
    second_bias,
    up_weight,
    up_bias,
    down_weight,
    down_bias,
    file_lengths,
    pad_mask,
):
    groups = lax.axis_size("cp")
    queries, gathered = head(
        tokens, query_weight, key_weight, value_weight, (first_gain, first_bias, query_bias, value_bias), groups
    )
    attended, attended_low, log_total = attend(queries, gathered, file_lengths, pad_mask)
    block_low, grad_mixed, grad_attended, down_own, down_in, up_own, up_part, out_part, out_own, sums, up_sum = middle(
        attended_low, tokens, cotangent, out_weight, up_weight, down_weight,
        (second_gain, second_bias, out_bias, down_bias, up_bias), groups,
    )
    grad_queries, key_value_parts, block_out, down_grad = attend_back(
        queries, grad_attended, attended, log_total, gathered, file_lengths, pad_mask,
        block_low, down_own, down_in,
    )
    tokens_low, out_in, up_in, own_grads, sums = tail(
        grad_queries, key_value_parts.reshape(groups, -1, gathered.shape[1]), query_weight,
        key_weight, value_weight, (first_gain, first_bias), sums, up_sum, tokens, grad_mixed, out_part, up_part, groups,
    )
    (
        tokens_grad, query_grad, key_grad, value_grad, up_grad, out_grad,
        down_bias_grad, second_gain_grad, second_bias_grad, out_bias_grad, first_gain_grad, first_bias_grad,
        up_bias_grad, query_bias_grad, value_bias_grad,
    ) = emit(
        tokens_low, own_grads, up_own, up_in, out_own, out_in, sums, query_weight.shape[1]
    )
    return (
        block_out,
        tokens_grad,
        first_gain_grad,
        first_bias_grad,
        query_grad,
        query_bias_grad,
        key_grad,
        value_grad,
        value_bias_grad,
        out_grad,
        out_bias_grad,
        second_gain_grad,
        second_bias_grad,
        up_grad,
        up_bias_grad,
        down_grad,
        down_bias_grad,
    )


def solution(mesh):
    placed = (
        P("cp", None),
        P("cp", None),
        P(),
        P(),
        P(None, "tp"),
        P("tp"),
        P(),
        P(),
        P(),
        P("tp", None),
        P(),
        P(),
        P(),
        P(None, "tp"),
        P("tp"),
        P("tp", None),
        P(),
        P(),
        P(),
    )
    return jax.shard_map(
        shards,
        mesh=mesh,
        in_specs=placed,
        out_specs=(
            P("cp", None),
            P("cp", None),
            P(),
            P(),
            P("cp", "tp"),
            P("tp"),
            P("cp", None),
            P("cp", None),
            P(),
            P("tp", "cp"),
            P(),
            P(),
            P(),
            P("cp", "tp"),
            P("tp"),
            P("tp", "cp"),
            P(),
        ),
        check_vma=False,
    )
```

```python
import functools
import math

import jax
import jax.numpy as jnp
from jax import lax
from jax.experimental import pallas as pl
from jax.experimental.pallas import tpu as pltpu
from jax.sharding import PartitionSpec as P

EPSILON = 1e-05
NEGATIVE = -1e30
LOG2E = 1.4426950408889634
LN2 = 0.6931471805599453
NT = (((1,), (1,)), ((), ()))
NN = (((1,), (0,)), ((), ()))
TN = (((0,), (0,)), ((), ()))
MIB = 2**20


def mm(a, b, dims=NN):
    return lax.dot_general(a, b, dims, preferred_element_type=jnp.float32)


def file_start(lengths, pos):
    end, start = 0, jnp.zeros_like(pos)
    for i in range(lengths.shape[0]):
        end = end + lengths[i]
        start = jnp.where(pos >= end, end, start)
    return start


def key_ids(pad, j, keys):
    pos = j * keys + lax.broadcasted_iota(jnp.int32, (1, keys), 1)
    return jnp.where(pad[pl.ds(pl.multiple_of(j * keys, keys), keys)].reshape(1, -1) == 1, pos, -1)


def as_column(row):
    return jnp.transpose(jnp.broadcast_to(row, (128, row.shape[1])))[:, :1]


def attend_kernel(rows, keys, heads, size, len_ref, q_ref, kv_ref, pad_ref, o_ref, low_ref, lse_ref):
    scale2 = LOG2E / math.sqrt(size)
    base = (lax.axis_index("cp") * pl.num_programs(0) + pl.program_id(0)) * rows
    row_pos = base + lax.broadcasted_iota(jnp.int32, (rows, 1), 0)
    row_start = as_column(file_start(len_ref, base + lax.broadcasted_iota(jnp.int32, (1, rows), 1)))
    ones = jnp.ones((keys, size), jnp.bfloat16)

    def block(j, carry, diagonal):
        here = pl.ds(pl.multiple_of(j * keys, keys), keys)
        k = kv_ref[here, :size]
        v1 = jnp.concatenate([kv_ref[here, size:], ones], axis=1)
        kid = key_ids(pad_ref, j, keys)
        ok = kid >= row_start
        if diagonal:
            col = j * keys + lax.broadcasted_iota(jnp.int32, (1, keys), 1)
            ok = (ok & (kid <= row_pos)) | (col == row_pos)
        out = []
        for h in range(heads):
            top, acc = carry[h]
            s = jnp.where(ok, mm(q_ref[:, h * size : (h + 1) * size], k, NT) * scale2, NEGATIVE)
            new = jnp.maximum(top, jnp.max(s, axis=1, keepdims=True))
            w = jnp.exp2(s - new).astype(jnp.bfloat16)
            out.append((new, acc * jnp.exp2(top - new) + mm(w, v1)))
        return tuple(out)

    carry = tuple(
        (jnp.full((rows, 1), NEGATIVE, jnp.float32), jnp.zeros((rows, 2 * size), jnp.float32))
        for _ in range(heads)
    )
    full = base // keys
    carry = lax.fori_loop(file_start(len_ref, base) // keys, full, lambda j, c: block(j, c, False), carry)
    last = (base + rows + keys - 1) // keys
    carry = lax.fori_loop(full, last, lambda j, c: block(j, c, True), carry)
    for h in range(heads):
        top, acc = carry[h]
        total = acc[:, size:]
        out = acc[:, :size] / total
        o_ref[:, h * size : (h + 1) * size] = out
        low_ref[:, h * size : (h + 1) * size] = out.astype(jnp.bfloat16)
        lse_ref[h : h + 1, :] = jnp.transpose(top + jnp.log2(total))[0:1]


def attend(q, kv, lengths, pad, rows=512, keys=512):
    total, wide = q.shape
    size = kv.shape[1] // 2
    heads = wide // size
    by_row = pl.BlockSpec((rows, wide), lambda i, f: (i, 0))
    return pl.pallas_call(
        functools.partial(attend_kernel, rows, keys, heads, size),
        out_shape=(
            jax.ShapeDtypeStruct((total, wide), jnp.float32),
            jax.ShapeDtypeStruct((total, wide), jnp.bfloat16),
            jax.ShapeDtypeStruct((heads, total), jnp.float32),
        ),
        grid_spec=pltpu.PrefetchScalarGridSpec(
            num_scalar_prefetch=1,
            grid=(total // rows,),
            in_specs=[
                by_row,
                pl.BlockSpec(kv.shape, lambda i, f: (0, 0)),
                pl.BlockSpec(pad.shape, lambda i, f: (0,)),
            ],
            out_specs=[by_row, by_row, pl.BlockSpec((heads, rows), lambda i, f: (0, i))],
        ),
        compiler_params=pltpu.CompilerParams(vmem_limit_bytes=61 * MIB),
        name="attend",
    )(lengths, q, kv, pad)


def attend_back_kernel(
    rows, keys, heads, size, len_ref, q_ref, do_ref, o_ref, lse_ref, kv_ref, pad_ref, block_h, down_h, in_h,
    dq_ref, dkv_ref, block_o, down_o, acc_ref, block_v, down_v, in_v, pass_s,
):
    i = pl.program_id(0)
    scale = 1.0 / math.sqrt(size)
    base = (lax.axis_index("cp") * pl.num_programs(0) + i) * rows
    row_pos = base + lax.broadcasted_iota(jnp.int32, (1, rows), 1)
    row_start = file_start(len_ref, row_pos)
    fetched = [
        pltpu.make_async_copy(src, dst, pass_s.at[k])
        for k, (src, dst) in enumerate(((block_h, block_v), (down_h, down_v), (in_h, in_v)))
    ]
    passed = [
        pltpu.make_async_copy(block_v, block_o, pass_s.at[3]),
        pltpu.make_async_copy(down_v, down_o, pass_s.at[4]),
    ]

    @pl.when(i == 0)
    def _():
        for copy in fetched:
            copy.start()
        acc_ref[...] = jnp.zeros_like(acc_ref)

    @pl.when(i == pl.num_programs(0) - 1)
    def _():
        for copy in fetched:
            copy.wait()
        passed[0].start()

        @pl.loop(0, 8)
        def _(j):
            r = chunk_rows(j, down_v.shape[0] // 8)
            total = down_v[r, :]
            for k in range(in_v.shape[0]):
                total += in_v[k, r, :].astype(jnp.float32)
            down_v[r, :] = total

        passed[1].start()

    deltas = []
    for h in range(heads):
        cols = slice(h * size, (h + 1) * size)
        both = do_ref[:, cols].astype(jnp.float32) * o_ref[:, cols]
        deltas.append(jnp.sum(jnp.transpose(both), axis=0, keepdims=True))

    def block(j, carry, diagonal):
        here = pl.ds(pl.multiple_of(j * keys, keys), keys)
        k = kv_ref[here, :size]
        v = kv_ref[here, size:]
        kid = as_column(key_ids(pad_ref, j, keys))
        ok = kid >= row_start
        if diagonal:
            col = j * keys + lax.broadcasted_iota(jnp.int32, (keys, 1), 0)
            ok = (ok & (kid <= row_pos)) | (col == row_pos)
        out = []
        dk = acc_ref[here, :size]
        dv = acc_ref[here, size:]
        for h in range(heads):
            cols = slice(h * size, (h + 1) * size)
            q = q_ref[:, cols]
            do = do_ref[:, cols]
            s = mm(k, q, NT) * (scale * LOG2E) - lse_ref[h : h + 1, :]
            p = jnp.where(ok, jnp.exp2(s), 0.0)
            ds = (p * (mm(v, do, NT) - deltas[h])).astype(jnp.bfloat16)
            dv = dv + mm(p.astype(jnp.bfloat16), do)
            dk = dk + mm(ds, q)
            out.append(carry[h] + mm(ds, k, TN))
        acc_ref[here, :size] = dk
        acc_ref[here, size:] = dv
        return tuple(out)

    carry = tuple(jnp.zeros((rows, size), jnp.float32) for _ in range(heads))
    full = base // keys
    carry = lax.fori_loop(file_start(len_ref, base) // keys, full, lambda j, c: block(j, c, False), carry)
    last = (base + rows + keys - 1) // keys
    carry = lax.fori_loop(full, last, lambda j, c: block(j, c, True), carry)
    for h in range(heads):
        dq_ref[:, h * size : (h + 1) * size] = (carry[h] * scale).astype(dq_ref.dtype)

    @pl.when(i == pl.num_programs(0) - 1)
    def _():
        dkv_ref[:, :size] = (acc_ref[:, :size] * scale).astype(dkv_ref.dtype)
        dkv_ref[:, size:] = acc_ref[:, size:].astype(dkv_ref.dtype)
        for copy in passed:
            copy.wait()


def attend_back(q, do, o, lse, kv, lengths, pad, block, down, down_in, rows=512, keys=512):
    total, wide = q.shape
    size = kv.shape[1] // 2
    heads = wide // size
    by_row = pl.BlockSpec((rows, wide), lambda i, f: (i, 0))
    whole = pl.BlockSpec(kv.shape, lambda i, f: (0, 0))
    far = pl.BlockSpec(memory_space=pl.ANY)
    return pl.pallas_call(
        functools.partial(attend_back_kernel, rows, keys, heads, size),
        out_shape=(
            jax.ShapeDtypeStruct((total, wide), jnp.bfloat16),
            jax.ShapeDtypeStruct(kv.shape, jnp.bfloat16),
            jax.ShapeDtypeStruct(block.shape, block.dtype),
            jax.ShapeDtypeStruct(down.shape, down.dtype),
        ),
        grid_spec=pltpu.PrefetchScalarGridSpec(
            num_scalar_prefetch=1,
            grid=(total // rows,),
            in_specs=[
                by_row,
                by_row,
                by_row,
                pl.BlockSpec((heads, rows), lambda i, f: (0, i)),
                whole,
                pl.BlockSpec(pad.shape, lambda i, f: (0,)),
                far,
                far,
                far,
            ],
            out_specs=[by_row, whole, far, far],
            scratch_shapes=[
                pltpu.VMEM(kv.shape, jnp.float32),
                pltpu.VMEM(block.shape, block.dtype),
                pltpu.VMEM(down.shape, down.dtype),
                pltpu.VMEM(down_in.shape, down_in.dtype),
                pltpu.SemaphoreType.DMA((5,)),
            ],
        ),
        compiler_params=pltpu.CompilerParams(vmem_limit_bytes=61 * MIB),
        name="attend_back",
    )(lengths, q, do, o, lse, kv, pad, block, down, down_in)


def emit_kernel(
    heads_wide, low, own, up, up_in, out, out_in, sums, tokens_o, q_o, k_o, v_o, up_o, out_o, *vectors
):
    total = up[...].astype(jnp.float32)
    for i in range(up_in.shape[0]):
        total += up_in[i].astype(jnp.float32)
    up_o[...] = total
    tokens_o[...] = low[...].astype(jnp.float32)
    size = k_o.shape[1]
    q_o[...] = own[:, :heads_wide]
    k_o[...] = own[:, heads_wide : heads_wide + size]
    v_o[...] = own[:, heads_wide + size :]
    total = out[...]
    for i in range(out_in.shape[0]):
        total += out_in[i].astype(jnp.float32)
    out_o[...] = total

    @pl.when(pl.program_id(0) == 0)
    def _():
        for i in range(6):
            vectors[i][...] = sums[i : i + 1, :].reshape(-1)
        at = 0
        for ref in vectors[6:]:
            ref[...] = sums[6:7, at : at + ref.shape[0]].reshape(-1)
            at += ref.shape[0]


def emit(low, own, up, up_in, out, out_in, sums, heads_wide, steps=4):
    size = (own.shape[1] - heads_wide) // 2
    wide, hidden = low.shape[1], up.shape[1]
    f32 = jnp.float32

    def rows_of(shape):
        if len(shape) == 3:
            return pl.BlockSpec((shape[0], shape[1] // steps, shape[2]), lambda i: (0, i, 0))
        return pl.BlockSpec((shape[0] // steps, shape[1]), lambda i: (i, 0))

    lengths = (wide,) * 6 + (hidden, heads_wide, size)
    per = own.shape[0]
    shapes = (low.shape, (per, heads_wide), (per, size), (per, size), up.shape, out.shape)
    blocks = (low, own, up, up_in, out, out_in)
    return pl.pallas_call(
        functools.partial(emit_kernel, heads_wide),
        out_shape=tuple(jax.ShapeDtypeStruct(x, f32) for x in (*shapes, *((n,) for n in lengths))),
        grid=(steps,),
        in_specs=[*(rows_of(x.shape) for x in blocks), pl.BlockSpec(sums.shape, lambda i: (0, 0))],
        out_specs=(*(rows_of(x) for x in shapes), *(pl.BlockSpec((n,), lambda i: (0,)) for n in lengths)),
        compiler_params=pltpu.CompilerParams(vmem_limit_bytes=61 * MIB),
        name="emit",
    )(*blocks, sums)


def as_row(ref):
    return ref[...].astype(jnp.float32).reshape(1, -1)


MESH = pl.DeviceIdType.MESH


class Chain:
    def __init__(self, chunks, quarter, part, out, mate, in0, in1, tmp, sems, hop=1):
        tp = lax.axis_index("tp")
        self.n = lax.axis_size("tp") // 2
        self.p, self.c = tp // 2, tp % 2
        self.chunks, self.q = chunks, quarter
        self.part, self.out, self.mate, self.in0, self.in1, self.tmp = part, out, mate, in0, in1, tmp
        (self.mate_s, self.mate_r, self.ch_s, self.in0_r, self.in1_r, self.bl_s, self.br_s, self.bc_r, self.fin_s, self.fin_r) = sems
        self.roots = (self.n // 2 - 1, self.n // 2)
        self.hop = hop
        self.reach = hop * max(self.roots[0], self.n - 1 - self.roots[0])

    @staticmethod
    def sems(chunks):
        one, two = pltpu.SemaphoreType.DMA((chunks,)), pltpu.SemaphoreType.DMA((chunks, 2))
        return [one, one, two, two, one, two, two, two, two, two]

    def at(self, p, c):
        return {"tp": p * 2 + c}

    def rows(self, g, c, part):
        q = self.q
        return pl.ds(pl.multiple_of(g * (4 * q) + c * (2 * q) + part * q, q), q)

    def own(self, g, part):
        q = self.q
        return pl.ds(pl.multiple_of(g * (2 * q) + part * q, q), q)

    def copy(self, src, dst, s, r, p, c):
        return pltpu.make_async_remote_copy(src, dst, s, r, device_id=self.at(p, c), device_id_type=MESH)

    def mate_copy(self, g):
        q = self.q
        src = self.part.at[pl.ds(pl.multiple_of(g * (4 * q) + (1 - self.c) * (2 * q), 2 * q), 2 * q)]
        dst = self.mate.at[pl.ds(pl.multiple_of(g * (2 * q), 2 * q), 2 * q)]
        return self.copy(src, dst, self.mate_s.at[g], self.mate_r.at[g], self.p, 1 - self.c)

    def in_copy(self, g, k, to):
        return self.copy(self.part.at[self.rows(g, self.c, k)], self.in0.at[self.own(g, k)], self.ch_s.at[g, k], self.in0_r.at[g, k], to, self.c)

    def in1_copy(self, g, k, to):
        q = self.q
        dst = self.in1.at[pl.ds(pl.multiple_of(g * q, q), q)]
        return self.copy(self.part.at[self.rows(g, self.c, k)], dst, self.ch_s.at[g, k], self.in1_r.at[g], to, self.c)

    def out_copy(self, g, k, to, sem):
        here = self.out.at[self.rows(g, self.c, k)]
        return self.copy(here, here, sem.at[g, k], self.bc_r.at[g, k], to, self.c)

    def fin_copy(self, g, k):
        here = self.out.at[self.rows(g, self.c, k)]
        return self.copy(here, here, self.fin_s.at[g, k], self.fin_r.at[g, k], self.p, 1 - self.c)

    def lag_up(self, k):
        root = self.roots[k]
        return jnp.where(
            self.p == root, self.reach, self.hop * jnp.where(self.p < root, self.p, self.n - 1 - self.p)
        )

    def lag_down(self, k):
        return self.reach + self.hop * jnp.abs(self.p - self.roots[k])

    def start_mate(self, g):
        self.mate_copy(g).start()

    def reduce(self, g, k):
        root, p, n, q = self.roots[k], self.p, self.n, self.q
        rows, own, tmp = self.rows(g, self.c, k), self.own(g, k), self.tmp
        if self.mate is None:
            tmp[...] = self.part[rows, :].astype(jnp.float32)
        else:
            tmp[...] = self.part[rows, :].astype(jnp.float32) + self.mate[own, :].astype(jnp.float32)

        @pl.when(((p > 0) & (p <= root)) | ((p > root) & (p < n - 1)))
        def _():
            self.in_copy(g, k, p).wait_recv()
            tmp[...] += self.in0[own, :].astype(jnp.float32)

        @pl.when((p == root) & (p < n - 1))
        def _():
            self.in1_copy(g, k, p).wait_recv()
            tmp[...] += self.in1[pl.ds(pl.multiple_of(g * q, q), q), :].astype(jnp.float32)

        @pl.when(p != root)
        def _():
            self.part[rows, :] = tmp[...].astype(jnp.bfloat16)

        @pl.when(p < root)
        def _():
            self.in_copy(g, k, p + 1).start()

        @pl.when(p > root + 1)
        def _():
            self.in_copy(g, k, p - 1).start()

        @pl.when(p == root + 1)
        def _():
            self.in1_copy(g, k, p - 1).start()

        @pl.when(p == root)
        def _():
            self.out[rows, :] = tmp[...].astype(jnp.bfloat16)
            self.spread(g, k)

    def spread(self, g, k):
        root, p, n = self.roots[k], self.p, self.n

        @pl.when((p <= root) & (p > 0))
        def _():
            self.out_copy(g, k, p - 1, self.bl_s).start()

        @pl.when((p >= root) & (p < n - 1))
        def _():
            self.out_copy(g, k, p + 1, self.br_s).start()

        self.fin_copy(g, k).start()

    def down(self, g, k):
        @pl.when(self.p != self.roots[k])
        def _():
            self.out_copy(g, k, self.p, self.bl_s).wait_recv()
            self.spread(g, k)

    def done(self, g):
        for k in range(2):
            self.fin_copy(g, k).wait_recv()

    def drain(self, g):
        p, n = self.p, self.n
        if self.mate is not None:
            self.mate_copy(g).wait_send()
        for k, root in enumerate(self.roots):

            @pl.when(p != root)
            def _():
                self.in_copy(g, k, p).wait_send()

            @pl.when((p <= root) & (p > 0))
            def _():
                self.out_copy(g, k, p, self.bl_s).wait_send()

            @pl.when((p >= root) & (p < n - 1))
            def _():
                self.out_copy(g, k, p, self.br_s).wait_send()

            self.fin_copy(g, k).wait_send()


def within(g, chunks):
    return (g >= 0) & (g < chunks)


def chunk_rows(g, rows):
    return pl.ds(pl.multiple_of(g * rows, rows), rows)


def norm_parts(values):
    centre = jnp.mean(values, axis=1, keepdims=True)
    centred = values - centre
    inv = lax.rsqrt(jnp.mean(centred * centred, axis=1, keepdims=True) + EPSILON)
    return centred * inv, inv


def norm_back(grad, unit, inv, gain):
    e = grad * gain
    return inv * (
        e - jnp.mean(e, axis=1, keepdims=True) - unit * jnp.mean(e * unit, axis=1, keepdims=True)
    )


def greet(chips, peers):
    tp, me = lax.axis_index("tp"), lax.axis_index("cp")
    n, groups = lax.axis_size("tp") // 2, lax.axis_size("cp")
    p, c = tp // 2, tp % 2
    bar = pltpu.get_barrier_semaphore()
    count = 1
    pl.semaphore_signal(bar, 1, device_id={"tp": p * 2 + 1 - c}, device_id_type=MESH)
    if chips:

        @pl.when(p > 0)
        def _():
            pl.semaphore_signal(bar, 1, device_id={"tp": tp - 2}, device_id_type=MESH)

        @pl.when(p < n - 1)
        def _():
            pl.semaphore_signal(bar, 1, device_id={"tp": tp + 2}, device_id_type=MESH)

        count += (p > 0).astype(jnp.int32) + (p < n - 1).astype(jnp.int32)
    if peers:
        for i in range(1, groups):
            pl.semaphore_signal(bar, 1, device_id={"cp": lax.rem(me + i, groups)}, device_id_type=MESH)
        count += groups - 1
    return lambda: pl.semaphore_wait(bar, count)


def cp_copy(i, src, dst, send, recv):
    to = lax.rem(lax.axis_index("cp") + i + 1, lax.axis_size("cp"))
    return pltpu.make_async_remote_copy(
        src, dst, send.at[i], recv.at[i], device_id={"cp": to}, device_id_type=MESH
    )


SLACK = 0
HOP = 1


def middle_kernel(
    chunks,
    attn_h, wo_h, gain_v, bias_v, ob_v, db_v, ub_v, tok_h, cot_h, wu_h, wd_h,
    out_h, gmix_h, gattn, down_own, down_in, up_own_h, up_h, outw_h, out_own, sums, usum,
    attn, wo, tok, cot, wu, wd, hid, h2, gup, pa, pc, pb, out1, out2, out3, mate, in0, in1, tmp,
    load_s, save_s, gm_s, up_o, ow_s, dn_s, dn_r,
    *sems,
):
    rows = tok.shape[0] // chunks
    groups, me = lax.axis_size("cp"), lax.axis_index("cp")
    wide = tok.shape[1]
    per = wide // groups
    bf = jnp.bfloat16
    third = len(sems) // 3
    ch1 = Chain(chunks, rows // 4, pa, out1, mate, in0, in1, tmp, sems[:third], HOP)
    ch3 = Chain(chunks, rows // 4, pc, out3, mate, in0, in1, tmp, sems[third : 2 * third], HOP)
    ch2 = Chain(chunks, rows // 4, pb, out2, mate, in0, in1, tmp, sems[2 * third :], HOP)
    first = (lax.axis_index("tp") == 0).astype(jnp.float32)
    loads = [
        pltpu.make_async_copy(src, dst, load_s.at[i])
        for i, (src, dst) in enumerate(
            ((attn_h, attn), (wo_h, wo), (tok_h, tok), (wu_h, wu), (wd_h, wd), (cot_h, cot))
        )
    ]
    for load in loads:
        load.start()
    greet(True, True)()
    gain, bias, out_bias, down_bias, up_bias = (as_row(x) for x in (gain_v, bias_v, ob_v, db_v, ub_v))
    sums[...] = jnp.zeros_like(sums)
    usum[...] = jnp.zeros_like(usum)

    def project(g):
        r = chunk_rows(g, rows)
        pa[r, :] = mm(attn[r, :], wo[...]).astype(bf)
        ch1.start_mate(g)

    def halves(g):
        return [chunk_rows(2 * g + i, rows // 2) for i in range(2)]

    def middle_of(r):
        return tok[r, :].astype(jnp.float32) + out1[r, :].astype(jnp.float32) + out_bias

    def feed(g):
        r = chunk_rows(g, rows)
        ch1.done(g)
        for part in halves(g):
            unit, _ = norm_parts(middle_of(part))
            h2[part, :] = (unit * gain + bias).astype(bf)
        up = mm(h2[r, :], wu[...]) + up_bias
        sq = up * up
        t = jnp.tanh(0.7978845608028654 * up * (1.0 + 0.044715 * sq))
        half = 0.5 * (1.0 + t)
        hid[r, :] = (half * up).astype(bf)
        slope = half + 0.5 * up * (1.0 - t * t) * (0.7978845608028654 * (1.0 + 3.0 * 0.044715 * sq))
        gu = (slope * mm(cot[r, :], wd[...], NT)).astype(bf)
        gup[r, :] = gu
        usum[...] += jnp.sum(gu.astype(jnp.float32), axis=0, keepdims=True)
        sums[0:1, :] += jnp.sum(cot[r, :].astype(jnp.float32), axis=0, keepdims=True)
        pc[r, :] = mm(gup[r, :], wu[...], NT).astype(bf)
        ch3.start_mate(g)
        for part in halves(g):
            base = first * (middle_of(part) + down_bias)
            pb[part, :] = (mm(hid[part, :], wd[...]) + base).astype(bf)

    def back(g):
        r = chunk_rows(g, rows)
        ch3.done(g)
        ch1.drain(g)
        for part in halves(g):
            unit, inv = norm_parts(middle_of(part))
            grad = out3[part, :].astype(jnp.float32)
            sums[1:2, :] += jnp.sum(grad * unit, axis=0, keepdims=True)
            sums[2:3, :] += jnp.sum(grad, axis=0, keepdims=True)
            gm = (cot[part, :].astype(jnp.float32) + norm_back(grad, unit, inv, gain)).astype(bf)
            sums[3:4, :] += jnp.sum(gm.astype(jnp.float32), axis=0, keepdims=True)
            pa[part, :] = gm
        pltpu.make_async_copy(pa.at[r], gmix_h.at[r], gm_s.at[g]).start()
        gattn[r, :] = mm(pa[r, :], wo[...], NT).astype(bf)
        ch2.start_mate(g)

    def finish(g):
        r = chunk_rows(g, rows)
        ch2.done(g)
        pltpu.make_async_copy(out2.at[r], out_h.at[r], save_s.at[g]).start()

    def down_copy(i):
        to = lax.rem(me + i + 1, groups)
        cols = pl.ds(pl.multiple_of(to * per, per), per)
        return cp_copy(i, wd.at[:, cols], down_in.at[i], dn_s, dn_r)

    def down_block(i):
        cols = pl.ds(pl.multiple_of(lax.rem(me + i + 1, groups) * per, per), per)
        half = hid.shape[1] // 2
        for j in range(2):
            part = mm(hid[:, j * half : (j + 1) * half], cot[:, cols], TN)

            @pl.when(i < groups - 1)
            def _():
                wd[j * half : (j + 1) * half, cols] = part.astype(bf)

            @pl.when(i == groups - 1)
            def _():
                down_own[j * half : (j + 1) * half, :] = part

        pl.when(i < groups - 1)(lambda: down_copy(i).start())

    def up_rows(i):
        return chunk_rows(lax.rem(me + i + 1, groups), per)

    def up_save(i):
        return pltpu.make_async_copy(wu.at[up_rows(i)], up_h.at[up_rows(i)], up_o.at[i])

    up_keep = pltpu.make_async_copy(wu.at[chunk_rows(me, per)], up_own_h, up_o.at[groups - 1])

    def up_block(i):
        for k in range(2):
            r = chunk_rows(2 * lax.rem(me + i + 1, groups) + k, per // 2)
            wu[r, :] = mm(h2[:, r], gup[...], TN).astype(bf)
        pl.when(i < groups - 1)(lambda: up_save(i).start())
        pl.when(i == groups - 1)(lambda: up_keep.start())

    def serve(ch, s):
        for k in range(2):
            g = s - ch.lag_up(k)
            pl.when(within(g, chunks))(functools.partial(ch.reduce, g, k))
        for k in range(2):
            g = s - ch.lag_down(k) - SLACK
            pl.when(within(g, chunks))(functools.partial(ch.down, g, k))

    def due(ch, s):
        pl.when(within(s, chunks))(lambda: ch.mate_copy(s).wait_recv())

    turn = 2 * ch1.reach + SLACK
    for load in loads[:2]:
        load.wait()
    project(0)
    project(1)

    @pl.loop(0, chunks + max(3 * turn, turn + 2 * groups))
    def _(s):
        pl.when(s + 2 < chunks)(lambda: project(s + 2))
        due(ch1, s)
        serve(ch1, s)

        @pl.when(s == turn)
        def _():
            for load in loads[2:]:
                load.wait()

        g = s - turn
        pl.when(within(g, chunks))(functools.partial(feed, g))
        due(ch3, g)
        serve(ch3, g)
        g = s - 2 * turn
        pl.when(within(g, chunks))(functools.partial(back, g))
        i = s - turn - chunks
        pl.when(within(i, groups))(functools.partial(down_block, i))
        due(ch2, g)
        serve(ch2, g)
        j = i - groups
        pl.when(within(j, groups))(functools.partial(up_block, j))
        g = s - 3 * turn
        pl.when(within(g, chunks))(functools.partial(finish, g))

    for j in range(4):
        cols = slice(j * (wide // 4), (j + 1) * (wide // 4))
        mate[0 : attn.shape[1], cols] = mm(attn[...], pa[:, cols], TN).astype(bf)
    out_save = pltpu.make_async_copy(mate.at[pl.ds(0, attn.shape[1])], outw_h, ow_s)
    out_save.start()
    out_own[...] = mate[0 : attn.shape[1], pl.ds(pl.multiple_of(me * per, per), per)].astype(jnp.float32)

    @pl.loop(0, groups - 1)
    def _(i):
        down_copy(i).wait()

    @pl.loop(0, chunks)
    def _(g):
        r = chunk_rows(g, rows)
        pltpu.make_async_copy(pa.at[r], gmix_h.at[r], gm_s.at[g]).wait()
        pltpu.make_async_copy(out2.at[r], out_h.at[r], save_s.at[g]).wait()
        ch3.drain(g)
        ch2.drain(g)

    for i in range(groups - 1):
        up_save(i).wait()
    up_keep.wait()
    out_save.wait()


def middle(attn, tokens, cotangent, wo, wu, wd, vectors, groups, chunks=8):
    rows, wide = tokens.shape
    heads_wide, hidden = wo.shape[0], wu.shape[1]
    bf, f32 = jnp.bfloat16, jnp.float32
    sds, vm = jax.ShapeDtypeStruct, pltpu.VMEM
    v, a = pl.BlockSpec(memory_space=pltpu.VMEM), pl.BlockSpec(memory_space=pl.ANY)
    dma = pltpu.SemaphoreType.DMA
    return pl.pallas_call(
        functools.partial(middle_kernel, chunks),
        out_shape=(
            sds((rows, wide), bf),
            sds((rows, wide), bf),
            sds((rows, heads_wide), bf),
            sds((hidden, wide // groups), f32),
            sds((groups - 1, hidden, wide // groups), bf),
            sds((wide // groups, hidden), bf),
            sds((wide, hidden), bf),
            sds((heads_wide, wide), bf),
            sds((heads_wide, wide // groups), f32),
            sds((8, wide), f32),
            sds((1, hidden), f32),
        ),
        in_specs=[a] * 2 + [v] * 5 + [a] * 4,
        out_specs=(a, a, v, v, a, a, a, a, v, v, v),
        scratch_shapes=[
            vm(attn.shape, bf), vm(wo.shape, bf),
            vm((rows, wide), bf), vm((rows, wide), bf), vm((wide, hidden), bf), vm((hidden, wide), bf),
            vm((rows, hidden), bf), vm((rows, wide), bf), vm((rows, hidden), bf),
            *[vm((rows, wide), bf)] * 6,
            vm((rows // 2, wide), bf), vm((rows // 2, wide), bf), vm((rows // 4, wide), bf),
            vm((rows // (4 * chunks), wide), f32),
            dma((6,)), dma((chunks,)), dma((chunks,)), dma((groups,)), dma, dma((groups - 1,)), dma((groups - 1,)),
            *Chain.sems(chunks), *Chain.sems(chunks), *Chain.sems(chunks),
        ],
        compiler_params=pltpu.CompilerParams(
            collective_id=2, has_side_effects=True, vmem_limit_bytes=61 * MIB
        ),
        name="middle",
    )(attn, wo, *vectors, tokens, cotangent, wu, wd)


HEAD_PARTS = 8


def head_kernel(
    gain_v, bias_v, qb_v, vb_v, tok_h, wq_h, wk_h, wv_h, q, kv, tok, h1, wq, wkv, load_s, w_s, x_s, x_r, f_s, f_r
):
    local = tok.shape[0]
    rows = local // HEAD_PARTS
    mine = HEAD_PARTS // 2
    groups, me = lax.axis_size("cp"), lax.axis_index("cp")
    tp = lax.axis_index("tp")
    core = tp % 2
    bf = jnp.bfloat16

    def load(part):
        r = chunk_rows(part, rows)
        return pltpu.make_async_copy(tok_h.at[r], tok.at[r], load_s.at[part])

    def part_at(i):
        return lax.rem(mine * core + i, HEAD_PARTS)

    def block(source, part):
        return pl.ds(pl.multiple_of(source * local + part * rows, rows), rows)

    def spread(j, i):
        here = kv.at[block(me, part_at(i))]
        to = lax.rem(me + j + 1, groups)
        return pltpu.make_async_remote_copy(
            here, here, x_s.at[j, i], x_r.at[j, i], device_id={"cp": to}, device_id_type=MESH
        )

    def forward(j, i):
        here = kv.at[block(lax.rem(me - j - 1 + groups, groups), part_at(i))]
        return pltpu.make_async_remote_copy(
            here, here, f_s.at[j, i], f_r.at[j, i], device_id={"tp": tp + 1 - 2 * core}, device_id_type=MESH
        )

    size = wk_h.shape[1]
    weights = [
        pltpu.make_async_copy(wk_h, wkv.at[:, pl.ds(0, size)], w_s.at[0]),
        pltpu.make_async_copy(wv_h, wkv.at[:, pl.ds(size, size)], w_s.at[1]),
        pltpu.make_async_copy(wq_h, wq, w_s.at[2]),
    ]
    load(part_at(0)).start()
    weights[0].start()
    weights[1].start()
    for i in range(1, HEAD_PARTS):
        load(part_at(i)).start()
    weights[2].start()
    greeted = greet(False, True)
    gain, bias, q_bias, v_bias = (as_row(x) for x in (gain_v, bias_v, qb_v, vb_v))
    kv_bias = jnp.concatenate([jnp.zeros_like(v_bias), v_bias], axis=1)
    for i in range(HEAD_PARTS):
        load(part_at(i)).wait()
        r = chunk_rows(part_at(i), rows)
        unit, _ = norm_parts(tok[r, :].astype(jnp.float32))
        h1[r, :] = (unit * gain + bias).astype(bf)
        if i == 0:
            weights[0].wait()
            weights[1].wait()
        kv[block(me, part_at(i)), :] = (mm(h1[r, :], wkv[...]) + kv_bias).astype(bf)
        if i == 0:
            greeted()
        if i < mine:
            for j in range(groups - 1):
                spread(j, i).start()
    weights[2].wait()
    for i in range(HEAD_PARTS):
        r = chunk_rows(part_at(i), rows)
        q[r, :] = (mm(h1[r, :], wq[...]) + q_bias).astype(bf)
    for i in range(mine):
        for j in range(groups - 1):
            spread(j, i).wait_recv()
            forward(j, i).start()
    for i in range(mine):
        for j in range(groups - 1):
            forward(j, i).wait()
            spread(j, i).wait_send()


def head(tokens, wq, wk, wv, vectors, groups):
    rows, wide = tokens.shape
    bf = jnp.bfloat16
    sds, vm = jax.ShapeDtypeStruct, pltpu.VMEM
    v, a = pl.BlockSpec(memory_space=pltpu.VMEM), pl.BlockSpec(memory_space=pl.ANY)
    dma, two = pltpu.SemaphoreType.DMA, 2 * wk.shape[1]
    pairs = dma((groups - 1, HEAD_PARTS // 2))
    return pl.pallas_call(
        head_kernel,
        out_shape=(sds((rows, wq.shape[1]), bf), sds((groups * rows, two), bf)),
        in_specs=[v] * 4 + [a] * 4,
        out_specs=(v, v),
        scratch_shapes=[
            vm((rows, wide), bf), vm((rows, wide), bf), vm(wq.shape, bf), vm((wide, two), bf),
            dma((HEAD_PARTS,)), dma((3,)), pairs, pairs, pairs, pairs,
        ],
        compiler_params=pltpu.CompilerParams(
            collective_id=1, has_side_effects=True, vmem_limit_bytes=61 * MIB
        ),
        name="head",
    )(*vectors, tokens, wq, wk, wv)


KV_STEP = 2
TAIL_HOP = 1


def tail_kernel(
    chunks,
    gq_h, dkv_h, wq_h, wk_h, wv_h, gain_v, bias_v, sums, usum, tok_h, gmix_h, outw_h, up_h,
    tgrad_h, out_in, up_in, own, vout,
    gq, dkv, wq, wkv, tok, gmix, h1, pa, out1, mate, in0, in1, tmp, kvm, kvs, kv_in, pkv, okv, kin0, kin1, ktmp,
    stage, w_in, acc, v_in,
    load_s, save_s, o_s, o_r, u_s, u_r, km_s, km_r, kx_s, kx_r, w_s, w_r, v_s, v_r,
    *sems,
):
    local, wide = tok.shape
    rows = local // chunks
    groups, me = lax.axis_size("cp"), lax.axis_index("cp")
    core = lax.axis_index("tp") % 2
    tp = lax.axis_index("tp")
    per = wide // groups
    heads_wide, size = gq.shape[1], wk_h.shape[1]
    bf = jnp.bfloat16
    half_sems = len(sems) // 2
    ch1 = Chain(chunks, rows // 4, pa, out1, mate, in0, in1, tmp, sems[:half_sems], TAIL_HOP)
    chk = Chain(1, local // 4, pkv, okv, None, kin0, kin1, ktmp, sems[half_sems:])
    loads = [
        pltpu.make_async_copy(src, dst, load_s.at[i])
        for i, (src, dst) in enumerate(
            (
                (gq_h, gq), (wq_h, wq), (dkv_h, dkv), (tok_h, tok), (gmix_h, gmix),
                (wk_h, wkv.at[:, pl.ds(0, size)]), (wv_h, wkv.at[:, pl.ds(size, size)]),
            )
        )
    ]
    for load in loads:
        load.start()
    greet(True, True)()
    own_half = chunk_rows(core, local // 2)
    kv_mate = pltpu.make_async_remote_copy(
        dkv_h.at[:, chunk_rows(1 - core, local // 2), :], kvm, km_s, km_r,
        device_id={"tp": tp + 1 - 2 * core}, device_id_type=MESH,
    )
    kv_mate.start()
    gain, bias = as_row(gain_v), as_row(bias_v)

    def project(g):
        r = chunk_rows(g, rows)
        pa[r, :] = mm(gq[r, :], wq[...], NT).astype(bf)
        ch1.start_mate(g)

    for load in loads[:2]:
        load.wait()
    project(0)
    project(1)
    acc[...] = sums[...]

    def kv_copy(i):
        to = lax.rem(me + i + 1, groups)
        return cp_copy(i, kvs.at[to], kv_in.at[i], kx_s, kx_r)

    def kv_send():
        kv_mate.wait_recv()

        @pl.loop(0, groups)
        def _(i):
            to = lax.rem(me + i + 1, groups)
            both = dkv[to, own_half, :].astype(jnp.float32) + kvm[to].astype(jnp.float32)
            kvs[to] = both.astype(bf)
            pl.when(i < groups - 1)(lambda: kv_copy(i).start())

        for i in range(groups - 1):
            out_copy(i).start()
        for i in range(groups - 1):
            up_copy(i).start()

    def normed(g):
        r = chunk_rows(g, rows)
        unit, _ = norm_parts(tok[r, :].astype(jnp.float32))
        h1[r, :] = (unit * gain + bias).astype(bf)

    def kv_gather():
        total = kvs[me].astype(jnp.float32)
        for i in range(groups - 1):
            kv_copy(i).wait_recv()
            total += kv_in[i].astype(jnp.float32)
        pkv[own_half, :] = total.astype(bf)

    def serve(ch, s, count, slack):
        for k in range(2):
            g = s - ch.lag_up(k)
            pl.when(within(g, count))(functools.partial(ch.reduce, g, k))
        for k in range(2):
            g = s - ch.lag_down(k) - slack
            pl.when(within(g, count))(functools.partial(ch.down, g, k))

    def w_copy(i):
        return cp_copy(i, stage.at[i], w_in.at[i], w_s, w_r)

    def weights(i):
        cols = pl.ds(pl.multiple_of(lax.rem(me + i + 1, groups) * per, per), per)
        part = mm(h1[:, cols], jnp.concatenate([gq[...], okv[...]], axis=1), TN)

        @pl.when(i < groups - 1)
        def _():
            stage[i] = part.astype(bf)
            w_copy(i).start()

        @pl.when(i == groups - 1)
        def _():
            own[...] = part

    def save(g):
        r = chunk_rows(g, rows)
        return pltpu.make_async_copy(gmix.at[r], tgrad_h.at[r], save_s.at[g])

    def finish(g):
        r = chunk_rows(g, rows)
        ch1.done(g)
        grad = out1[r, :].astype(jnp.float32) + mm(okv[r, :], wkv[...], NT)
        unit, inv = norm_parts(tok[r, :].astype(jnp.float32))
        acc[4:5, :] += jnp.sum(grad * unit, axis=0, keepdims=True)
        acc[5:6, :] += jnp.sum(grad, axis=0, keepdims=True)
        gmix[r, :] = (gmix[r, :].astype(jnp.float32) + norm_back(grad, unit, inv, gain)).astype(bf)
        save(g).start()

    turn = 2 * ch1.reach + SLACK
    ready = KV_STEP + chk.reach

    def finished(s):
        return jnp.clip(jnp.minimum(2 * (s - ready), s - turn + 1), 0, chunks)

    def up_copy(i):
        r = chunk_rows(lax.rem(me + i + 1, groups), per)
        return cp_copy(i, up_h.at[r], up_in.at[i], u_s, u_r)

    def out_copy(i):
        to = lax.rem(me + i + 1, groups)
        return cp_copy(i, outw_h.at[:, pl.ds(pl.multiple_of(to * per, per), per)], out_in.at[i], o_s, o_r)

    @pl.loop(0, max(chunks + turn, ready + 1 + chunks // 2, ready + 1 + groups))
    def _(s):
        pl.when(s + 2 < chunks)(lambda: project(s + 2))
        pl.when(within(s, chunks))(lambda: ch1.mate_copy(s).wait_recv())
        serve(ch1, s, chunks, SLACK)

        @pl.when(s == 0)
        def _():
            loads[2].wait()
            kv_send()
            for load in loads[3:]:
                load.wait()

        @pl.when(s < chunks // 2)
        def _():
            normed(2 * s)
            normed(2 * s + 1)

        pl.when(s == KV_STEP)(kv_gather)
        serve(chk, 2 * (s - KV_STEP), 1, 0)
        serve(chk, 2 * (s - KV_STEP) + 1, 1, 0)
        pl.when(s == ready)(lambda: chk.done(0))
        i = s - ready - 1
        pl.when(within(i, groups))(lambda: weights(i))
        pl.loop(finished(s - 1), finished(s))(finish)

    acc[6:7, 0 : usum.shape[1]] = usum[...]
    at = usum.shape[1]
    acc[6:7, at : at + heads_wide] = jnp.sum(gq[...].astype(jnp.float32), axis=0, keepdims=True)
    at += heads_wide
    acc[6:7, at : at + size] = jnp.sum(okv[:, size:].astype(jnp.float32), axis=0, keepdims=True)

    def v_copy(i):
        return cp_copy(i, acc, v_in.at[i], v_s, v_r)

    for i in range(groups - 1):
        v_copy(i).start()
    kv_mate.wait_send()
    chk.drain(0)
    for i in range(groups - 1):
        up_copy(i).wait()

    @pl.loop(0, groups - 1)
    def _(i):
        w_copy(i).wait_recv()
        own[...] += w_in[i].astype(jnp.float32)
        w_copy(i).wait_send()
        kv_copy(i).wait_send()
        out_copy(i).wait()

    @pl.loop(0, chunks)
    def _(g):
        save(g).wait()
        ch1.drain(g)

    total = jnp.zeros_like(acc)
    for i in range(groups - 1):
        v_copy(i).wait_recv()
    for source in range(groups):
        slot = lax.rem(me - source - 1 + groups, groups)
        theirs = v_in[jnp.minimum(slot, groups - 2)]
        total += jnp.where(slot == groups - 1, acc[...], theirs)
    vout[...] = total
    for i in range(groups - 1):
        v_copy(i).wait_send()


def tail(gq, dkv, wq, wk, wv, vectors, sums, usum, tokens, grad_mixed, outw, up, groups, chunks=8):
    rows, wide = tokens.shape
    heads_wide, two = gq.shape[1], 2 * wk.shape[1]
    bf, f32 = jnp.bfloat16, jnp.float32
    sds, vm = jax.ShapeDtypeStruct, pltpu.VMEM
    v, a = pl.BlockSpec(memory_space=pltpu.VMEM), pl.BlockSpec(memory_space=pl.ANY)
    dma = pltpu.SemaphoreType.DMA
    per, both = wide // groups, heads_wide + two
    return pl.pallas_call(
        functools.partial(tail_kernel, chunks),
        out_shape=(
            sds((rows, wide), bf),
            sds((groups - 1, heads_wide, per), bf),
            sds((groups - 1, per, up.shape[1]), bf),
            sds((per, both), f32),
            sds((8, wide), f32),
        ),
        in_specs=[a] * 5 + [v] * 4 + [a] * 4,
        out_specs=(a, a, a, v, v),
        scratch_shapes=[
            vm(gq.shape, bf), vm(dkv.shape, bf), vm(wq.shape, bf), vm((wide, two), bf),
            *[vm((rows, wide), bf)] * 5,
            vm((rows // 2, wide), bf), vm((rows // 2, wide), bf), vm((rows // 4, wide), bf),
            vm((rows // (4 * chunks), wide), f32),
            vm((groups, rows // 2, two), bf),
            vm((groups, rows // 2, two), bf),
            vm((groups - 1, rows // 2, two), bf),
            vm((rows, two), bf),
            vm((rows, two), bf),
            vm((rows // 2, two), bf),
            vm((rows // 4, two), bf),
            vm((rows // 4, two), f32),
            vm((groups - 1, per, both), bf),
            vm((groups - 1, per, both), bf),
            vm((8, wide), f32),
            vm((groups - 1, 8, wide), f32),
            dma((7,)), dma((chunks,)), *[dma((groups - 1,))] * 4, dma, dma,
            dma((groups - 1,)), dma((groups - 1,)), dma((groups - 1,)), dma((groups - 1,)),
            dma((groups - 1,)), dma((groups - 1,)),
            *Chain.sems(chunks), *Chain.sems(1),
        ],
        compiler_params=pltpu.CompilerParams(
            collective_id=3, has_side_effects=True, vmem_limit_bytes=61 * MIB
        ),
        name="tail",
    )(gq, dkv, wq, wk, wv, *vectors, sums, usum, tokens, grad_mixed, outw, up)


def shards(
    tokens,
    cotangent,
    first_gain,
    first_bias,
    query_weight,
    query_bias,
    key_weight,
    value_weight,
    value_bias,
    out_weight,
    out_bias,
    second_gain,
    second_bias,
    up_weight,
    up_bias,
    down_weight,
    down_bias,
    file_lengths,
    pad_mask,
):
    groups = lax.axis_size("cp")
    queries, gathered = head(
        tokens, query_weight, key_weight, value_weight, (first_gain, first_bias, query_bias, value_bias), groups
    )
    attended, attended_low, log_total = attend(queries, gathered, file_lengths, pad_mask)
    block_low, grad_mixed, grad_attended, down_own, down_in, up_own, up_part, out_part, out_own, sums, up_sum = middle(
        attended_low, tokens, cotangent, out_weight, up_weight, down_weight,
        (second_gain, second_bias, out_bias, down_bias, up_bias), groups,
    )
    grad_queries, key_value_parts, block_out, down_grad = attend_back(
        queries, grad_attended, attended, log_total, gathered, file_lengths, pad_mask,
        block_low, down_own, down_in,
    )
    tokens_low, out_in, up_in, own_grads, sums = tail(
        grad_queries, key_value_parts.reshape(groups, -1, gathered.shape[1]), query_weight,
        key_weight, value_weight, (first_gain, first_bias), sums, up_sum, tokens, grad_mixed, out_part, up_part, groups,
    )
    (
        tokens_grad, query_grad, key_grad, value_grad, up_grad, out_grad,
        down_bias_grad, second_gain_grad, second_bias_grad, out_bias_grad, first_gain_grad, first_bias_grad,
        up_bias_grad, query_bias_grad, value_bias_grad,
    ) = emit(
        tokens_low, own_grads, up_own, up_in, out_own, out_in, sums, query_weight.shape[1]
    )
    return (
        block_out,
        tokens_grad,
        first_gain_grad,
        first_bias_grad,
        query_grad,
        query_bias_grad,
        key_grad,
        value_grad,
        value_bias_grad,
        out_grad,
        out_bias_grad,
        second_gain_grad,
        second_bias_grad,
        up_grad,
        up_bias_grad,
        down_grad,
        down_bias_grad,
    )


def solution(mesh):
    placed = (
        P("cp", None),
        P("cp", None),
        P(),
        P(),
        P(None, "tp"),
        P("tp"),
        P(),
        P(),
        P(),
        P("tp", None),
        P(),
        P(),
        P(),
        P(None, "tp"),
        P("tp"),
        P("tp", None),
        P(),
        P(),
        P(),
    )
    return jax.shard_map(
        shards,
        mesh=mesh,
        in_specs=placed,
        out_specs=(
            P("cp", None),
            P("cp", None),
            P(),
            P(),
            P("cp", "tp"),
            P("tp"),
            P("cp", None),
            P("cp", None),
            P(),
            P("tp", "cp"),
            P(),
            P(),
            P(),
            P("cp", "tp"),
            P("tp"),
            P("tp", "cp"),
            P(),
        ),
        check_vma=False,
    )
```
